32 devices in a mesh: item: 2 (over x), tok: 16 (over z, y, core).
Axes of the slice: x: 2, y: 2, z: 4, core: 2. Of those that a mesh axis runs over, the one named last changes fastest.
Arguments:
- tokens: bfloat16 [4, 2048, 1024], P('item', 'tok'), may hold values from -6 to 6
- norm_gain: bfloat16 [1024], P(('item', 'tok')), may hold values from 0.5 to 1.5
- norm_shift: bfloat16 [1024], P(('item', 'tok')), may hold values from -3 to 3
- w_up: bfloat16 [1024, 3072], P(('item', 'tok')), may hold values from -0.1875 to 0.1875
- w_value: bfloat16 [1024, 512], P(('item', 'tok')), may hold values from -0.1875 to 0.1875
- w_back: bfloat16 [512, 3072], P(('item', 'tok')), may hold values from -0.25 to 0.25
- w_down: bfloat16 [3072, 1024], P(('item', 'tok')), may hold values from -0.21875 to 0.21875
- mode_coef: bfloat16 [512, 1024], P('tok', 'item'), may hold values from -0.015625 to 0.015625
- skip_gain: bfloat16 [512], P('tok'), may hold values from -3 to 3
- cotangent: bfloat16 [4, 2048, 1024], P('item', 'tok'), may hold values from -6 to 6
Outputs:
- result: bfloat16 [4, 2048, 1024], P('item', 'tok')
- grad_tokens: float32 [4, 2048, 1024], P('item', 'tok')
- grad_norm_gain: float32 [1024], P(('item', 'tok'))
- grad_norm_shift: float32 [1024], P(('item', 'tok'))
- grad_w_up: float32 [1024, 3072], P(('item', 'tok'))
- grad_w_value: float32 [1024, 512], P(('item', 'tok'))
- grad_w_back: float32 [512, 3072], P(('item', 'tok'))
- grad_w_down: float32 [3072, 1024], P(('item', 'tok'))
- grad_mode_coef: float32 [512, 1024], P('tok', 'item')
- grad_skip_gain: float32 [512], P('tok')
The draws below stay inside these ranges and needn't reach their ends.
All inputs are finite; a program needn't handle non-finite values.
Results may differ from the reference program's by a relative error of at most 0.0082.
Values may be sent and summed in bfloat16 or wider, within the bound.
A program may use at most 192 MiB of HBM per device.

```python
import jax
import jax.numpy as jnp
from jax import lax

D = 1024
FF = 3072
DV = 512
NSTATE = 512
SEQ_LEN = 2048
ITEMS = 4


def steps_of(key, dims, split, low, high):
    gain = 1.0
    for dim, shards_of in split:
        heights = jax.random.uniform(jax.random.fold_in(jax.random.fold_in(key, 6), dim), (shards_of,), jnp.float32, low / len(split), high / len(split))
        gain = gain * jnp.repeat(jnp.exp(heights), dims[dim] // shards_of).reshape((-1,) + (1,) * (len(dims) - 1 - dim))
    return gain


def gaussian(own_key, extent, deviation, reach, pieces=(), kind=jnp.bfloat16):
    level = steps_of(own_key, extent, pieces, -0.22, 0.18) if pieces else 1.0
    entries = jax.random.normal(own_key, extent, jnp.float32) * deviation * level
    return jnp.minimum(jnp.maximum(entries, -reach), reach).astype(kind)


def setup_inputs(seed: int = 0) -> dict:
    streams_of = jax.random.split(jax.random.key(seed), 11)
    tokens = gaussian(streams_of[0], (ITEMS, SEQ_LEN, D), 1.0, 6.0, ((0, 2), (1, 16)))
    norm_gain = jnp.clip(1.0 + 0.1 * jax.random.normal(streams_of[1], (D,), jnp.float32), 0.5, 1.5).astype(jnp.bfloat16)
    norm_shift = gaussian(streams_of[2], (D,), 0.5, 3.0, ((0, 32),))
    w_up = gaussian(streams_of[3], (D, FF), D ** -0.5, 0.1875, ((0, 32),))
    w_value = gaussian(streams_of[4], (D, DV), D ** -0.5, 0.1875, ((0, 32),))
    w_back = gaussian(streams_of[5], (DV, FF), DV ** -0.5, 0.25, ((0, 32),))
    w_down = gaussian(streams_of[6], (FF, D), (FF // 4) ** -0.5, 0.21875, ((0, 32),))
    mode_coef = gaussian(streams_of[7], (DV, 2 * NSTATE), (NSTATE * SEQ_LEN // 8) ** -0.5, 0.015625, ((0, 16), (1, 2)))
    skip_gain = gaussian(streams_of[8], (DV,), 0.5, 3.0, ((0, 16),))
    cotangent = gaussian(streams_of[9], (ITEMS, SEQ_LEN, D), 1.0, 6.0, ((0, 2), (1, 16)))
    return {"tokens": tokens, "norm_gain": norm_gain, "norm_shift": norm_shift, "w_up": w_up, "w_value": w_value, "w_back": w_back, "w_down": w_down, "mode_coef": mode_coef, "skip_gain": skip_gain, "cotangent": cotangent}


@jax.custom_vjp
def low(v):
    return lax.optimization_barrier(v.astype(jnp.bfloat16)).astype(jnp.float32)

@jax.custom_vjp
def low_back(v):
    return v

def low_keep(v):
    return (low(v), None)

def low_pass(kept, grad):
    return (grad,)

def back_keep(v):
    return (v, None)

def back_low(kept, grad):
    return (low(grad),)
low.defvjp(low_keep, low_pass)
low_back.defvjp(back_keep, back_low)
highest = lax.Precision.HIGHEST

def basis_table(length, states):
    places = jnp.arange(length, dtype=jnp.int32)
    mode_ids = jnp.arange(states, dtype=jnp.int32)
    fraction = (mode_ids * 41 % states).astype(jnp.float32) / states
    mode_rates = jnp.exp(jnp.log(1.0 / 32.0) + fraction * jnp.log(32.0 / (4.0 * length)))
    decays = jnp.exp(-mode_rates[:, None] * places[None, :].astype(jnp.float32))
    phase_turns = (mode_ids[:, None] * places[None, :] % (2 * states)).astype(jnp.float32) * (jnp.pi / states)
    return jnp.concatenate([decays * jnp.cos(phase_turns), decays * jnp.sin(phase_turns)], axis=0)

def layer_norm(token_rows, gain_row, shift_row):
    row_mean = lax.optimization_barrier(jnp.mean(token_rows, axis=-1, keepdims=True))
    centered = token_rows - row_mean
    variance = lax.optimization_barrier(jnp.mean(centered * centered, axis=-1, keepdims=True))
    return centered * lax.rsqrt(variance + 1e-05) * gain_row + shift_row

def causal_conv(signal, kernel):
    length = signal.shape[-1]
    product = jnp.fft.rfft(signal, n=2 * length) * jnp.fft.rfft(kernel, n=2 * length)
    return jnp.fft.irfft(product, n=2 * length)[..., :length]

def forward(tokens, norm_gain, norm_shift, w_up, w_value, w_back, w_down, mode_coef, skip_gain):
    kernel = jnp.dot(mode_coef, basis_table(SEQ_LEN, NSTATE), precision=highest)

    def one_item(token_rows):
        normed = low(layer_norm(token_rows, norm_gain, norm_shift))
        up_pre = low_back(jnp.dot(normed, w_up, precision=highest))
        value_pre = low_back(jnp.dot(normed, w_value, precision=highest))
        value = low_back(low(jax.nn.gelu(value_pre)))
        signal = value.T
        mixed = low_back(low(causal_conv(signal, kernel) + skip_gain[:, None] * signal))
        gate = low_back(jnp.dot(mixed.T, w_back, precision=highest))
        hidden = low(jax.nn.gelu(up_pre) * gate)
        branch = low_back(jnp.dot(hidden, w_down, precision=highest))
        return token_rows + branch
    return lax.map(jax.checkpoint(one_item), tokens)

def reference(tokens, norm_gain, norm_shift, w_up, w_value, w_back, w_down, mode_coef, skip_gain, cotangent):
    output, pullback = jax.vjp(forward, tokens.astype(jnp.float32), norm_gain.astype(jnp.float32), norm_shift.astype(jnp.float32), w_up.astype(jnp.float32), w_value.astype(jnp.float32), w_back.astype(jnp.float32), w_down.astype(jnp.float32), mode_coef.astype(jnp.float32), skip_gain.astype(jnp.float32))
    grads = pullback(cotangent.astype(jnp.float32))
    return (output.astype(jnp.bfloat16), grads[0], grads[1], grads[2], grads[3], grads[4], grads[5], grads[6], grads[7], grads[8])
```

```python
import functools
import math
import types

import jax
import jax.numpy as jnp
import ml_dtypes
import numpy as np
from jax import lax
from jax.experimental import pallas as pl
from jax.experimental.pallas import tpu as pltpu
from jax.sharding import PartitionSpec as P

highest = lax.Precision.HIGHEST


def basis_block(start_index, block_width, length, states):
    places = start_index + jnp.arange(block_width, dtype=jnp.int32)
    mode_ids = jnp.arange(states, dtype=jnp.int32)
    fraction = (mode_ids * 41 % states).astype(jnp.float32) / states
    mode_rates = jnp.exp(jnp.log(1.0 / 32.0) + fraction * jnp.log(32.0 / (4.0 * length)))
    decays = jnp.exp(-mode_rates[:, None] * places[None, :].astype(jnp.float32))
    phase_turns = (mode_ids[:, None] * places[None, :] % (2 * states)).astype(jnp.float32) * (
        jnp.pi / states
    )
    return jnp.concatenate([decays * jnp.cos(phase_turns), decays * jnp.sin(phase_turns)], axis=0)


def make_kernel(coef_full, length):
    states = coef_full.shape[1] // 2
    block_width = math.gcd(length, 2048)
    block_count = length // block_width

    def one_block(block_index):
        table = basis_block(block_index * block_width, block_width, length, states)
        return jnp.dot(coef_full, table, precision=highest)

    pieces = lax.map(one_block, jnp.arange(block_count, dtype=jnp.int32))
    return jnp.transpose(pieces, (1, 0, 2)).reshape(coef_full.shape[0], length)


def coef_gradient(grad_kernel, states):
    channels, length = grad_kernel.shape
    block_width = math.gcd(length, 2048)
    block_count = length // block_width
    slabs = grad_kernel.reshape(channels, block_count, block_width)

    def add_block(running, block_index):
        slab_part = lax.dynamic_index_in_dim(slabs, block_index, 1, keepdims=False)
        table = basis_block(block_index * block_width, block_width, length, states)
        return (running + jnp.dot(slab_part, table.T, precision=highest), None)

    start_total = jnp.zeros((channels, 2 * states), jnp.float32)
    summed, unused = lax.scan(add_block, start_total, jnp.arange(block_count, dtype=jnp.int32))
    return summed


def unit_tables(row_count, column_count, period):
    row_ids = jnp.arange(row_count, dtype=jnp.int32)[:, None]
    column_ids = jnp.arange(column_count, dtype=jnp.int32)[None, :]
    phase_turns = (row_ids * column_ids % period).astype(jnp.float32) * (2.0 * jnp.pi / period)
    return (jnp.cos(phase_turns), jnp.sin(phase_turns))


def right_product(left_part, table):
    return jnp.einsum("...kq,qm->...km", left_part, table, precision=highest)


def spectrum(signal):
    length = signal.shape[-1]
    padded_size = 2 * length
    outer_size = padded_size // 128
    half_size = outer_size // 2
    folded = signal.reshape(signal.shape[:-1] + (half_size, 128))
    cos_outer, sin_outer = unit_tables(outer_size, half_size, outer_size)
    section_real = jnp.einsum("kp,...pq->...kq", cos_outer, folded, precision=highest)
    section_imag = -jnp.einsum("kp,...pq->...kq", sin_outer, folded, precision=highest)
    twist_cos, twist_sin = unit_tables(outer_size, 128, padded_size)
    turned_real = section_real * twist_cos + section_imag * twist_sin
    turned_imag = section_imag * twist_cos - section_real * twist_sin
    cos_inner, sin_inner = unit_tables(128, 128, 128)
    out_real = right_product(turned_real, cos_inner) + right_product(turned_imag, sin_inner)
    out_imag = right_product(turned_imag, cos_inner) - right_product(turned_real, sin_inner)
    return (out_real, out_imag)


def inverse(spec_real, spec_imag):
    outer_size = spec_real.shape[-2]
    padded_size = outer_size * 128
    half_size = outer_size // 2
    cos_inner, sin_inner = unit_tables(128, 128, 128)
    back_real = right_product(spec_real, cos_inner) - right_product(spec_imag, sin_inner)
    back_imag = right_product(spec_real, sin_inner) + right_product(spec_imag, cos_inner)
    twist_cos, twist_sin = unit_tables(outer_size, 128, padded_size)
    turned_real = back_real * twist_cos - back_imag * twist_sin
    turned_imag = back_real * twist_sin + back_imag * twist_cos
    cos_outer, sin_outer = unit_tables(half_size, outer_size, outer_size)
    signal = jnp.einsum("pk,...kq->...pq", cos_outer, turned_real, precision=highest)
    signal = signal - jnp.einsum("pk,...kq->...pq", sin_outer, turned_imag, precision=highest)
    return signal.reshape(signal.shape[:-2] + (half_size * 128,)) / padded_size


def layer_norm(token_rows, gain_row, shift_row):
    row_mean = jnp.mean(token_rows, axis=-1, keepdims=True)
    centered = token_rows - row_mean
    variance = jnp.mean(centered * centered, axis=-1, keepdims=True)
    return centered * lax.rsqrt(variance + 1e-05) * gain_row + shift_row


def body(
    tokens, norm_gain, norm_shift, w_up, w_value, w_back, w_down, mode_coef, skip_gain, cotangent
):
    gain_full, shift_full, up_full, value_full = (
        lax.all_gather(norm_gain, ("item", "tok"), axis=0, tiled=True),
        lax.all_gather(norm_shift, ("item", "tok"), axis=0, tiled=True),
        lax.all_gather(w_up, ("item", "tok"), axis=0, tiled=True),
        lax.all_gather(w_value, ("item", "tok"), axis=0, tiled=True),
    )
    back_full, down_full = (
        lax.all_gather(w_back, ("item", "tok"), axis=0, tiled=True),
        lax.all_gather(w_down, ("item", "tok"), axis=0, tiled=True),
    )
    coef_full = lax.all_gather(mode_coef, "item", axis=1, tiled=True)
    token_rows = tokens.astype(jnp.float32)
    gain_float = gain_full.astype(jnp.float32)
    shift_float = shift_full.astype(jnp.float32)
    normed = layer_norm(token_rows, gain_float, shift_float).astype(jnp.bfloat16)
    up_pre = jnp.einsum("std,df->stf", normed, up_full, preferred_element_type=jnp.float32)
    value_pre = jnp.einsum("std,dh->sht", normed, value_full, preferred_element_type=jnp.float32)
    value = jax.nn.gelu(value_pre).astype(jnp.bfloat16)
    channel_values = lax.all_to_all(value, "tok", split_axis=1, concat_axis=2, tiled=True)
    length = channel_values.shape[-1]
    kernel = make_kernel(coef_full.astype(jnp.float32), length)
    signal = channel_values.astype(jnp.float32)
    skip_column = skip_gain.astype(jnp.float32)[:, None]
    value_real, value_imag = spectrum(signal)
    kernel_real, kernel_imag = spectrum(kernel)
    conv_out = inverse(
        value_real * kernel_real - value_imag * kernel_imag,
        value_real * kernel_imag + value_imag * kernel_real,
    )
    mixed_channels = (conv_out + skip_column * signal).astype(jnp.bfloat16)
    mixed = lax.all_to_all(mixed_channels, "tok", split_axis=2, concat_axis=1, tiled=True)
    gate = jnp.einsum("sht,hf->stf", mixed, back_full, preferred_element_type=jnp.float32)
    up_act = jax.nn.gelu(up_pre)
    hidden = (up_act * gate).astype(jnp.bfloat16)
    branch = jnp.einsum("stf,fd->std", hidden, down_full, preferred_element_type=jnp.float32)
    result = (token_rows + branch).astype(jnp.bfloat16)
    grad_w_down = jnp.einsum("stf,std->fd", hidden, cotangent, preferred_element_type=jnp.float32)
    grad_hidden = jnp.einsum(
        "std,fd->stf", cotangent, down_full, preferred_element_type=jnp.float32
    )
    grad_gate = (grad_hidden * up_act).astype(jnp.bfloat16)
    grad_up_act = grad_hidden * gate
    grad_w_back = jnp.einsum("sht,stf->hf", mixed, grad_gate, preferred_element_type=jnp.float32)
    grad_mixed = jnp.einsum(
        "stf,hf->sht", grad_gate, back_full, preferred_element_type=jnp.float32
    ).astype(jnp.bfloat16)
    grad_channels = lax.all_to_all(grad_mixed, "tok", split_axis=1, concat_axis=2, tiled=True)
    grad_signal = grad_channels.astype(jnp.float32)
    grad_real, grad_imag = spectrum(grad_signal)
    grad_value_channels = inverse(
        kernel_real * grad_real + kernel_imag * grad_imag,
        kernel_real * grad_imag - kernel_imag * grad_real,
    )
    grad_value_channels = (grad_value_channels + skip_column * grad_signal).astype(jnp.bfloat16)
    grad_kernel = inverse(
        jnp.sum(grad_real * value_real + grad_imag * value_imag, axis=0),
        jnp.sum(grad_imag * value_real - grad_real * value_imag, axis=0),
    )
    grad_skip_part = jnp.sum(grad_signal * signal, axis=(0, 2))
    grad_coef_part = coef_gradient(grad_kernel, coef_full.shape[1] // 2)
    grad_mode_coef = lax.psum_scatter(grad_coef_part, "item", scatter_dimension=1, tiled=True)
    grad_skip_gain = lax.psum(grad_skip_part, "item")
    grad_value = lax.all_to_all(grad_value_channels, "tok", split_axis=2, concat_axis=1, tiled=True)
    gelu_value_back = jax.vjp(jax.nn.gelu, value_pre)[1]
    grad_value_pre = gelu_value_back(grad_value.astype(jnp.float32))[0].astype(jnp.bfloat16)
    gelu_up_back = jax.vjp(jax.nn.gelu, up_pre)[1]
    grad_up_pre = gelu_up_back(grad_up_act)[0].astype(jnp.bfloat16)
    grad_w_up = jnp.einsum("std,stf->df", normed, grad_up_pre, preferred_element_type=jnp.float32)
    grad_w_value = jnp.einsum(
        "std,sht->dh", normed, grad_value_pre, preferred_element_type=jnp.float32
    )
    grad_normed = jnp.einsum(
        "stf,df->std", grad_up_pre, up_full, preferred_element_type=jnp.float32
    )
    grad_normed = grad_normed + jnp.einsum(
        "sht,dh->std", grad_value_pre, value_full, preferred_element_type=jnp.float32
    )
    norm_back = jax.vjp(layer_norm, token_rows, gain_float, shift_float)[1]
    grad_rows, grad_gain_part, grad_shift_part = norm_back(grad_normed)
    grad_tokens = cotangent.astype(jnp.float32) + grad_rows
    owners = lax.axis_size("item") * lax.axis_size("tok")
    norm_flat = jnp.concatenate(
        [grad_gain_part.reshape(owners, -1), grad_shift_part.reshape(owners, -1)], axis=1
    )
    up_flat = grad_w_up.reshape(owners, -1)
    value_flat = grad_w_value.reshape(owners, -1)
    back_flat = grad_w_back.reshape(owners, -1)
    down_flat = grad_w_down.reshape(owners, -1)
    summed = (
        lax.psum_scatter(norm_flat, ("item", "tok"), scatter_dimension=0, tiled=True),
        lax.psum_scatter(up_flat, ("item", "tok"), scatter_dimension=0, tiled=True),
        lax.psum_scatter(value_flat, ("item", "tok"), scatter_dimension=0, tiled=True),
        lax.psum_scatter(back_flat, ("item", "tok"), scatter_dimension=0, tiled=True),
        lax.psum_scatter(down_flat, ("item", "tok"), scatter_dimension=0, tiled=True),
    )
    gain_count = norm_gain.shape[0]
    norm_row = summed[0].reshape(-1)
    grad_norm_gain = norm_row[:gain_count]
    grad_norm_shift = norm_row[gain_count:]
    grad_up_out = summed[1].reshape(w_up.shape)
    grad_value_out = summed[2].reshape(w_value.shape)
    grad_back_out = summed[3].reshape(w_back.shape)
    grad_down_out = summed[4].reshape(w_down.shape)
    return (
        result,
        grad_tokens,
        grad_norm_gain,
        grad_norm_shift,
        grad_up_out,
        grad_value_out,
        grad_back_out,
        grad_down_out,
        grad_mode_coef,
        grad_skip_gain,
    )


MESH_ID = pl.DeviceIdType.MESH
bf16, f32 = jnp.bfloat16, jnp.float32
NT = (((1,), (1,)), ((), ()))
GC = math.sqrt(2.0 / math.pi)


def dot(a, b):
    return jnp.dot(a, b, preferred_element_type=f32)


def dot_nt(a, b):
    return lax.dot_general(a, b, NT, preferred_element_type=f32)


def gelu_parts(v):
    t = jnp.tanh(GC * (v + 0.044715 * v * v * v))
    half = 0.5 * (1.0 + t)
    slope = half + 0.5 * v * (1.0 - t * t) * (GC * (1.0 + 3 * 0.044715 * v * v))
    return v * half, slope


def split(v):
    high = v.astype(bf16)
    return high, (v - high.astype(f32)).astype(bf16)


def mode_tables(states, length):
    n = np.arange(states)
    rates = np.exp(np.log(1.0 / 32.0) + (n * 41 % states) / states * np.log(32.0 / (4.0 * length)))

    def table(places):
        decay = np.exp(-rates[:, None] * places[None, :])
        turn = (n[:, None] * places[None, :] % (2 * states)) * (np.pi / states)
        return decay * np.cos(turn), decay * np.sin(turn)

    far_re, far_im = table(np.arange(0, length, 128))
    near = np.concatenate(table(np.arange(128)), axis=0).astype(np.float32)
    high = near.astype(ml_dtypes.bfloat16)
    low = (near - high.astype(np.float32)).astype(ml_dtypes.bfloat16)
    return (
        far_re.T.astype(np.float32).copy(),
        far_im.T.astype(np.float32).copy(),
        high,
        low,
        high.T.copy(),
        low.T.copy(),
    )


class Links:
    def __init__(self, send_sems, recv_sems, place):
        self.send_sems, self.recv_sems, self.place = send_sems, recv_sems, place
        self.count = 0
        self.pending = []

    def take(self, n=1):
        first = self.count
        self.count += n
        return first

    def make(self, src, dst, ssem, rsem, to):
        return pltpu.make_async_remote_copy(
            src_ref=src,
            dst_ref=dst,
            send_sem=self.send_sems.at[ssem],
            recv_sem=self.recv_sems.at[rsem],
            device_id=to,
            device_id_type=MESH_ID,
        )

    def put(self, src, dst, to):
        slot = self.take()
        copy = self.make(src, dst, slot, slot, to)
        copy.start()
        self.pending.append((copy, None))
        return slot

    def got(self, slot, region):
        self.make(region, region, slot, slot, self.place).wait_recv()

    def put_or_keep(self, src, dst, ssem, rsem, to, here):
        remote = self.make(src, dst, ssem, rsem, to)
        local = pltpu.make_async_copy(src, dst, self.recv_sems.at[rsem])
        away = jnp.logical_not(here)
        pl.when(here)(local.start)
        pl.when(away)(remote.start)
        self.pending.append((remote, away))

    def finish(self):
        for copy, away in self.pending:
            if away is None:
                copy.wait_send()
            else:
                pl.when(away)(copy.wait_send)


N_SEMS = 200


def layer_kernel(names, *refs):
    r_ = dict(zip(names, refs))
    g = types.SimpleNamespace(**r_)
    x = lax.axis_index("item")
    tok = lax.axis_index("tok")
    z, y, c = tok // 4, (tok // 2) % 2, tok % 2
    n = tok // 2
    r = 2 * x + c

    def dev(x_, z_, y_, c_):
        return (x_, z_ * 4 + y_ * 2 + c_)

    def zo(k):
        return lax.rem(z + k, 4)

    def zb(k):
        return lax.rem(z + 4 - k, 4)

    def node(z_, y_):
        return 2 * z_ + y_

    sib, xn, diag = dev(x, z, y, 1 - c), dev(1 - x, z, y, c), dev(1 - x, z, y, 1 - c)
    r_sib, r_xn, r_diag = 2 * x + 1 - c, 2 * (1 - x) + c, 2 * (1 - x) + 1 - c
    members = ((sib, x, 1 - c, r_sib), (xn, 1 - x, c, r_xn), (diag, 1 - x, 1 - c, r_diag))
    ynb = dev(x, z, 1 - y, c)
    lk = Links(g.ssem, g.rsem, ynb)
    aligned = pl.multiple_of

    barrier = pltpu.get_barrier_semaphore()
    partners = [m[0] for m in members]
    for k in range(1, 4):
        partners += [dev(x, zo(k), y, c), dev(x, zo(k), 1 - y, c), dev(x, zo(k), y, 1 - c)]
    partners.append(ynb)
    for p in partners:
        pl.semaphore_signal(barrier, inc=1, device_id=p, device_id_type=MESH_ID)

    eye = lax.broadcasted_iota(jnp.int32, (32, 128), 0) == lax.broadcasted_iota(
        jnp.int32, (32, 128), 1
    )
    eye = eye.astype(bf16)
    ch_i = lax.broadcasted_iota(jnp.int32, (512, 128), 0)
    p_i = lax.broadcasted_iota(jnp.int32, (512, 128), 1)
    row16 = lax.broadcasted_iota(jnp.int32, (16, 128), 0)
    gain_row = dot(g.norm_gain[...], eye)
    shift_row = dot(g.norm_shift[...], eye)
    norm_pack = jnp.where(
        row16 == 0,
        jnp.broadcast_to(gain_row, (16, 128)),
        jnp.where(row16 == 1, jnp.broadcast_to(shift_row, (16, 128)), 0.0),
    ).astype(bf16)
    for rr in range(4):
        pick = ch_i == 64 * (p_i // 16) + 32 * (rr % 2) + 16 * (rr // 2) + p_i % 16
        pick = pick.astype(bf16)
        g.perm[:, 128 * rr : 128 * rr + 128] = pick
        g.pk_send[rr, 0:32, :] = dot(g.w_value[...], pick).astype(bf16)
        g.pk_send[rr, 32:48, :] = norm_pack
    pl.semaphore_wait(barrier, len(partners))

    pk_s, up_s, back_s = [], [], []
    for to, xm, cm, rm in members:
        pk_s.append(lk.put(g.pk_send.at[rm], g.pk.at[x, n, c], to))
    coef_s = lk.put(g.mode_coef.at[pl.ds(aligned(16 * (1 - x), 16), 16), :], g.coef.at[x], xn)
    my_back = g.w_back_all.at[c, y, x, z]

    def cols(rm):
        return pl.ds(aligned(768 * rm, 128), 768)

    for to, xm, cm, rm in members:
        up_s.append(lk.put(g.w_up.at[:, cols(rm)], g.w_up_all.at[x, n, c], to))
    for to, xm, cm, rm in members:
        back_s.append(lk.put(g.w_back.at[:, cols(rm)], my_back, to))
    tok_sib = lk.put(g.tokens, g.tok_all.at[r], sib)
    tok_x = lk.put(g.tokens, g.tok_all.at[r], xn)
    cot_sib = lk.put(g.cot, g.cot_all.at[r], sib)
    cot_x = lk.put(g.cot, g.cot_all.at[r], xn)
    g.pk[x, n, c] = g.pk_send[r]
    g.w_up_all[x, n, c] = g.w_up[:, cols(r)]
    g.w_back_all[c, y, x, z] = g.w_back[:, cols(r)]
    g.cot_all[r] = g.cot[...]
    g.coef[x] = g.mode_coef[pl.ds(aligned(16 * x, 16), 16), :]

    def gather_start(region):
        slots = {}
        for k in (1, 2, 3):
            slots[k] = lk.put(region(z, y), region(z, y), dev(x, zo(k), y, c))
        slots[4] = lk.put(region(z, y), region(z, y), ynb)
        return slots

    def gather_pass(slots, region, k):
        lk.got(slots[k], region(zb(k), y))
        slots[4 + k] = lk.put(region(zb(k), y), region(zb(k), y), ynb)

    def gather_end(slots, region):
        for k in range(4):
            lk.got(slots[4 + k], region(zb(k), 1 - y))

    def pk_region(z_, y_):
        return g.pk.at[:, node(z_, y_)]

    def up_region(z_, y_):
        return g.w_up_all.at[:, node(z_, y_)]

    def back_region(z_, y_):
        return g.w_back_all.at[:, y_, :, z_]

    for i, (to, xm, cm, rm) in enumerate(members):
        lk.got(pk_s[i], g.pk.at[xm, n, cm])
    pk_g = gather_start(pk_region)

    dn_r = lk.take(4)
    dn_slot = dn_r + 2 * lax.rem(z, 2) + c
    dst = g.w_down_all.at[lax.rem(z, 2), y, c]
    owner = z // 2
    for k in (1, 2, 3, 0):
        lk.put_or_keep(
            g.w_down,
            dst,
            lk.take(),
            dn_slot,
            dev(x, zo(k), y, owner),
            jnp.logical_and(owner == c, k == 0),
        ) if k == 0 else lk.pending.append(
            (start_of(lk.make(g.w_down, dst, lk.take(), dn_slot, dev(x, zo(k), y, owner))), None)
        )

    for i, (to, xm, cm, rm) in enumerate(members):
        lk.got(up_s[i], g.w_up_all.at[xm, n, cm])
    up_g = gather_start(up_region)
    for i, (to, xm, cm, rm) in enumerate(members):
        lk.got(back_s[i], g.w_back_all.at[cm, y, xm, z])
    back_g = gather_start(back_region)

    for k in (1, 2, 3):
        gather_pass(pk_g, pk_region, k)

    lk.got(coef_s, g.coef.at[1 - x])
    cc = g.coef[0].astype(f32)
    sc = g.coef[1].astype(f32)

    def far(p, _):
        hr = g.far_re[pl.ds(p, 1), :]
        hi = g.far_im[pl.ds(p, 1), :]
        rows = pl.ds(aligned(16 * p, 16), 16)
        g.state[rows, 0:512] = cc * hr + sc * hi
        g.state[rows, 512:1024] = sc * hr - cc * hi
        return 0

    lax.fori_loop(0, 16, far, 0)
    for half in range(2):
        rows = slice(128 * half, 128 * half + 128)
        hi_, lo_ = split(g.state[rows, :])
        g.kern[rows, :] = (
            dot(hi_, g.near_hi[...]) + dot(lo_, g.near_hi[...]) + dot(hi_, g.near_lo[...])
        )
    ii = lax.broadcasted_iota(jnp.int32, (128, 128), 0)
    jj = lax.broadcasted_iota(jnp.int32, (128, 128), 1)

    def toeplitz(h, _):
        prev = jnp.zeros((128, 128), f32)
        for k in range(16):
            row = jnp.broadcast_to(g.kern[pl.ds(16 * k + h, 1), :], (128, 128))
            turned = pltpu.roll(row, 0, 1, stride=1, stride_axis=0)
            g.toep[h, k] = jnp.where(jj >= ii, turned, prev).astype(bf16)
            prev = turned
        return 0

    lax.fori_loop(0, 8, toeplitz, 0)
    for k in (1, 2, 3):
        gather_pass(up_g, up_region, k)
    lax.fori_loop(8, 16, toeplitz, 0)

    gather_end(pk_g, pk_region)
    e_i = lax.broadcasted_iota(jnp.int32, (128, 1024), 0)
    e_j = lax.broadcasted_iota(jnp.int32, (128, 1024), 1)
    spread = jnp.logical_and(e_i < 32, lax.rem(e_j, 32) == e_i).astype(bf16)
    blk = lax.broadcasted_iota(jnp.int32, (16, 1024), 1) // 32
    acc = jnp.zeros((16, 1024), f32)
    for xm in range(2):
        for nm in range(8):
            for cm in range(2):
                rows = g.pk[xm, nm, cm, 32:48, :]
                acc = acc + jnp.where(
                    blk == 16 * xm + 2 * nm + cm, dot(rows, spread), 0.0
                )
    gain = acc[0:1, :]
    shift = acc[1:2, :]
    g.norm_rows[0:1, :] = gain
    g.norm_rows[1:2, :] = shift
    wv = g.pk[:, :, :, 0:32, :].reshape(1024, 128)
    g.w_val[...] = wv
    g.w_val_t[...] = wv.T

    def norm_block(read, q):
        def part(s_, _):
            rows = read(s_).astype(f32)
            mean = jnp.mean(rows, axis=-1, keepdims=True)
            cen = rows - mean
            var = jnp.mean(cen * cen, axis=-1, keepdims=True)
            out = (cen * lax.rsqrt(var + 1e-5) * g.norm_rows[0:1, :] + g.norm_rows[1:2, :]).astype(
                bf16
            )
            at = aligned(256 * q + 128 * s_, 128)
            g.normed[pl.ds(at, 128), :] = out
            g.normed_t[:, pl.ds(at, 128)] = out.T
            return 0

        lax.fori_loop(0, 2, part, 0)
        at = pl.ds(aligned(256 * q, 128), 256)
        pre = dot(g.w_val_t[...], g.normed_t[:, at])
        act, slope = gelu_parts(pre)
        g.val_slope[:, at] = slope
        g.val[:, at] = act.astype(bf16)

    norm_block(lambda s_: g.tokens[s_], r)
    lk.got(tok_sib, g.tok_all.at[r_sib])
    norm_block(lambda s_: g.tok_all[r_sib, s_], r_sib)
    for k in (1, 2, 3):
        gather_pass(back_g, back_region, k)

    lk.got(tok_x, g.tok_all.at[r_xn])
    tok_f = lk.put(g.tok_all.at[r_xn], g.tok_all.at[r_xn], sib)
    norm_block(lambda s_: g.tok_all[r_xn, s_], r_xn)
    lk.got(tok_f, g.tok_all.at[r_diag])
    norm_block(lambda s_: g.tok_all[r_diag, s_], r_diag)

    def channel_send(src, landing):
        slots = []
        for k in range(1, 8):
            to = lax.rem(n + k, 8)
            slots.append(
                lk.put(
                    src.at[pl.ds(aligned(16 * to, 16), 16), :],
                    landing.at[n],
                    (x, 2 * to + c),
                )
            )
        return slots

    def channel_got(slots, landing):
        for k in range(1, 8):
            lk.got(slots[k - 1], landing.at[lax.rem(n + 8 - k, 8)])

    def unpack(landing, out, lead):
        def one(nm, _):
            for tb in range(8):
                s_, cm = 2 * (tb // 4) + tb % 2, (tb // 2) % 2
                at = aligned(((32 * s_ + lead) + 2 * nm + cm) * 16, 16)
                out[pl.ds(at, 16), :] = landing[nm, :, 128 * tb : 128 * tb + 128].astype(f32)
            return 0

        lax.fori_loop(0, 8, one, 0)

    val_s = channel_send(g.val, g.val_in)
    g.val_in[n] = g.val[pl.ds(aligned(16 * n, 16), 16), :]

    def down_got(zl):
        for cm in range(2):
            region = g.w_down_all.at[zl, y, cm]
            pltpu.make_async_copy(region, region, lk.recv_sems.at[dn_r + 2 * zl + cm]).wait()

    dn_y = []
    for zl in range(2):
        down_got(zl)
        dn_y.append(lk.put(g.w_down_all.at[zl, y], g.w_down_all.at[zl, y], ynb))

    zero = jnp.zeros((256, 128), f32)
    for s_ in range(4):
        g.v32[pl.ds(512 * s_, 256), :] = zero
        g.g32[pl.ds(512 * s_ + 256, 256), :] = zero
    diag_i = lax.broadcasted_iota(jnp.int32, (32, 32), 0) == lax.broadcasted_iota(
        jnp.int32, (32, 32), 1
    )
    skip_row = jnp.broadcast_to(g.skip[...].astype(f32), (32, 32))
    g.skip_b[...] = dot(jnp.where(diag_i, skip_row, 0.0).astype(bf16), jnp.ones((32, 128), bf16))

    lk.got(cot_x, g.cot_all.at[r_xn])
    cot_f = lk.put(g.cot_all.at[r_xn], g.cot_all.at[r_xn], sib)

    channel_got(val_s, g.val_in)
    unpack(g.val_in, g.v32, 16)

    def conv(h, _):
        parts = []
        for k in range(16):
            rows = [
                g.v32[pl.ds((32 * s_ + 16 - k) * 16 + h, 16, stride=16), :] for s_ in range(4)
            ]
            parts.append(jnp.concatenate(rows, axis=0))
        out = g.skip_b[pl.ds(16 * x + h, 1), :] * parts[0]
        for kk in range(8):
            lhs = jnp.concatenate([parts[2 * kk], parts[2 * kk + 1]], axis=1).astype(bf16)
            out = out + dot(lhs, g.toep[h, 2 * kk : 2 * kk + 2].reshape(256, 128))
        g.o32[pl.ds(h, 64, stride=16), :] = out
        return 0

    def pack(out):
        def one(nm, _):
            for tb in range(8):
                s_, cm = 2 * (tb // 4) + tb % 2, (tb // 2) % 2
                at = aligned((16 * s_ + 2 * nm + cm) * 16, 16)
                out[nm, :, 128 * tb : 128 * tb + 128] = g.o32[pl.ds(at, 16), :].astype(bf16)
            return 0

        lax.fori_loop(0, 8, one, 0)

    def channel_back(src, landing):
        slots = []
        for k in range(1, 8):
            to = lax.rem(n + k, 8)
            slots.append(
                lk.put(src.at[to], landing.at[pl.ds(aligned(16 * n, 16), 16), :], (x, 2 * to + c))
            )
        return slots

    def channel_back_got(slots, landing):
        for k in range(1, 8):
            at = aligned(16 * lax.rem(n + 8 - k, 8), 16)
            lk.got(slots[k - 1], landing.at[pl.ds(at, 16), :])

    lax.fori_loop(0, 16, conv, 0)
    pack(g.mix_out)
    mix_s = channel_back(g.mix_out, g.mix.at[r])
    g.mix[r, pl.ds(aligned(16 * n, 16), 16), :] = g.mix_out[n]

    gather_end(up_g, up_region)

    def up_tile(i, _):
        rows = pl.ds(aligned(256 * lax.rem(i, 4), 256), 256)
        at = pl.ds(aligned(256 * (i // 4), 256), 256)
        w = g.w_up_all[:, :, :, :, at].reshape(1024, 256)
        act, slope = gelu_parts(dot(g.normed[rows, :], w))
        g.act[rows, at] = act
        g.slope[rows, at] = slope
        return 0

    lax.fori_loop(0, 12, up_tile, 0)
    channel_back_got(mix_s, g.mix.at[r])
    mix_sib = lk.put(g.mix.at[r], g.mix.at[r], sib)
    mix_x = lk.put(g.mix.at[r], g.mix.at[r], xn)
    for zl in range(2):
        lk.got(dn_y[zl], g.w_down_all.at[zl, 1 - y])
    lk.got(cot_sib, g.cot_all.at[r_sib])
    lk.got(cot_f, g.cot_all.at[r_diag])
    down2d = g.w_down_all.reshape(768, 1024)

    def hidden_tile(i, _):
        q = i // 3
        at = pl.ds(aligned(256 * lax.rem(i, 3), 256), 256)
        rows = pl.ds(aligned(256 * q, 256), 256)
        gh = dot_nt(g.cot_all[q].reshape(256, 1024), down2d[at, :])
        g.g_gate[rows, at] = (gh * g.act[rows, at]).astype(bf16)
        g.slope[rows, at] = gh * g.slope[rows, at]
        return 0

    lax.fori_loop(0, 12, hidden_tile, 0)
    lk.got(mix_x, g.mix.at[r_xn])
    mix_f = lk.put(g.mix.at[r_xn], g.mix.at[r_xn], sib)
    gather_end(back_g, back_region)
    back2d = g.w_back_all.reshape(512, 768)

    def mixed_part(xm, cm, q):
        w = back2d[pl.ds(aligned(128 * (2 * xm + cm), 128), 128), :]
        return dot_nt(w, g.g_gate[pl.ds(aligned(256 * q, 256), 256), :])

    def gm_sib(i, _):
        xm, q = i // 4, lax.rem(i, 4)
        at = pl.ds(aligned(256 * q, 128), 256)
        g.gm_send[xm, :, at] = mixed_part(xm, 1 - c, q).astype(bf16)
        return 0

    lax.fori_loop(0, 8, gm_sib, 0)
    gm_s = lk.put(g.gm_send, g.gm_in, sib)

    def gm_far_add(q, _):
        at = pl.ds(aligned(256 * q, 128), 256)
        g.gm_x[:, at] = (mixed_part(1 - x, c, q) + g.gm_in[1 - x, :, at].astype(f32)).astype(bf16)
        return 0

    lk.got(gm_s, g.gm_in)
    lax.fori_loop(0, 4, gm_far_add, 0)
    gm_xs = lk.put(g.gm_x, g.gm_xin, xn)

    lk.got(mix_sib, g.mix.at[r_sib])
    lk.got(mix_f, g.mix.at[r_diag])

    def turn(i, _):
        rr, tb = i // 8, lax.rem(i, 8)
        rows = pl.ds(aligned(128 * tb, 128), 128)
        at = pl.ds(aligned(128 * rr, 128), 128)
        g.mix_tok[rows, at] = g.mix[rr, :, rows].T
        return 0

    lax.fori_loop(0, 32, turn, 0)

    def gate_tile(i, _):
        q = i // 3
        rows = pl.ds(aligned(256 * q, 256), 256)
        at = pl.ds(aligned(256 * lax.rem(i, 3), 256), 256)
        gate = dot(g.mix_tok[rows, :], back2d[:, at])
        hidden = (g.act[rows, at] * gate).astype(bf16)
        g.hidden[rows, at] = hidden
        g.hidden_t[at, rows] = hidden.T
        g.g_up[rows, at] = (g.slope[rows, at] * gate).astype(bf16)
        return 0

    lax.fori_loop(0, 12, gate_tile, 0)

    def gm_own(q, _):
        at = pl.ds(aligned(256 * q, 128), 256)
        g.gm[:, at] = (
            mixed_part(x, c, q) + g.gm_in[x, :, at].astype(f32) + g.gm_xin[:, at].astype(f32)
        ).astype(bf16)
        return 0

    lk.got(gm_xs, g.gm_xin)
    lax.fori_loop(0, 4, gm_own, 0)
    gm_cs = channel_send(g.gm, g.gm_land)
    g.gm_land[n] = g.gm[pl.ds(aligned(16 * n, 16), 16), :]

    cot2d = g.cot_all.reshape(1024, 1024)
    gd_y = []
    for zl in range(2):

        def down_tile(i, _):
            rows = pl.ds(aligned(384 * zl + 192 * (i // 4), 64), 192)
            at = pl.ds(aligned(256 * lax.rem(i, 4), 256), 256)
            g.gd[zl, i // 4, :, at] = dot(g.hidden_t[rows, :], cot2d[:, at]).astype(bf16)
            return 0

        lax.fori_loop(0, 8, down_tile, 0)
        gd_y.append(lk.put(g.gd.at[zl, 1 - y], g.gd_y.at[zl], ynb))

    up_y = []

    def up_grad(k):
        z_d = zo(k)
        for xm in range(2):
            t = 4 * xm + z_d

            def tile(i, _):
                rows = pl.ds(aligned(128 * t, 128), 128)
                at = pl.ds(aligned(256 * i, 256), 256)
                g.gu[xm, z_d, :, at] = dot(g.normed_t[rows, :], g.g_up[:, at]).astype(bf16)
                return 0

            lax.fori_loop(0, 3, tile, 0)
            other = pl.ds(aligned(64 * (1 - y), 64), 64)
            up_y.append((t, lk.put(g.gu.at[xm, z_d, other], g.gu_y.at[t], ynb)))

    own64 = pl.ds(aligned(64 * y, 64), 64)
    gu_s = {}

    def up_sum(i, k):
        z_d = zo(k)
        for xm in range(2):
            t, slot = up_y[2 * i + xm]
            lk.got(slot, g.gu_y.at[t])
            total = g.gu[xm, z_d, own64, :].astype(f32) + g.gu_y[t].astype(f32)
            g.gu[xm, z_d, own64, :] = total.astype(bf16)
        if k:
            gu_s[k] = lk.put(g.gu.at[:, z_d, own64], g.gu_in.at[k - 1], dev(x, z_d, y, c))

    gd_r = lk.take(4)

    def down_sum(zl):
        lk.got(gd_y[zl], g.gd_y.at[zl])
        for cm in range(2):
            part = pl.ds(96 * cm, 96)
            total = g.gd[zl, y, part, :].astype(f32) + g.gd_y[zl, part, :].astype(f32)
            g.gd[zl, y, part, :] = total.astype(bf16)
            z_d = 2 * c + zl
            here = jnp.logical_and(z_d == z, c == cm)
            lk.put_or_keep(
                g.gd.at[zl, y, part], g.gd_in.at[z], lk.take(), gd_r + z, dev(x, z_d, y, cm), here
            )

    up_grad(1)
    down_sum(0)
    up_grad(2)
    down_sum(1)
    up_sum(0, 1)
    up_grad(3)
    up_sum(1, 2)
    up_grad(0)
    up_sum(2, 3)

    mix2d = g.mix.reshape(512, 1024)

    def back_tile(rr):
        def tile(i, _):
            at = pl.ds(aligned(256 * i, 256), 256)
            rows = pl.ds(aligned(128 * rr, 128), 128)
            g.gb[rr // 2, lax.rem(rr, 2), :, at] = dot(
                mix2d[rows, :], g.g_gate[:, at]
            ).astype(bf16)
            return 0

        lax.fori_loop(0, 3, tile, 0)

    gb_y = []
    for cm in range(2):
        back_tile(2 * cm + 1 - y)
        gb_y.append(lk.put(g.gb.at[cm, 1 - y], g.gb_y.at[cm], ynb))
    up_sum(3, 0)
    for cm in range(2):
        back_tile(2 * cm + y)

    channel_got(gm_cs, g.gm_land)
    unpack(g.gm_land, g.g32, 0)
    g.xs[:, 2048:2176] = jnp.zeros((128, 128), f32)

    def conv_back(h, _):
        parts = []
        for k in range(16):
            rows = [g.g32[pl.ds((32 * s_ + k) * 16 + h, 16, stride=16), :] for s_ in range(4)]
            parts.append(jnp.concatenate(rows, axis=0))
        own = [g.v32[pl.ds((32 * s_ + 16) * 16 + h, 16, stride=16), :] for s_ in range(4)]
        own = jnp.concatenate(own, axis=0)
        g.skip_part[pl.ds(h, 1), :] = jnp.sum(own * parts[0], axis=0, keepdims=True)
        own_t = own.T.astype(bf16)
        out = g.skip_b[pl.ds(16 * x + h, 1), :] * parts[0]
        for kk in range(8):
            lhs = jnp.concatenate([parts[2 * kk], parts[2 * kk + 1]], axis=1).astype(bf16)
            rhs = jnp.concatenate([g.toep[h, 2 * kk], g.toep[h, 2 * kk + 1]], axis=1)
            out = out + dot_nt(lhs, rhs)
            g.xs[:, 256 * kk : 256 * kk + 256] = dot(own_t, lhs)
        g.o32[pl.ds(h, 64, stride=16), :] = out

        acc = g.xs[120:128, :]
        for b in range(14, -1, -1):
            acc = pltpu.roll(acc, 2176 - 8, 1) + g.xs[8 * b : 8 * b + 8, :]
        for k in range(17):
            at = pl.ds(aligned(128 * k + 8 * h, 8), 8)
            g.gk8[at, :] = acc[:, 128 * k : 128 * k + 128]
        return 0

    lax.fori_loop(0, 16, conv_back, 0)
    pack(g.gv_out)
    gv_s = channel_back(g.gv_out, g.g_val)
    g.g_val[pl.ds(aligned(16 * n, 16), 16), :] = g.gv_out[n]

    for cm in range(2):
        lk.got(gb_y[cm], g.gb_y.at[cm])
        total = g.gb[cm, y].astype(f32) + g.gb_y[cm].astype(f32)
        g.gb_z[pl.ds(2 * cm, 2)] = total.astype(bf16).reshape(2, 4, 16, 768)
    gb_s = {}
    for k in (1, 2, 3):
        gb_s[k] = lk.put(g.gb_z.at[:, zo(k)], g.gb_in.at[k - 1], dev(x, zo(k), y, c))


    def gk_rows(s_):
        tiles = [g.gk8[pl.ds(128 * k + s_, 16, stride=8), :] for k in range(17)]
        return jnp.concatenate(tiles, axis=1)

    acc = gk_rows(7)
    for s_ in range(6, -1, -1):
        acc = pltpu.roll(acc, 2176 - 1, 1) + gk_rows(s_)
    g.gk[...] = acc
    for half in range(2):
        tall = jnp.concatenate(
            [g.gk[:, 128 * k : 128 * k + 128] for k in range(8 * half, 8 * half + 8)], axis=0
        )
        hi_, lo_ = split(tall)
        g.state[128 * half : 128 * half + 128, :] = (
            dot(hi_, g.near_t_hi[...]) + dot(lo_, g.near_t_hi[...]) + dot(hi_, g.near_t_lo[...])
        )

    def far_back(p, carry):
        gc, gs = carry
        hr = g.far_re[pl.ds(p, 1), :]
        hi = g.far_im[pl.ds(p, 1), :]
        rows = pl.ds(aligned(16 * p, 16), 16)
        ur = g.state[rows, 0:512]
        ui = g.state[rows, 512:1024]
        return gc + hr * ur - hi * ui, gs + hr * ui + hi * ur

    blank = jnp.zeros((16, 512), f32)
    gc, gs = lax.fori_loop(0, 16, far_back, (blank, blank))
    g.gcoef[0] = gc
    g.gcoef[1] = gs
    gcoef_s = lk.put(g.gcoef.at[1 - x], g.gcoef_in, xn)
    g.skip_sum[...] = jnp.broadcast_to(jnp.sum(g.skip_part[...], axis=1, keepdims=True), (16, 128))
    skip_s = lk.put(g.skip_sum, g.skip_in, xn)

    def group_sum(part, send, land, xsend, xland):
        def to_sib(i, _):
            xm, j = i // 4, lax.rem(i, 4)
            at = pl.ds(aligned(256 * j, 256), 256)
            send[xm, :, at] = part(xm, 1 - c, at).astype(bf16)
            return 0

        lax.fori_loop(0, 8, to_sib, 0)
        first = lk.put(send, land, sib)

        def add_far(j, _):
            at = pl.ds(aligned(256 * j, 256), 256)
            xsend[:, at] = (part(1 - x, c, at) + land[1 - x, :, at].astype(f32)).astype(bf16)
            return 0

        lk.got(first, land)
        lax.fori_loop(0, 4, add_far, 0)
        second = lk.put(xsend, xland, xn)

        def own(at):
            return part(x, c, at) + land[x, :, at].astype(f32) + xland[:, at].astype(f32)

        return second, own

    spare = g.normed.reshape(2, 2, 256, 1024)

    def branch_part(xm, cm, at):
        rows = pl.ds(aligned(256 * (2 * xm + cm), 256), 256)
        return dot(g.hidden[rows, :], down2d[:, at])

    br_s, br_own = group_sum(
        branch_part, spare.at[0], g.br_in, g.tok_all.at[r].reshape(256, 1024), g.br_xin
    )

    channel_back_got(gv_s, g.g_val)
    gvp = (g.g_val[...].astype(f32) * g.val_slope[...]).astype(bf16)
    g.gvp_t[...] = gvp.T

    def val_tile(t, _):
        rows = pl.ds(aligned(128 * t, 128), 128)
        g.gv[t] = dot(g.normed_t[rows, :], g.gvp_t[...]).astype(bf16)
        return 0

    lax.fori_loop(0, 8, val_tile, 0)
    other = pl.ds(aligned(64 * (1 - y), 64), 64)
    gv_y = lk.put(g.gv.at[:, other], g.gv_y, ynb)

    up2d = g.w_up_all.reshape(1024, 768)

    def normed_part(xm, cm, at):
        rows = pl.ds(aligned(256 * (2 * xm + cm), 256), 256)
        return dot_nt(g.g_up[rows, :], up2d[at, :]) + dot_nt(g.gvp_t[rows, :], g.w_val[at, :])

    gn_s, gn_own = group_sum(
        normed_part, spare.at[1], g.gn_in, g.tok_all.at[r_sib].reshape(256, 1024), g.gn_xin
    )

    lk.got(gv_y, g.gv_y)
    total = (g.gv[:, own64, :].astype(f32) + g.gv_y[...].astype(f32)).astype(bf16)
    g.gv_z[...] = total.reshape(2, 4, 64, 128)
    gv_zs = {}
    for k in (1, 2, 3):
        gv_zs[k] = lk.put(g.gv_z.at[:, zo(k)], g.gv_in.at[k - 1], dev(x, zo(k), y, c))

    for k in (1, 2, 3):
        lk.got(gu_s[k], g.gu_in.at[k - 1])
    total = g.gu[:, z, own64, :].astype(f32)
    for k in range(3):
        total = total + g.gu_in[k].astype(f32)
    g.gu_f[...] = total.reshape(2, 2, 32, 768).astype(bf16)
    for k in (1, 2, 3):
        lk.got(gb_s[k], g.gb_in.at[k - 1])
    total = g.gb_z[:, z].astype(f32)
    for k in range(3):
        total = total + g.gb_in[k].astype(f32)
    g.gb_f[...] = total.astype(bf16)
    fin_u = [lk.put(g.gu_f.at[xm, cm], g.fu_in.at[r], to) for to, xm, cm, rm in members]
    fin_b = [lk.put(g.gb_f.at[2 * cm + xm], g.fb_in.at[r], to) for to, xm, cm, rm in members]
    g.fu_in[r] = g.gu_f[x, c]
    g.fb_in[r] = g.gb_f[2 * c + x]

    lk.got(br_s, g.br_xin)

    def result_tile(j, _):
        at = pl.ds(aligned(256 * j, 256), 256)
        out = br_own(at).reshape(2, 128, 256) + g.tokens[:, :, at].astype(f32)
        g.result[:, :, at] = out.astype(bf16)
        return 0

    lax.fori_loop(0, 4, result_tile, 0)

    for zs in range(4):
        region = g.gd_in.at[zs]
        pltpu.make_async_copy(region, region, lk.recv_sems.at[gd_r + zs]).wait()
    total = g.gd_in[0].astype(f32)
    for zs in range(1, 4):
        total = total + g.gd_in[zs].astype(f32)
    g.o_down[...] = total

    for k in (1, 2, 3):
        lk.got(gv_zs[k], g.gv_in.at[k - 1])
    total = g.gv_z[:, z].astype(f32)
    for k in range(3):
        total = total + g.gv_in[k].astype(f32)
    g.gv_f[...] = total.reshape(2, 2, 32, 128).astype(bf16)
    fin_v = [lk.put(g.gv_f.at[xm, cm], g.fv_in.at[r], to) for to, xm, cm, rm in members]
    g.fv_in[r] = g.gv_f[x, c]

    mine = pl.ds(aligned(16 * x, 16), 16)
    theirs = pl.ds(aligned(16 * (1 - x), 16), 16)
    lk.got(gcoef_s, g.gcoef_in)
    g.o_coef[mine, :] = g.gcoef[x]
    g.o_coef[theirs, :] = g.gcoef_in[...]
    lk.got(skip_s, g.skip_in)
    g.o_skip[mine, :] = g.skip_sum[...]
    g.o_skip[theirs, :] = g.skip_in[...]

    for i, (to, xm, cm, rm) in enumerate(members):
        lk.got(fin_u[i], g.fu_in.at[rm])
        lk.got(fin_b[i], g.fb_in.at[rm])
    for rr in range(4):
        g.o_up[:, 768 * rr : 768 * rr + 768] = g.fu_in[rr].astype(f32)
        g.o_back[:, 768 * rr : 768 * rr + 768] = g.fb_in[rr].astype(f32)

    lk.got(gn_s, g.gn_xin)

    def gn_tile(j, _):
        at = pl.ds(aligned(256 * j, 256), 256)
        g.state[:, at] = gn_own(at)
        return 0

    lax.fori_loop(0, 4, gn_tile, 0)

    def norm_back(i, carry):
        dg, ds = carry
        s_, part = i // 2, pl.ds(aligned(64 * lax.rem(i, 2), 64), 64)
        rows = g.tokens[s_, part, :].astype(f32)
        mean = jnp.mean(rows, axis=-1, keepdims=True)
        cen = rows - mean
        var = jnp.mean(cen * cen, axis=-1, keepdims=True)
        inv = lax.rsqrt(var + 1e-5)
        zn = cen * inv
        gn = g.state[pl.ds(aligned(64 * i, 64), 64), :]
        gg = gn * g.norm_rows[0:1, :]
        m1 = jnp.mean(gg, axis=-1, keepdims=True)
        m2 = jnp.mean(gg * zn, axis=-1, keepdims=True)
        g.g_tokens[s_, part, :] = g.cot[s_, part, :].astype(f32) + inv * (gg - m1 - zn * m2)
        dg = dg + jnp.sum(gn * zn, axis=0, keepdims=True)
        ds = ds + jnp.sum(gn, axis=0, keepdims=True)
        return dg, ds

    blank = jnp.zeros((1, 1024), f32)
    dg, ds = lax.fori_loop(0, 4, norm_back, (blank, blank))
    for zd in range(4):
        g.ng[zd, 0:1, :] = dg[:, 128 * zd : 128 * zd + 128]
        g.ng[zd, 1:2, :] = dg[:, 512 + 128 * zd : 640 + 128 * zd]
        g.ng[zd, 2:3, :] = ds[:, 128 * zd : 128 * zd + 128]
        g.ng[zd, 3:4, :] = ds[:, 512 + 128 * zd : 640 + 128 * zd]
        g.ng[zd, 4:8, :] = jnp.zeros((4, 128), f32)
    ng_s = []
    for k in range(1, 8):
        to = lax.rem(n + k, 8)
        ng_s.append(lk.put(g.ng.at[to // 2], g.ng_in.at[k - 1], (x, 2 * to + c)))
    for i, (to, xm, cm, rm) in enumerate(members):
        lk.got(fin_v[i], g.fv_in.at[rm])
    wide = jnp.concatenate([g.fv_in[rr] for rr in range(4)], axis=1)
    g.o_value[...] = dot_nt(wide, g.perm[...])
    total = g.ng[z]
    for k in range(1, 8):
        lk.got(ng_s[k - 1], g.ng_in.at[k - 1])
        total = total + g.ng_in[k - 1]
    g.ng_f[...] = total
    ng_t = [lk.put(g.ng_f, g.ng_fin.at[i], to) for i, (to, xm, cm, rm) in enumerate(members)]
    for i in range(3):
        lk.got(ng_t[i], g.ng_fin.at[i])
        total = total + g.ng_fin[i]
    total = jnp.where(x == 0, total, pltpu.roll(total, 7, 0))
    g.o_norm[...] = pltpu.roll(total, 128 - (64 * y + 32 * c), 1)
    lk.finish()
    assert lk.count <= N_SEMS


def start_of(copy):
    copy.start()
    return copy


def fast_body(
    tokens, norm_gain, norm_shift, w_up, w_value, w_back, w_down, mode_coef, skip_gain, cotangent
):
    states = 512
    length = tokens.shape[1] * lax.axis_size("tok")
    far_re, far_im, near_hi, near_lo, near_t_hi, near_t_lo = mode_tables(states, length)
    ins = dict(
        tokens=tokens,
        norm_gain=norm_gain.reshape(1, -1),
        norm_shift=norm_shift.reshape(1, -1),
        w_up=w_up,
        w_value=w_value,
        w_back=w_back,
        w_down=w_down,
        mode_coef=mode_coef,
        skip=skip_gain.reshape(1, -1),
        cot=cotangent,
        far_re=far_re,
        far_im=far_im,
        near_hi=near_hi,
        near_lo=near_lo,
        near_t_hi=near_t_hi,
        near_t_lo=near_t_lo,
    )
    outs = dict(
        result=((2, 128, 1024), bf16),
        g_tokens=((2, 128, 1024), f32),
        o_norm=((8, 128), f32),
        o_up=((32, 3072), f32),
        o_value=((32, 512), f32),
        o_back=((16, 3072), f32),
        o_down=((96, 1024), f32),
        o_coef=((32, 512), f32),
        o_skip=((32, 128), f32),
    )
    scratch = dict(
        perm=((512, 512), bf16),
        pk_send=((4, 48, 128), bf16),
        pk=((2, 8, 2, 48, 128), bf16),
        coef=((2, 16, 512), bf16),
        w_up_all=((2, 8, 2, 32, 768), bf16),
        w_back_all=((2, 2, 2, 4, 16, 768), bf16),
        w_down_all=((2, 2, 2, 96, 1024), bf16),
        tok_all=((4, 2, 128, 1024), bf16),
        cot_all=((4, 2, 128, 1024), bf16),
        state=((256, 1024), f32),
        kern=((256, 128), f32),
        toep=((16, 16, 128, 128), bf16),
        norm_rows=((8, 1024), f32),
        w_val=((1024, 128), bf16),
        w_val_t=((128, 1024), bf16),
        normed=((1024, 1024), bf16),
        normed_t=((1024, 1024), bf16),
        val_slope=((128, 1024), f32),
        val=((128, 1024), bf16),
        val_in=((8, 16, 1024), bf16),
        v32=((2048, 128), f32),
        g32=((2048, 128), f32),
        o32=((1024, 128), f32),
        skip_b=((32, 128), f32),
        mix_out=((8, 16, 1024), bf16),
        mix=((4, 128, 1024), bf16),
        act=((1024, 768), f32),
        slope=((1024, 768), f32),
        g_gate=((1024, 768), bf16),
        gm_send=((2, 128, 1024), bf16),
        gm_in=((2, 128, 1024), bf16),
        gm_x=((128, 1024), bf16),
        gm_xin=((128, 1024), bf16),
        gm=((128, 1024), bf16),
        gm_land=((8, 16, 1024), bf16),
        mix_tok=((1024, 512), bf16),
        hidden=((1024, 768), bf16),
        hidden_t=((768, 1024), bf16),
        g_up=((1024, 768), bf16),
        gd=((2, 2, 192, 1024), bf16),
        gd_y=((2, 192, 1024), bf16),
        gd_in=((4, 96, 1024), bf16),
        gu=((2, 4, 128, 768), bf16),
        gu_y=((8, 64, 768), bf16),
        gu_in=((3, 2, 64, 768), bf16),
        gu_f=((2, 2, 32, 768), bf16),
        fu_in=((4, 32, 768), bf16),
        gb=((2, 2, 128, 768), bf16),
        gb_y=((2, 128, 768), bf16),
        gb_z=((4, 4, 16, 768), bf16),
        gb_in=((3, 4, 16, 768), bf16),
        gb_f=((4, 16, 768), bf16),
        fb_in=((4, 16, 768), bf16),
        gv=((8, 128, 128), bf16),
        gv_y=((8, 64, 128), bf16),
        gv_z=((2, 4, 64, 128), bf16),
        gv_in=((3, 2, 64, 128), bf16),
        gv_f=((2, 2, 32, 128), bf16),
        fv_in=((4, 32, 128), bf16),
        xs=((128, 2176), f32),
        gk8=((2176, 128), f32),
        gk=((16, 2176), f32),
        skip_part=((16, 128), f32),
        skip_sum=((16, 128), f32),
        skip_in=((16, 128), f32),
        gcoef=((2, 16, 512), f32),
        gcoef_in=((16, 512), f32),
        gv_out=((8, 16, 1024), bf16),
        g_val=((128, 1024), bf16),
        gvp_t=((1024, 128), bf16),
        br_in=((2, 256, 1024), bf16),
        br_xin=((256, 1024), bf16),
        gn_in=((2, 256, 1024), bf16),
        gn_xin=((256, 1024), bf16),
        ng=((4, 8, 128), f32),
        ng_in=((7, 8, 128), f32),
        ng_f=((8, 128), f32),
        ng_fin=((3, 8, 128), f32),
    )
    names = list(ins) + list(outs) + list(scratch) + ["ssem", "rsem"]
    vmem = pl.BlockSpec(memory_space=pltpu.VMEM)
    got = pl.pallas_call(
        functools.partial(layer_kernel, names),
        out_shape=[jax.ShapeDtypeStruct(s, t) for s, t in outs.values()],
        in_specs=[vmem] * len(ins),
        out_specs=[vmem] * len(outs),
        scratch_shapes=[pltpu.VMEM(s, t) for s, t in scratch.values()]
        + [pltpu.SemaphoreType.DMA((N_SEMS,)), pltpu.SemaphoreType.DMA((N_SEMS,))],
        compiler_params=pltpu.CompilerParams(
            collective_id=0, has_side_effects=True, vmem_limit_bytes=64 << 20
        ),
    )(*ins.values())
    o = types.SimpleNamespace(**dict(zip(outs, got)))
    return (
        o.result,
        o.g_tokens,
        o.o_norm[0, :32],
        o.o_norm[2, :32],
        o.o_up,
        o.o_value,
        o.o_back,
        o.o_down,
        o.o_coef,
        o.o_skip[:, 0],
    )


def run(tokens, *rest):
    sizes = (lax.axis_size("item"), lax.axis_size("tok"), tokens.shape)
    if sizes == (2, 16, (2, 128, 1024)):
        return fast_body(tokens, *rest)
    return body(tokens, *rest)


def solution(mesh):
    in_specs = (
        P("item", "tok", None),
        P(("item", "tok")),
        P(("item", "tok")),
        P(("item", "tok"), None),
        P(("item", "tok"), None),
        P(("item", "tok"), None),
        P(("item", "tok"), None),
        P("tok", "item"),
        P("tok"),
        P("item", "tok", None),
    )
    out_specs = (
        P("item", "tok", None),
        P("item", "tok", None),
        P(("item", "tok")),
        P(("item", "tok")),
        P(("item", "tok"), None),
        P(("item", "tok"), None),
        P(("item", "tok"), None),
        P(("item", "tok"), None),
        P("tok", "item"),
        P("tok"),
    )
    return jax.shard_map(run, mesh=mesh, in_specs=in_specs, out_specs=out_specs, check_vma=False)
```

```python
import functools
import math
import types

import jax
import jax.numpy as jnp
import ml_dtypes
import numpy as np
from jax import lax
from jax.experimental import pallas as pl
from jax.experimental.pallas import tpu as pltpu
from jax.sharding import PartitionSpec as P

highest = lax.Precision.HIGHEST


def basis_block(start_index, block_width, length, states):
    places = start_index + jnp.arange(block_width, dtype=jnp.int32)
    mode_ids = jnp.arange(states, dtype=jnp.int32)
    fraction = (mode_ids * 41 % states).astype(jnp.float32) / states
    mode_rates = jnp.exp(jnp.log(1.0 / 32.0) + fraction * jnp.log(32.0 / (4.0 * length)))
    decays = jnp.exp(-mode_rates[:, None] * places[None, :].astype(jnp.float32))
    phase_turns = (mode_ids[:, None] * places[None, :] % (2 * states)).astype(jnp.float32) * (
        jnp.pi / states
    )
    return jnp.concatenate([decays * jnp.cos(phase_turns), decays * jnp.sin(phase_turns)], axis=0)


def make_kernel(coef_full, length):
    states = coef_full.shape[1] // 2
    block_width = math.gcd(length, 2048)
    block_count = length // block_width

    def one_block(block_index):
        table = basis_block(block_index * block_width, block_width, length, states)
        return jnp.dot(coef_full, table, precision=highest)

    pieces = lax.map(one_block, jnp.arange(block_count, dtype=jnp.int32))
    return jnp.transpose(pieces, (1, 0, 2)).reshape(coef_full.shape[0], length)


def coef_gradient(grad_kernel, states):
    channels, length = grad_kernel.shape
    block_width = math.gcd(length, 2048)
    block_count = length // block_width
    slabs = grad_kernel.reshape(channels, block_count, block_width)

    def add_block(running, block_index):
        slab_part = lax.dynamic_index_in_dim(slabs, block_index, 1, keepdims=False)
        table = basis_block(block_index * block_width, block_width, length, states)
        return (running + jnp.dot(slab_part, table.T, precision=highest), None)

    start_total = jnp.zeros((channels, 2 * states), jnp.float32)
    summed, unused = lax.scan(add_block, start_total, jnp.arange(block_count, dtype=jnp.int32))
    return summed


def unit_tables(row_count, column_count, period):
    row_ids = jnp.arange(row_count, dtype=jnp.int32)[:, None]
    column_ids = jnp.arange(column_count, dtype=jnp.int32)[None, :]
    phase_turns = (row_ids * column_ids % period).astype(jnp.float32) * (2.0 * jnp.pi / period)
    return (jnp.cos(phase_turns), jnp.sin(phase_turns))


def right_product(left_part, table):
    return jnp.einsum("...kq,qm->...km", left_part, table, precision=highest)


def spectrum(signal):
    length = signal.shape[-1]
    padded_size = 2 * length
    outer_size = padded_size // 128
    half_size = outer_size // 2
    folded = signal.reshape(signal.shape[:-1] + (half_size, 128))
    cos_outer, sin_outer = unit_tables(outer_size, half_size, outer_size)
    section_real = jnp.einsum("kp,...pq->...kq", cos_outer, folded, precision=highest)
    section_imag = -jnp.einsum("kp,...pq->...kq", sin_outer, folded, precision=highest)
    twist_cos, twist_sin = unit_tables(outer_size, 128, padded_size)
    turned_real = section_real * twist_cos + section_imag * twist_sin
    turned_imag = section_imag * twist_cos - section_real * twist_sin
    cos_inner, sin_inner = unit_tables(128, 128, 128)
    out_real = right_product(turned_real, cos_inner) + right_product(turned_imag, sin_inner)
    out_imag = right_product(turned_imag, cos_inner) - right_product(turned_real, sin_inner)
    return (out_real, out_imag)


def inverse(spec_real, spec_imag):
    outer_size = spec_real.shape[-2]
    padded_size = outer_size * 128
    half_size = outer_size // 2
    cos_inner, sin_inner = unit_tables(128, 128, 128)
    back_real = right_product(spec_real, cos_inner) - right_product(spec_imag, sin_inner)
    back_imag = right_product(spec_real, sin_inner) + right_product(spec_imag, cos_inner)
    twist_cos, twist_sin = unit_tables(outer_size, 128, padded_size)
    turned_real = back_real * twist_cos - back_imag * twist_sin
    turned_imag = back_real * twist_sin + back_imag * twist_cos
    cos_outer, sin_outer = unit_tables(half_size, outer_size, outer_size)
    signal = jnp.einsum("pk,...kq->...pq", cos_outer, turned_real, precision=highest)
    signal = signal - jnp.einsum("pk,...kq->...pq", sin_outer, turned_imag, precision=highest)
    return signal.reshape(signal.shape[:-2] + (half_size * 128,)) / padded_size


def layer_norm(token_rows, gain_row, shift_row):
    row_mean = jnp.mean(token_rows, axis=-1, keepdims=True)
    centered = token_rows - row_mean
    variance = jnp.mean(centered * centered, axis=-1, keepdims=True)
    return centered * lax.rsqrt(variance + 1e-05) * gain_row + shift_row


def body(
    tokens, norm_gain, norm_shift, w_up, w_value, w_back, w_down, mode_coef, skip_gain, cotangent
):
    gain_full, shift_full, up_full, value_full = (
        lax.all_gather(norm_gain, ("item", "tok"), axis=0, tiled=True),
        lax.all_gather(norm_shift, ("item", "tok"), axis=0, tiled=True),
        lax.all_gather(w_up, ("item", "tok"), axis=0, tiled=True),
        lax.all_gather(w_value, ("item", "tok"), axis=0, tiled=True),
    )
    back_full, down_full = (
        lax.all_gather(w_back, ("item", "tok"), axis=0, tiled=True),
        lax.all_gather(w_down, ("item", "tok"), axis=0, tiled=True),
    )
    coef_full = lax.all_gather(mode_coef, "item", axis=1, tiled=True)
    token_rows = tokens.astype(jnp.float32)
    gain_float = gain_full.astype(jnp.float32)
    shift_float = shift_full.astype(jnp.float32)
    normed = layer_norm(token_rows, gain_float, shift_float).astype(jnp.bfloat16)
    up_pre = jnp.einsum("std,df->stf", normed, up_full, preferred_element_type=jnp.float32)
    value_pre = jnp.einsum("std,dh->sht", normed, value_full, preferred_element_type=jnp.float32)
    value = jax.nn.gelu(value_pre).astype(jnp.bfloat16)
    channel_values = lax.all_to_all(value, "tok", split_axis=1, concat_axis=2, tiled=True)
    length = channel_values.shape[-1]
    kernel = make_kernel(coef_full.astype(jnp.float32), length)
    signal = channel_values.astype(jnp.float32)
    skip_column = skip_gain.astype(jnp.float32)[:, None]
    value_real, value_imag = spectrum(signal)
    kernel_real, kernel_imag = spectrum(kernel)
    conv_out = inverse(
        value_real * kernel_real - value_imag * kernel_imag,
        value_real * kernel_imag + value_imag * kernel_real,
    )
    mixed_channels = (conv_out + skip_column * signal).astype(jnp.bfloat16)
    mixed = lax.all_to_all(mixed_channels, "tok", split_axis=2, concat_axis=1, tiled=True)
    gate = jnp.einsum("sht,hf->stf", mixed, back_full, preferred_element_type=jnp.float32)
    up_act = jax.nn.gelu(up_pre)
    hidden = (up_act * gate).astype(jnp.bfloat16)
    branch = jnp.einsum("stf,fd->std", hidden, down_full, preferred_element_type=jnp.float32)
    result = (token_rows + branch).astype(jnp.bfloat16)
    grad_w_down = jnp.einsum("stf,std->fd", hidden, cotangent, preferred_element_type=jnp.float32)
    grad_hidden = jnp.einsum(
        "std,fd->stf", cotangent, down_full, preferred_element_type=jnp.float32
    )
    grad_gate = (grad_hidden * up_act).astype(jnp.bfloat16)
    grad_up_act = grad_hidden * gate
    grad_w_back = jnp.einsum("sht,stf->hf", mixed, grad_gate, preferred_element_type=jnp.float32)
    grad_mixed = jnp.einsum(
        "stf,hf->sht", grad_gate, back_full, preferred_element_type=jnp.float32
    ).astype(jnp.bfloat16)
    grad_channels = lax.all_to_all(grad_mixed, "tok", split_axis=1, concat_axis=2, tiled=True)
    grad_signal = grad_channels.astype(jnp.float32)
    grad_real, grad_imag = spectrum(grad_signal)
    grad_value_channels = inverse(
        kernel_real * grad_real + kernel_imag * grad_imag,
        kernel_real * grad_imag - kernel_imag * grad_real,
    )
    grad_value_channels = (grad_value_channels + skip_column * grad_signal).astype(jnp.bfloat16)
    grad_kernel = inverse(
        jnp.sum(grad_real * value_real + grad_imag * value_imag, axis=0),
        jnp.sum(grad_imag * value_real - grad_real * value_imag, axis=0),
    )
    grad_skip_part = jnp.sum(grad_signal * signal, axis=(0, 2))
    grad_coef_part = coef_gradient(grad_kernel, coef_full.shape[1] // 2)
    grad_mode_coef = lax.psum_scatter(grad_coef_part, "item", scatter_dimension=1, tiled=True)
    grad_skip_gain = lax.psum(grad_skip_part, "item")
    grad_value = lax.all_to_all(grad_value_channels, "tok", split_axis=2, concat_axis=1, tiled=True)
    gelu_value_back = jax.vjp(jax.nn.gelu, value_pre)[1]
    grad_value_pre = gelu_value_back(grad_value.astype(jnp.float32))[0].astype(jnp.bfloat16)
    gelu_up_back = jax.vjp(jax.nn.gelu, up_pre)[1]
    grad_up_pre = gelu_up_back(grad_up_act)[0].astype(jnp.bfloat16)
    grad_w_up = jnp.einsum("std,stf->df", normed, grad_up_pre, preferred_element_type=jnp.float32)
    grad_w_value = jnp.einsum(
        "std,sht->dh", normed, grad_value_pre, preferred_element_type=jnp.float32
    )
    grad_normed = jnp.einsum(
        "stf,df->std", grad_up_pre, up_full, preferred_element_type=jnp.float32
    )
    grad_normed = grad_normed + jnp.einsum(
        "sht,dh->std", grad_value_pre, value_full, preferred_element_type=jnp.float32
    )
    norm_back = jax.vjp(layer_norm, token_rows, gain_float, shift_float)[1]
    grad_rows, grad_gain_part, grad_shift_part = norm_back(grad_normed)
    grad_tokens = cotangent.astype(jnp.float32) + grad_rows
    owners = lax.axis_size("item") * lax.axis_size("tok")
    norm_flat = jnp.concatenate(
        [grad_gain_part.reshape(owners, -1), grad_shift_part.reshape(owners, -1)], axis=1
    )
    up_flat = grad_w_up.reshape(owners, -1)
    value_flat = grad_w_value.reshape(owners, -1)
    back_flat = grad_w_back.reshape(owners, -1)
    down_flat = grad_w_down.reshape(owners, -1)
    summed = (
        lax.psum_scatter(norm_flat, ("item", "tok"), scatter_dimension=0, tiled=True),
        lax.psum_scatter(up_flat, ("item", "tok"), scatter_dimension=0, tiled=True),
        lax.psum_scatter(value_flat, ("item", "tok"), scatter_dimension=0, tiled=True),
        lax.psum_scatter(back_flat, ("item", "tok"), scatter_dimension=0, tiled=True),
        lax.psum_scatter(down_flat, ("item", "tok"), scatter_dimension=0, tiled=True),
    )
    gain_count = norm_gain.shape[0]
    norm_row = summed[0].reshape(-1)
    grad_norm_gain = norm_row[:gain_count]
    grad_norm_shift = norm_row[gain_count:]
    grad_up_out = summed[1].reshape(w_up.shape)
    grad_value_out = summed[2].reshape(w_value.shape)
    grad_back_out = summed[3].reshape(w_back.shape)
    grad_down_out = summed[4].reshape(w_down.shape)
    return (
        result,
        grad_tokens,
        grad_norm_gain,
        grad_norm_shift,
        grad_up_out,
        grad_value_out,
        grad_back_out,
        grad_down_out,
        grad_mode_coef,
        grad_skip_gain,
    )


MESH_ID = pl.DeviceIdType.MESH
bf16, f32 = jnp.bfloat16, jnp.float32
NT = (((1,), (1,)), ((), ()))
GC = math.sqrt(2.0 / math.pi)


def dot(a, b):
    return jnp.dot(a, b, preferred_element_type=f32)


def dot_nt(a, b):
    return lax.dot_general(a, b, NT, preferred_element_type=f32)


def gelu_parts(v):
    t = jnp.tanh(GC * (v + 0.044715 * v * v * v))
    half = 0.5 * (1.0 + t)
    slope = half + 0.5 * v * (1.0 - t * t) * (GC * (1.0 + 3 * 0.044715 * v * v))
    return v * half, slope


def split(v):
    high = v.astype(bf16)
    return high, (v - high.astype(f32)).astype(bf16)


def mode_tables(states, length):
    n = np.arange(states)
    rates = np.exp(np.log(1.0 / 32.0) + (n * 41 % states) / states * np.log(32.0 / (4.0 * length)))

    def table(places):
        decay = np.exp(-rates[:, None] * places[None, :])
        turn = (n[:, None] * places[None, :] % (2 * states)) * (np.pi / states)
        return decay * np.cos(turn), decay * np.sin(turn)

    far_re, far_im = table(np.arange(0, length, 128))
    near = np.concatenate(table(np.arange(128)), axis=0).astype(np.float32)
    high = near.astype(ml_dtypes.bfloat16)
    low = (near - high.astype(np.float32)).astype(ml_dtypes.bfloat16)
    return (
        far_re.T.astype(np.float32).copy(),
        far_im.T.astype(np.float32).copy(),
        high,
        low,
        high.T[::-1].copy(),
        low.T[::-1].copy(),
    )


class Links:
    def __init__(self, send_sems, recv_sems, place):
        self.send_sems, self.recv_sems, self.place = send_sems, recv_sems, place
        self.count = 0
        self.pending = []

    def take(self, n=1):
        first = self.count
        self.count += n
        return first

    def make(self, src, dst, ssem, rsem, to):
        return pltpu.make_async_remote_copy(
            src_ref=src,
            dst_ref=dst,
            send_sem=self.send_sems.at[ssem],
            recv_sem=self.recv_sems.at[rsem],
            device_id=to,
            device_id_type=MESH_ID,
        )

    def put(self, src, dst, to):
        slot = self.take()
        copy = self.make(src, dst, slot, slot, to)
        copy.start()
        self.pending.append((copy, None))
        return slot

    def got(self, slot, region):
        self.make(region, region, slot, slot, self.place).wait_recv()

    def put_or_keep(self, src, dst, ssem, rsem, to, here):
        remote = self.make(src, dst, ssem, rsem, to)
        local = pltpu.make_async_copy(src, dst, self.recv_sems.at[rsem])
        away = jnp.logical_not(here)
        pl.when(here)(local.start)
        pl.when(away)(remote.start)
        self.pending.append((remote, away))

    def finish(self):
        for copy, away in self.pending:
            if away is None:
                copy.wait_send()
            else:
                pl.when(away)(copy.wait_send)


N_SEMS = 200


def layer_kernel(names, *refs):
    r_ = dict(zip(names, refs))
    g = types.SimpleNamespace(**r_)
    x = lax.axis_index("item")
    tok = lax.axis_index("tok")
    z, y, c = tok // 4, (tok // 2) % 2, tok % 2
    n = tok // 2
    r = 2 * x + c

    def dev(x_, z_, y_, c_):
        return (x_, z_ * 4 + y_ * 2 + c_)

    def zo(k):
        return lax.rem(z + k, 4)

    def zb(k):
        return lax.rem(z + 4 - k, 4)

    def node(z_, y_):
        return 2 * z_ + y_

    sib, xn, diag = dev(x, z, y, 1 - c), dev(1 - x, z, y, c), dev(1 - x, z, y, 1 - c)
    r_sib, r_xn, r_diag = 2 * x + 1 - c, 2 * (1 - x) + c, 2 * (1 - x) + 1 - c
    members = ((sib, x, 1 - c, r_sib), (xn, 1 - x, c, r_xn), (diag, 1 - x, 1 - c, r_diag))
    ynb = dev(x, z, 1 - y, c)
    lk = Links(g.ssem, g.rsem, ynb)
    aligned = pl.multiple_of

    barrier = pltpu.get_barrier_semaphore()
    partners = [m[0] for m in members]
    for k in range(1, 4):
        partners += [dev(x, zo(k), y, c), dev(x, zo(k), 1 - y, c), dev(x, zo(k), y, 1 - c)]
    partners.append(ynb)
    for p in partners:
        pl.semaphore_signal(barrier, inc=1, device_id=p, device_id_type=MESH_ID)

    eye = lax.broadcasted_iota(jnp.int32, (32, 128), 0) == lax.broadcasted_iota(
        jnp.int32, (32, 128), 1
    )
    eye = eye.astype(bf16)
    ch_i = lax.broadcasted_iota(jnp.int32, (512, 128), 0)
    p_i = lax.broadcasted_iota(jnp.int32, (512, 128), 1)
    row16 = lax.broadcasted_iota(jnp.int32, (16, 128), 0)
    gain_row = dot(g.norm_gain[...], eye)
    shift_row = dot(g.norm_shift[...], eye)
    norm_pack = jnp.where(
        row16 == 0,
        jnp.broadcast_to(gain_row, (16, 128)),
        jnp.where(row16 == 1, jnp.broadcast_to(shift_row, (16, 128)), 0.0),
    ).astype(bf16)
    for rr in range(4):
        pick = ch_i == 64 * (p_i // 16) + 32 * (rr % 2) + 16 * (rr // 2) + p_i % 16
        pick = pick.astype(bf16)
        g.perm[:, 128 * rr : 128 * rr + 128] = pick
        g.pk_send[rr, 0:32, :] = dot(g.w_value[...], pick).astype(bf16)
        g.pk_send[rr, 32:48, :] = norm_pack
    pl.semaphore_wait(barrier, len(partners))

    pk_s, up_s, back_s = [], [], []
    for to, xm, cm, rm in members:
        pk_s.append(lk.put(g.pk_send.at[rm], g.pk.at[x, n, c], to))
    coef_s = lk.put(g.mode_coef.at[pl.ds(aligned(16 * (1 - x), 16), 16), :], g.coef.at[x], xn)
    tok_x = lk.put(g.tokens, g.tok_all.at[r], xn)
    my_back = g.w_back_all.at[c, y, x, z]

    def cols(rm):
        return pl.ds(aligned(768 * rm, 128), 768)

    for to, xm, cm, rm in members:
        up_s.append(lk.put(g.w_up.at[:, cols(rm)], g.w_up_all.at[x, n, c], to))
    for to, xm, cm, rm in members:
        back_s.append(lk.put(g.w_back.at[:, cols(rm)], my_back, to))
    tok_sib = lk.put(g.tokens, g.tok_all.at[r], sib)
    cot_x = lk.put(g.cot, g.cot_all.at[r], xn)
    cot_sib = lk.put(g.cot, g.cot_all.at[r], sib)
    g.pk[x, n, c] = g.pk_send[r]
    g.w_up_all[x, n, c] = g.w_up[:, cols(r)]
    g.w_back_all[c, y, x, z] = g.w_back[:, cols(r)]
    g.cot_all[r] = g.cot[...]
    g.coef[x] = g.mode_coef[pl.ds(aligned(16 * x, 16), 16), :]

    def gather_start(region):
        slots = {}
        for k in (1, 2, 3):
            slots[k] = lk.put(region(z, y), region(z, y), dev(x, zo(k), y, c))
        slots[4] = lk.put(region(z, y), region(z, y), ynb)
        return slots

    def gather_pass(slots, region, k):
        lk.got(slots[k], region(zb(k), y))
        slots[4 + k] = lk.put(region(zb(k), y), region(zb(k), y), ynb)

    def gather_end(slots, region):
        for k in range(4):
            lk.got(slots[4 + k], region(zb(k), 1 - y))

    def pk_region(z_, y_):
        return g.pk.at[:, node(z_, y_)]

    def up_region(z_, y_):
        return g.w_up_all.at[:, node(z_, y_)]

    def back_region(z_, y_):
        return g.w_back_all.at[:, y_, :, z_]

    for i, (to, xm, cm, rm) in enumerate(members):
        lk.got(pk_s[i], g.pk.at[xm, n, cm])
    pk_g = gather_start(pk_region)

    dn_r = lk.take(4)
    dn_slot = dn_r + 2 * lax.rem(z, 2) + c
    dst = g.w_down_all.at[lax.rem(z, 2), y, c]
    owner = z // 2
    lk.put_or_keep(g.w_down, dst, lk.take(), dn_slot, dev(x, z, y, owner), owner == c)
    for k in (1, 2, 3):
        lk.pending.append(
            (start_of(lk.make(g.w_down, dst, lk.take(), dn_slot, dev(x, zo(k), y, owner))), None)
        )
    dn_first = jnp.where(owner == c, lax.rem(z, 2), 1 - c)
    dn_y = lk.take(2)

    def down_pass(zl):
        for cm in range(2):
            region = g.w_down_all.at[zl, y, cm]
            pltpu.make_async_copy(region, region, lk.recv_sems.at[dn_r + 2 * zl + cm]).wait()
        region = g.w_down_all.at[zl, y]
        lk.pending.append((start_of(lk.make(region, region, lk.take(), dn_y + zl, ynb)), None))

    lk.got(coef_s, g.coef.at[1 - x])
    cc = g.coef[0].astype(f32)
    sc = g.coef[1].astype(f32)

    def far(p, _):
        hr = g.far_re[pl.ds(p, 1), :]
        hi = g.far_im[pl.ds(p, 1), :]
        rows = pl.ds(aligned(16 * p, 16), 16)
        g.state[rows, 0:512] = cc * hr + sc * hi
        g.state[rows, 512:1024] = sc * hr - cc * hi
        return 0

    lax.fori_loop(0, 16, far, 0)
    for half in range(2):
        rows = slice(128 * half, 128 * half + 128)
        hi_, lo_ = split(g.state[rows, :])
        g.kern[rows, :] = (
            dot(hi_, g.near_hi[...]) + dot(lo_, g.near_hi[...]) + dot(hi_, g.near_lo[...])
        )
    for k in (1, 2, 3):
        gather_pass(pk_g, pk_region, k)
    ii = lax.broadcasted_iota(jnp.int32, (128, 128), 0)
    jj = lax.broadcasted_iota(jnp.int32, (128, 128), 1)
    flip = (ii + jj == 127).astype(bf16)

    def toeplitz(h, _):
        prev = jnp.zeros((128, 128), f32)
        for k in range(16):
            row = jnp.broadcast_to(g.kern[pl.ds(16 * k + h, 1), :], (128, 128))
            turned = pltpu.roll(row, 0, 1, stride=1, stride_axis=0)
            g.toep[h, k] = jnp.where(jj >= ii, turned, prev).astype(bf16)
            prev = turned
        return 0

    lax.fori_loop(0, 16, toeplitz, 0)
    down_pass(dn_first)

    gather_end(pk_g, pk_region)
    e_i = lax.broadcasted_iota(jnp.int32, (128, 1024), 0)
    e_j = lax.broadcasted_iota(jnp.int32, (128, 1024), 1)
    spread = jnp.logical_and(e_i < 32, lax.rem(e_j, 32) == e_i).astype(bf16)
    blk = lax.broadcasted_iota(jnp.int32, (16, 1024), 1) // 32
    acc = jnp.zeros((16, 1024), f32)
    for xm in range(2):
        for nm in range(8):
            for cm in range(2):
                rows = g.pk[xm, nm, cm, 32:48, :]
                acc = acc + jnp.where(
                    blk == 16 * xm + 2 * nm + cm, dot(rows, spread), 0.0
                )
    gain = acc[0:1, :]
    shift = acc[1:2, :]
    g.norm_rows[0:1, :] = gain
    g.norm_rows[1:2, :] = shift
    wv = g.pk[:, :, :, 0:32, :].reshape(1024, 128)
    g.w_val[...] = wv
    wvt = wv.T
    for t in range(8):
        at = 256 * (t % 4) + 128 * (t // 4)
        g.w_val_t[:, at : at + 128] = wvt[:, 128 * t : 128 * t + 128]

    def norm_block(read, q):
        def part(s_, _):
            rows = read(s_).astype(f32)
            mean = jnp.mean(rows, axis=-1, keepdims=True)
            cen = rows - mean
            var = jnp.mean(cen * cen, axis=-1, keepdims=True)
            out = (cen * lax.rsqrt(var + 1e-5) * g.norm_rows[0:1, :] + g.norm_rows[1:2, :]).astype(
                bf16
            )
            at = aligned(256 * q + 128 * s_, 128)
            g.normed[pl.ds(at, 128), :] = out
            for t in range(8):
                low = 256 * (t % 4) + 128 * (t // 4)
                g.normed_t[low : low + 128, pl.ds(at, 128)] = out[:, 128 * t : 128 * t + 128].T
            return 0

        lax.fori_loop(0, 2, part, 0)
        at = pl.ds(aligned(256 * q, 128), 256)
        pre = dot(g.w_val_t[...], g.normed_t[:, at])
        act, slope = gelu_parts(pre)
        g.val_slope[:, at] = slope
        g.val[:, at] = act.astype(bf16)

    norm_block(lambda s_: g.tokens[s_], r)
    lk.got(tok_sib, g.tok_all.at[r_sib])
    norm_block(lambda s_: g.tok_all[r_sib, s_], r_sib)
    lk.got(tok_x, g.tok_all.at[r_xn])
    tok_f = lk.put(g.tok_all.at[r_xn], g.tok_all.at[r_xn], sib)
    norm_block(lambda s_: g.tok_all[r_xn, s_], r_xn)
    lk.got(tok_f, g.tok_all.at[r_diag])
    norm_block(lambda s_: g.tok_all[r_diag, s_], r_diag)

    def channel_send(src, landing):
        slots = []
        for k in range(1, 8):
            to = lax.rem(n + k, 8)
            slots.append(
                lk.put(
                    src.at[pl.ds(aligned(16 * to, 16), 16), :],
                    landing.at[n],
                    (x, 2 * to + c),
                )
            )
        return slots

    def channel_got(slots, landing):
        for k in range(1, 8):
            lk.got(slots[k - 1], landing.at[lax.rem(n + 8 - k, 8)])

    def unpack(landing, put):
        def one(nm, _):
            for tb in range(8):
                s_, cm = 2 * (tb // 4) + tb % 2, (tb // 2) % 2
                put(s_, 2 * nm + cm, landing[nm, :, 128 * tb : 128 * tb + 128].astype(f32))
            return 0

        lax.fori_loop(0, 8, one, 0)

    def put_val(s_, i, tile):
        g.v32[pl.ds(aligned((32 * s_ + 16 + i) * 16, 16), 16), :] = tile
        g.vr32[pl.ds(aligned((16 * s_ + 15 - i) * 16, 16), 16), :] = tile

    def put_grad(s_, i, tile):
        g.v32[pl.ds(aligned((32 * s_ + 31 - i) * 16, 16), 16), :] = tile

    val_s = channel_send(g.val, g.val_in)
    g.val_in[n] = g.val[pl.ds(aligned(16 * n, 16), 16), :]
    for i, (to, xm, cm, rm) in enumerate(members):
        lk.got(up_s[i], g.w_up_all.at[xm, n, cm])
    up_g = gather_start(up_region)
    down_pass(1 - dn_first)

    zero = jnp.zeros((256, 128), f32)
    for s_ in range(4):
        g.v32[pl.ds(512 * s_, 256), :] = zero
    diag_i = lax.broadcasted_iota(jnp.int32, (32, 32), 0) == lax.broadcasted_iota(
        jnp.int32, (32, 32), 1
    )
    skip_row = jnp.broadcast_to(g.skip[...].astype(f32), (32, 32))
    g.skip_b[...] = dot(jnp.where(diag_i, skip_row, 0.0).astype(bf16), jnp.ones((32, 128), bf16))
    gather_pass(up_g, up_region, 1)

    channel_got(val_s, g.val_in)
    unpack(g.val_in, put_val)

    def conv_rows(h, k):
        rows = [g.v32[pl.ds((32 * s_ + 16 - k) * 16 + h, 16, stride=16), :] for s_ in range(4)]
        return jnp.concatenate(rows, axis=0)

    def conv(h, _):
        parts = [conv_rows(h, k) for k in range(16)]
        out = g.skip_b[pl.ds(16 * x + h, 1), :] * parts[0]
        for kk in range(8):
            lhs = jnp.concatenate([parts[2 * kk], parts[2 * kk + 1]], axis=1).astype(bf16)
            out = out + dot(lhs, g.toep[h, 2 * kk : 2 * kk + 2].reshape(256, 128))
        g.o32[pl.ds(h, 64, stride=16), :] = out
        return 0

    def pack(out, back):
        def one(nm, _):
            for tb in range(8):
                s_, cm = 2 * (tb // 4) + tb % 2, (tb // 2) % 2
                i = 2 * nm + cm
                at = aligned((16 * s_ + (15 - i if back else i)) * 16, 16)
                out[nm, :, 128 * tb : 128 * tb + 128] = g.o32[pl.ds(at, 16), :].astype(bf16)
            return 0

        lax.fori_loop(0, 8, one, 0)

    def channel_back(src, landing):
        slots = []
        for k in range(1, 8):
            to = lax.rem(n + k, 8)
            slots.append(
                lk.put(src.at[to], landing.at[pl.ds(aligned(16 * n, 16), 16), :], (x, 2 * to + c))
            )
        return slots

    def channel_back_got(slots, landing):
        for k in range(1, 8):
            at = aligned(16 * lax.rem(n + 8 - k, 8), 16)
            lk.got(slots[k - 1], landing.at[pl.ds(at, 16), :])

    lax.fori_loop(0, 16, conv, 0, unroll=2)
    pack(g.mix_out, False)
    mix_s = channel_back(g.mix_out, g.mix.at[r])
    g.mix[r, pl.ds(aligned(16 * n, 16), 16), :] = g.mix_out[n]

    gather_pass(up_g, up_region, 2)
    for i, (to, xm, cm, rm) in enumerate(members):
        lk.got(back_s[i], g.w_back_all.at[cm, y, xm, z])
    back_g = gather_start(back_region)
    lk.got(cot_x, g.cot_all.at[r_xn])
    cot_f = lk.put(g.cot_all.at[r_xn], g.cot_all.at[r_xn], sib)
    gather_pass(up_g, up_region, 3)
    for zl in range(2):
        region = g.w_down_all.at[zl, 1 - y]
        pltpu.make_async_copy(region, region, lk.recv_sems.at[dn_y + zl]).wait()
    lk.got(cot_sib, g.cot_all.at[r_sib])
    lk.got(cot_f, g.cot_all.at[r_diag])
    down2d = g.w_down_all.reshape(768, 1024)
    cot2d = g.cot_all.reshape(1024, 1024)

    def hidden_tile(q, _):
        rows = pl.ds(aligned(256 * q, 256), 256)
        g.slope[rows, :] = dot_nt(cot2d[rows, :], down2d[...])
        return 0

    lax.fori_loop(0, 4, hidden_tile, 0)
    channel_back_got(mix_s, g.mix.at[r])
    mix_x = lk.put(g.mix.at[r], g.mix.at[r], xn)
    mix_sib = lk.put(g.mix.at[r], g.mix.at[r], sib)
    gather_pass(back_g, back_region, 1)

    gather_end(up_g, up_region)
    up2d = g.w_up_all.reshape(1024, 768)

    def up_tile(q, _):
        rows = pl.ds(aligned(256 * q, 256), 256)
        act, slope = gelu_parts(dot(g.normed[rows, :], up2d[...]))
        gh = g.slope[rows, :]
        g.act[rows, :] = act
        g.g_gate[rows, :] = (gh * act).astype(bf16)
        g.slope[rows, :] = gh * slope
        return 0

    lax.fori_loop(0, 2, up_tile, 0)
    gather_pass(back_g, back_region, 2)
    lax.fori_loop(2, 4, up_tile, 0)
    gather_pass(back_g, back_region, 3)
    lk.got(mix_x, g.mix.at[r_xn])
    mix_f = lk.put(g.mix.at[r_xn], g.mix.at[r_xn], sib)
    gather_end(back_g, back_region)
    back2d = g.w_back_all.reshape(512, 768)

    def mixed_part(ranks, q):
        w = [back2d[pl.ds(aligned(128 * rr, 128), 128), :] for rr in ranks]
        w = w[0] if len(w) == 1 else jnp.concatenate(w, axis=0)
        return dot_nt(w, g.g_gate[pl.ds(aligned(512 * q, 512), 512), :])

    def gm_sib(q, _):
        at = pl.ds(aligned(512 * q, 128), 512)
        both = mixed_part((1 - c, 2 + 1 - c), q).astype(bf16)
        g.gm_send[:, :, at] = both.reshape(2, 128, 512)
        return 0

    lax.fori_loop(0, 2, gm_sib, 0)
    gm_s = lk.put(g.gm_send, g.gm_in, sib)

    def gm_mine(q, _):
        at = pl.ds(aligned(512 * q, 128), 512)
        both = mixed_part((2 * (1 - x) + c, 2 * x + c), q)
        g.gm_x[:, at] = both[0:128, :].astype(bf16)
        g.gm_own[:, at] = both[128:256, :]
        return 0

    lax.fori_loop(0, 2, gm_mine, 0)
    lk.got(gm_s, g.gm_in)
    g.gm_x[...] = (g.gm_x[...].astype(f32) + g.gm_in[1 - x].astype(f32)).astype(bf16)
    gm_xs = lk.put(g.gm_x, g.gm_xin, xn)

    lk.got(mix_sib, g.mix.at[r_sib])
    lk.got(mix_f, g.mix.at[r_diag])

    def turn(i, _):
        rr, tb = i // 8, lax.rem(i, 8)
        rows = pl.ds(aligned(128 * tb, 128), 128)
        at = pl.ds(aligned(128 * rr, 128), 128)
        g.mix_tok[rows, at] = g.mix[rr, :, rows].T
        return 0

    lax.fori_loop(0, 32, turn, 0, unroll=4)

    def gate_tile(q, _):
        rows = pl.ds(aligned(256 * q, 256), 256)
        gate = dot(g.mix_tok[rows, :], back2d[...])
        hidden = (g.act[rows, :] * gate).astype(bf16)
        g.hidden[rows, :] = hidden
        g.hidden_t[:, rows] = hidden.T
        g.g_up[rows, :] = (g.slope[rows, :] * gate).astype(bf16)
        return 0

    lax.fori_loop(0, 4, gate_tile, 0)

    gd_y = []

    def down_grad(zl):
        def tile(i, _):
            at = pl.ds(aligned(512 * i, 512), 512)
            part = dot(g.hidden_t[384 * zl : 384 * zl + 384, :], cot2d[:, at]).astype(bf16)
            g.gd[zl, :, :, at] = part.reshape(2, 192, 512)
            return 0

        lax.fori_loop(0, 2, tile, 0)
        gd_y.append(lk.put(g.gd.at[zl, 1 - y], g.gd_y.at[zl], ynb))

    down_grad(0)

    lk.got(gm_xs, g.gm_xin)
    for tb in range(8):
        at = slice(128 * tb, 128 * tb + 128)
        total = g.gm_own[:, at] + g.gm_in[x, :, at].astype(f32) + g.gm_xin[:, at].astype(f32)
        g.gm[:, at] = dot(total.astype(bf16), flip).astype(bf16)
    gm_cs = channel_send(g.gm, g.gm_land)
    g.gm_land[n] = g.gm[pl.ds(aligned(16 * n, 16), 16), :]

    down_grad(1)
    gd_r = lk.take(4)

    def down_sum(zl):
        lk.got(gd_y[zl], g.gd_y.at[zl])
        for cm in range(2):
            part = pl.ds(96 * cm, 96)
            total = g.gd[zl, y, part, :].astype(f32) + g.gd_y[zl, part, :].astype(f32)
            g.gd[zl, y, part, :] = total.astype(bf16)
            z_d = 2 * c + zl
            here = jnp.logical_and(z_d == z, c == cm)
            lk.put_or_keep(
                g.gd.at[zl, y, part], g.gd_in.at[z], lk.take(), gd_r + z, dev(x, z_d, y, cm), here
            )

    channel_got(gm_cs, g.gm_land)
    unpack(g.gm_land, put_grad)
    down_sum(0)

    def conv_back(h, _):
        parts = [conv_rows(h, k) for k in range(16)]
        own = g.vr32[pl.ds(h, 64, stride=16), :].T.astype(bf16)
        out = g.skip_b[pl.ds(16 * x + h, 1), :] * parts[0]
        lhs = []
        for kk in range(8):
            lhs.append(jnp.concatenate([parts[2 * kk], parts[2 * kk + 1]], axis=1).astype(bf16))
            out = out + dot(lhs[kk], g.toep[h, 2 * kk : 2 * kk + 2].reshape(256, 128))
        g.o32[pl.ds(h, 64, stride=16), :] = out
        after = jnp.zeros((128, 128), f32)
        for kk in range(7, -1, -1):
            pair = dot(own, lhs[kk])
            for half in (1, 0):
                turned = pltpu.roll(
                    pair[:, 128 * half : 128 * half + 128], 0, 1, stride=1, stride_axis=0
                )
                lag = jnp.where(jj >= ii, turned, after)
                after = turned
                at = pl.ds(aligned((16 * (2 * kk + half) + h) * 8, 8), 8)
                g.gk8[at, :] = jnp.sum(lag.reshape(16, 8, 128), axis=0)
        return 0

    lax.fori_loop(0, 16, conv_back, 0)
    pack(g.gv_out, True)
    gv_s = channel_back(g.gv_out, g.g_val)
    g.g_val[pl.ds(aligned(16 * n, 16), 16), :] = g.gv_out[n]

    other = pl.ds(aligned(64 * (1 - y), 64), 64)
    own64 = pl.ds(aligned(64 * y, 64), 64)
    up_y, gu_s = {}, {}

    def up_grad(k):
        z_d = zo(k)
        rows = pl.ds(aligned(256 * z_d, 256), 256)
        part = dot(g.normed_t[rows, :], g.g_up[...]).astype(bf16)
        g.gu[z_d] = part.reshape(2, 128, 768)
        up_y[k] = lk.put(g.gu.at[z_d, :, other], g.gu_y.at[z_d], ynb)

    def up_sum(k):
        z_d = zo(k)
        lk.got(up_y[k], g.gu_y.at[z_d])
        total = g.gu[z_d, :, own64, :].astype(f32) + g.gu_y[z_d].astype(f32)
        g.gu[z_d, :, own64, :] = total.astype(bf16)
        if k:
            gu_s[k] = lk.put(g.gu.at[z_d, :, own64], g.gu_in.at[k - 1], dev(x, z_d, y, c))

    up_grad(2)
    up_grad(1)
    up_grad(3)
    up_grad(0)
    down_sum(1)

    mix2d = g.mix.reshape(512, 1024)

    def back_tile(i, _):
        at = pl.ds(aligned(384 * i, 128), 384)
        part = dot(mix2d[...], g.g_gate[:, at]).astype(bf16)
        g.gb[:, :, :, at] = part.reshape(2, 2, 128, 384)
        return 0

    lax.fori_loop(0, 2, back_tile, 0)
    gb_y = lk.put(g.gb.at[:, 1 - y], g.gb_y, ynb)

    tall = g.gk8[pl.ds(0, 256, stride=8), :]
    for s_ in range(1, 8):
        tall = tall + g.gk8[pl.ds(s_, 256, stride=8), :]
    for half in range(2):
        hi_, lo_ = split(tall[128 * half : 128 * half + 128, :])
        g.state[128 * half : 128 * half + 128, :] = (
            dot(hi_, g.near_t_hi[...]) + dot(lo_, g.near_t_hi[...]) + dot(hi_, g.near_t_lo[...])
        )
    g.skip_sum[...] = tall[0:16, :]

    def far_back(p, carry):
        gc, gs = carry
        hr = g.far_re[pl.ds(p, 1), :]
        hi = g.far_im[pl.ds(p, 1), :]
        rows = pl.ds(aligned(16 * p, 16), 16)
        ur = g.state[rows, 0:512]
        ui = g.state[rows, 512:1024]
        return gc + hr * ur - hi * ui, gs + hr * ui + hi * ur

    blank = jnp.zeros((16, 512), f32)
    gc, gs = lax.fori_loop(0, 16, far_back, (blank, blank))
    g.gcoef[0] = gc
    g.gcoef[1] = gs
    gcoef_s = lk.put(g.gcoef.at[1 - x], g.gcoef_in, xn)
    skip_s = lk.put(g.skip_sum, g.skip_in, xn)

    channel_back_got(gv_s, g.g_val)
    for tb in range(8):
        at = slice(128 * tb, 128 * tb + 128)
        back = dot(g.g_val[:, at], flip)
        g.gvp_t[at, :] = (back * g.val_slope[:, at]).astype(bf16).T
    part = dot(g.normed_t[...], g.gvp_t[...]).astype(bf16)
    g.gv[...] = part.reshape(4, 2, 128, 128)
    gv_y = lk.put(g.gv.at[:, :, other], g.gv_y, ynb)

    def group_sum(part, send, land, xsend, xland):
        for xm in range(2):
            send[xm] = part(xm, 1 - c).astype(bf16)
        first = lk.put(send, land, sib)
        mine = part(1 - x, c)
        lk.got(first, land)
        xsend[...] = (mine + land[1 - x].astype(f32)).astype(bf16)
        second = lk.put(xsend, xland, xn)

        def own():
            return part(x, c) + land[x].astype(f32) + xland[...].astype(f32)

        return second, own

    def branch_part(xm, cm):
        rows = pl.ds(aligned(256 * (2 * xm + cm), 256), 256)
        return dot(g.hidden[rows, :], down2d[...])

    def normed_part(xm, cm):
        rows = pl.ds(aligned(256 * (2 * xm + cm), 256), 256)
        return dot_nt(g.g_up[rows, :], up2d[...]) + dot_nt(g.gvp_t[rows, :], g.w_val[...])

    spare = g.normed.reshape(2, 2, 256, 1024)
    gn_s, gn_own = group_sum(
        normed_part, spare.at[1], g.gn_in, g.tok_all.at[r_sib].reshape(256, 1024), g.gn_xin
    )
    up_sum(2)
    up_sum(1)
    br_s, br_own = group_sum(
        branch_part, spare.at[0], g.br_in, g.tok_all.at[r].reshape(256, 1024), g.br_xin
    )
    up_sum(3)
    up_sum(0)

    lk.got(gb_y, g.gb_y)
    total = g.gb[:, y].astype(f32) + g.gb_y[...].astype(f32)
    g.gb_z[...] = total.astype(bf16).reshape(4, 4, 16, 768)
    gb_s = {}
    for k in (2, 1, 3):
        gb_s[k] = lk.put(g.gb_z.at[:, zo(k)], g.gb_in.at[k - 1], dev(x, zo(k), y, c))
    lk.got(gv_y, g.gv_y)
    g.gv_z[...] = (g.gv[:, :, own64, :].astype(f32) + g.gv_y[...].astype(f32)).astype(bf16)
    gv_zs = {}
    for k in (2, 1, 3):
        gv_zs[k] = lk.put(g.gv_z.at[zo(k)], g.gv_in.at[k - 1], dev(x, zo(k), y, c))

    lk.got(gn_s, g.gn_xin)
    g.state[...] = gn_own()

    def norm_back(i, carry):
        dg, ds = carry
        s_, part = i // 2, pl.ds(aligned(64 * lax.rem(i, 2), 64), 64)
        rows = g.tokens[s_, part, :].astype(f32)
        mean = jnp.mean(rows, axis=-1, keepdims=True)
        cen = rows - mean
        var = jnp.mean(cen * cen, axis=-1, keepdims=True)
        inv = lax.rsqrt(var + 1e-5)
        zn = cen * inv
        gn = g.state[pl.ds(aligned(64 * i, 64), 64), :]
        gg = gn * g.norm_rows[0:1, :]
        m1 = jnp.mean(gg, axis=-1, keepdims=True)
        m2 = jnp.mean(gg * zn, axis=-1, keepdims=True)
        g.g_tokens[s_, part, :] = g.cot[s_, part, :].astype(f32) + inv * (gg - m1 - zn * m2)
        dg = dg + jnp.sum(gn * zn, axis=0, keepdims=True)
        ds = ds + jnp.sum(gn, axis=0, keepdims=True)
        return dg, ds

    blank = jnp.zeros((1, 1024), f32)
    dg, ds = lax.fori_loop(0, 4, norm_back, (blank, blank))
    for zd in range(4):
        g.ng[zd, 0:1, :] = dg[:, 128 * zd : 128 * zd + 128]
        g.ng[zd, 1:2, :] = dg[:, 512 + 128 * zd : 640 + 128 * zd]
        g.ng[zd, 2:3, :] = ds[:, 128 * zd : 128 * zd + 128]
        g.ng[zd, 3:4, :] = ds[:, 512 + 128 * zd : 640 + 128 * zd]
        g.ng[zd, 4:8, :] = jnp.zeros((4, 128), f32)
    ng_s = []
    for k in range(1, 8):
        to = lax.rem(n + k, 8)
        ng_s.append(lk.put(g.ng.at[to // 2], g.ng_in.at[k - 1], (x, 2 * to + c)))

    lk.got(br_s, g.br_xin)
    out = br_own().reshape(2, 128, 1024) + g.tokens[...].astype(f32)
    g.result[...] = out.astype(bf16)

    for k in (2, 1, 3):
        lk.got(gu_s[k], g.gu_in.at[k - 1])
    total = g.gu[z, :, own64, :].astype(f32)
    for k in range(3):
        total = total + g.gu_in[k].astype(f32)
    g.gu_f[...] = total.reshape(2, 2, 32, 768).astype(bf16)
    fin_u = [lk.put(g.gu_f.at[xm, cm], g.fu_in.at[r], to) for to, xm, cm, rm in members]
    for k in (2, 1, 3):
        lk.got(gb_s[k], g.gb_in.at[k - 1])
    total = g.gb_z[:, z].astype(f32)
    for k in range(3):
        total = total + g.gb_in[k].astype(f32)
    g.gb_f[...] = total.astype(bf16)
    fin_b = [lk.put(g.gb_f.at[2 * cm + xm], g.fb_in.at[r], to) for to, xm, cm, rm in members]
    for k in (2, 1, 3):
        lk.got(gv_zs[k], g.gv_in.at[k - 1])
    total = g.gv_z[z].astype(f32)
    for k in range(3):
        total = total + g.gv_in[k].astype(f32)
    g.gv_f[...] = total.reshape(2, 2, 32, 128).astype(bf16)
    fin_v = [lk.put(g.gv_f.at[xm, cm], g.fv_in.at[r], to) for to, xm, cm, rm in members]
    g.fu_in[r] = g.gu_f[x, c]
    g.fb_in[r] = g.gb_f[2 * c + x]
    g.fv_in[r] = g.gv_f[x, c]

    for zs in range(4):
        region = g.gd_in.at[zs]
        pltpu.make_async_copy(region, region, lk.recv_sems.at[gd_r + zs]).wait()
    total = g.gd_in[0].astype(f32)
    for zs in range(1, 4):
        total = total + g.gd_in[zs].astype(f32)
    g.o_down[...] = total

    mine = pl.ds(aligned(16 * x, 16), 16)
    theirs = pl.ds(aligned(16 * (1 - x), 16), 16)
    lk.got(gcoef_s, g.gcoef_in)
    g.o_coef[mine, :] = g.gcoef[x]
    g.o_coef[theirs, :] = g.gcoef_in[...]
    lk.got(skip_s, g.skip_in)
    g.o_skip[mine, :] = g.skip_sum[...]
    g.o_skip[theirs, :] = g.skip_in[...]

    total = g.ng[z]
    for k in range(1, 8):
        lk.got(ng_s[k - 1], g.ng_in.at[k - 1])
        total = total + g.ng_in[k - 1]
    g.ng_f[...] = total
    ng_t = [lk.put(g.ng_f, g.ng_fin.at[i], to) for i, (to, xm, cm, rm) in enumerate(members)]

    for i, (to, xm, cm, rm) in enumerate(members):
        lk.got(fin_u[i], g.fu_in.at[rm])
        lk.got(fin_b[i], g.fb_in.at[rm])
        lk.got(fin_v[i], g.fv_in.at[rm])
    for rr in range(4):
        g.o_up[:, 768 * rr : 768 * rr + 768] = g.fu_in[rr].astype(f32)
        g.o_back[:, 768 * rr : 768 * rr + 768] = g.fb_in[rr].astype(f32)
    wide = jnp.concatenate([g.fv_in[rr] for rr in range(4)], axis=1)
    g.o_value[...] = dot_nt(wide, g.perm[...])
    for i in range(3):
        lk.got(ng_t[i], g.ng_fin.at[i])
        total = total + g.ng_fin[i]
    total = jnp.where(x == 0, total, pltpu.roll(total, 7, 0))
    g.o_norm[...] = pltpu.roll(total, 128 - (64 * y + 32 * c), 1)
    lk.finish()
    assert lk.count <= N_SEMS


def start_of(copy):
    copy.start()
    return copy


def fast_body(
    tokens, norm_gain, norm_shift, w_up, w_value, w_back, w_down, mode_coef, skip_gain, cotangent
):
    states = 512
    length = tokens.shape[1] * lax.axis_size("tok")
    far_re, far_im, near_hi, near_lo, near_t_hi, near_t_lo = mode_tables(states, length)
    ins = dict(
        tokens=tokens,
        norm_gain=norm_gain.reshape(1, -1),
        norm_shift=norm_shift.reshape(1, -1),
        w_up=w_up,
        w_value=w_value,
        w_back=w_back,
        w_down=w_down,
        mode_coef=mode_coef,
        skip=skip_gain.reshape(1, -1),
        cot=cotangent,
        far_re=far_re,
        far_im=far_im,
        near_hi=near_hi,
        near_lo=near_lo,
        near_t_hi=near_t_hi,
        near_t_lo=near_t_lo,
    )
    outs = dict(
        result=((2, 128, 1024), bf16),
        g_tokens=((2, 128, 1024), f32),
        o_norm=((8, 128), f32),
        o_up=((32, 3072), f32),
        o_value=((32, 512), f32),
        o_back=((16, 3072), f32),
        o_down=((96, 1024), f32),
        o_coef=((32, 512), f32),
        o_skip=((32, 128), f32),
    )
    scratch = dict(
        perm=((512, 512), bf16),
        pk_send=((4, 48, 128), bf16),
        pk=((2, 8, 2, 48, 128), bf16),
        coef=((2, 16, 512), bf16),
        w_up_all=((2, 8, 2, 32, 768), bf16),
        w_back_all=((2, 2, 2, 4, 16, 768), bf16),
        w_down_all=((2, 2, 2, 96, 1024), bf16),
        tok_all=((4, 2, 128, 1024), bf16),
        cot_all=((4, 2, 128, 1024), bf16),
        state=((256, 1024), f32),
        kern=((256, 128), f32),
        toep=((16, 16, 128, 128), bf16),
        norm_rows=((8, 1024), f32),
        w_val=((1024, 128), bf16),
        w_val_t=((128, 1024), bf16),
        normed=((1024, 1024), bf16),
        normed_t=((1024, 1024), bf16),
        val_slope=((128, 1024), f32),
        val=((128, 1024), bf16),
        val_in=((8, 16, 1024), bf16),
        v32=((2048, 128), f32),
        vr32=((1024, 128), f32),
        o32=((1024, 128), f32),
        skip_b=((32, 128), f32),
        mix_out=((8, 16, 1024), bf16),
        mix=((4, 128, 1024), bf16),
        act=((1024, 768), f32),
        slope=((1024, 768), f32),
        g_gate=((1024, 768), bf16),
        gm_send=((2, 128, 1024), bf16),
        gm_in=((2, 128, 1024), bf16),
        gm_x=((128, 1024), bf16),
        gm_xin=((128, 1024), bf16),
        gm=((128, 1024), bf16),
        gm_land=((8, 16, 1024), bf16),
        mix_tok=((1024, 512), bf16),
        hidden=((1024, 768), bf16),
        hidden_t=((768, 1024), bf16),
        g_up=((1024, 768), bf16),
        gd=((2, 2, 192, 1024), bf16),
        gd_y=((2, 192, 1024), bf16),
        gd_in=((4, 96, 1024), bf16),
        gu=((4, 2, 128, 768), bf16),
        gu_y=((4, 2, 64, 768), bf16),
        gu_in=((3, 2, 64, 768), bf16),
        gu_f=((2, 2, 32, 768), bf16),
        fu_in=((4, 32, 768), bf16),
        gb=((2, 2, 128, 768), bf16),
        gb_y=((2, 128, 768), bf16),
        gb_z=((4, 4, 16, 768), bf16),
        gb_in=((3, 4, 16, 768), bf16),
        gb_f=((4, 16, 768), bf16),
        fb_in=((4, 16, 768), bf16),
        gv=((4, 2, 128, 128), bf16),
        gv_y=((4, 2, 64, 128), bf16),
        gv_z=((4, 2, 64, 128), bf16),
        gv_in=((3, 2, 64, 128), bf16),
        gv_f=((2, 2, 32, 128), bf16),
        fv_in=((4, 32, 128), bf16),
        gk8=((2048, 128), f32),
        gm_own=((128, 1024), f32),
        skip_sum=((16, 128), f32),
        skip_in=((16, 128), f32),
        gcoef=((2, 16, 512), f32),
        gcoef_in=((16, 512), f32),
        gv_out=((8, 16, 1024), bf16),
        g_val=((128, 1024), bf16),
        gvp_t=((1024, 128), bf16),
        br_in=((2, 256, 1024), bf16),
        br_xin=((256, 1024), bf16),
        gn_in=((2, 256, 1024), bf16),
        gn_xin=((256, 1024), bf16),
        ng=((4, 8, 128), f32),
        ng_in=((7, 8, 128), f32),
        ng_f=((8, 128), f32),
        ng_fin=((3, 8, 128), f32),
    )
    names = list(ins) + list(outs) + list(scratch) + ["ssem", "rsem"]
    vmem = pl.BlockSpec(memory_space=pltpu.VMEM)
    got = pl.pallas_call(
        functools.partial(layer_kernel, names),
        out_shape=[jax.ShapeDtypeStruct(s, t) for s, t in outs.values()],
        in_specs=[vmem] * len(ins),
        out_specs=[vmem] * len(outs),
        scratch_shapes=[pltpu.VMEM(s, t) for s, t in scratch.values()]
        + [pltpu.SemaphoreType.DMA((N_SEMS,)), pltpu.SemaphoreType.DMA((N_SEMS,))],
        compiler_params=pltpu.CompilerParams(
            collective_id=0, has_side_effects=True, vmem_limit_bytes=64 << 20
        ),
    )(*ins.values())
    o = types.SimpleNamespace(**dict(zip(outs, got)))
    return (
        o.result,
        o.g_tokens,
        o.o_norm[0, :32],
        o.o_norm[2, :32],
        o.o_up,
        o.o_value,
        o.o_back,
        o.o_down,
        o.o_coef,
        o.o_skip[:, 127],
    )


def run(tokens, *rest):
    sizes = (lax.axis_size("item"), lax.axis_size("tok"), tokens.shape)
    if sizes == (2, 16, (2, 128, 1024)):
        return fast_body(tokens, *rest)
    return body(tokens, *rest)


def solution(mesh):
    in_specs = (
        P("item", "tok", None),
        P(("item", "tok")),
        P(("item", "tok")),
        P(("item", "tok"), None),
        P(("item", "tok"), None),
        P(("item", "tok"), None),
        P(("item", "tok"), None),
        P("tok", "item"),
        P("tok"),
        P("item", "tok", None),
    )
    out_specs = (
        P("item", "tok", None),
        P("item", "tok", None),
        P(("item", "tok")),
        P(("item", "tok")),
        P(("item", "tok"), None),
        P(("item", "tok"), None),
        P(("item", "tok"), None),
        P(("item", "tok"), None),
        P("tok", "item"),
        P("tok"),
    )
    return jax.shard_map(run, mesh=mesh, in_specs=in_specs, out_specs=out_specs, check_vma=False)
```

```python
import functools
import math
import types

import jax
import jax.numpy as jnp
import ml_dtypes
import numpy as np
from jax import lax
from jax.experimental import pallas as pl
from jax.experimental.pallas import tpu as pltpu
from jax.sharding import PartitionSpec as P

highest = lax.Precision.HIGHEST


def basis_block(start_index, block_width, length, states):
    places = start_index + jnp.arange(block_width, dtype=jnp.int32)
    mode_ids = jnp.arange(states, dtype=jnp.int32)
    fraction = (mode_ids * 41 % states).astype(jnp.float32) / states
    mode_rates = jnp.exp(jnp.log(1.0 / 32.0) + fraction * jnp.log(32.0 / (4.0 * length)))
    decays = jnp.exp(-mode_rates[:, None] * places[None, :].astype(jnp.float32))
    phase_turns = (mode_ids[:, None] * places[None, :] % (2 * states)).astype(jnp.float32) * (
        jnp.pi / states
    )
    return jnp.concatenate([decays * jnp.cos(phase_turns), decays * jnp.sin(phase_turns)], axis=0)


def make_kernel(coef_full, length):
    states = coef_full.shape[1] // 2
    block_width = math.gcd(length, 2048)
    block_count = length // block_width

    def one_block(block_index):
        table = basis_block(block_index * block_width, block_width, length, states)
        return jnp.dot(coef_full, table, precision=highest)

    pieces = lax.map(one_block, jnp.arange(block_count, dtype=jnp.int32))
    return jnp.transpose(pieces, (1, 0, 2)).reshape(coef_full.shape[0], length)


def coef_gradient(grad_kernel, states):
    channels, length = grad_kernel.shape
    block_width = math.gcd(length, 2048)
    block_count = length // block_width
    slabs = grad_kernel.reshape(channels, block_count, block_width)

    def add_block(running, block_index):
        slab_part = lax.dynamic_index_in_dim(slabs, block_index, 1, keepdims=False)
        table = basis_block(block_index * block_width, block_width, length, states)
        return (running + jnp.dot(slab_part, table.T, precision=highest), None)

    start_total = jnp.zeros((channels, 2 * states), jnp.float32)
    summed, unused = lax.scan(add_block, start_total, jnp.arange(block_count, dtype=jnp.int32))
    return summed


def unit_tables(row_count, column_count, period):
    row_ids = jnp.arange(row_count, dtype=jnp.int32)[:, None]
    column_ids = jnp.arange(column_count, dtype=jnp.int32)[None, :]
    phase_turns = (row_ids * column_ids % period).astype(jnp.float32) * (2.0 * jnp.pi / period)
    return (jnp.cos(phase_turns), jnp.sin(phase_turns))


def right_product(left_part, table):
    return jnp.einsum("...kq,qm->...km", left_part, table, precision=highest)


def spectrum(signal):
    length = signal.shape[-1]
    padded_size = 2 * length
    outer_size = padded_size // 128
    half_size = outer_size // 2
    folded = signal.reshape(signal.shape[:-1] + (half_size, 128))
    cos_outer, sin_outer = unit_tables(outer_size, half_size, outer_size)
    section_real = jnp.einsum("kp,...pq->...kq", cos_outer, folded, precision=highest)
    section_imag = -jnp.einsum("kp,...pq->...kq", sin_outer, folded, precision=highest)
    twist_cos, twist_sin = unit_tables(outer_size, 128, padded_size)
    turned_real = section_real * twist_cos + section_imag * twist_sin
    turned_imag = section_imag * twist_cos - section_real * twist_sin
    cos_inner, sin_inner = unit_tables(128, 128, 128)
    out_real = right_product(turned_real, cos_inner) + right_product(turned_imag, sin_inner)
    out_imag = right_product(turned_imag, cos_inner) - right_product(turned_real, sin_inner)
    return (out_real, out_imag)


def inverse(spec_real, spec_imag):
    outer_size = spec_real.shape[-2]
    padded_size = outer_size * 128
    half_size = outer_size // 2
    cos_inner, sin_inner = unit_tables(128, 128, 128)
    back_real = right_product(spec_real, cos_inner) - right_product(spec_imag, sin_inner)
    back_imag = right_product(spec_real, sin_inner) + right_product(spec_imag, cos_inner)
    twist_cos, twist_sin = unit_tables(outer_size, 128, padded_size)
    turned_real = back_real * twist_cos - back_imag * twist_sin
    turned_imag = back_real * twist_sin + back_imag * twist_cos
    cos_outer, sin_outer = unit_tables(half_size, outer_size, outer_size)
    signal = jnp.einsum("pk,...kq->...pq", cos_outer, turned_real, precision=highest)
    signal = signal - jnp.einsum("pk,...kq->...pq", sin_outer, turned_imag, precision=highest)
    return signal.reshape(signal.shape[:-2] + (half_size * 128,)) / padded_size


def layer_norm(token_rows, gain_row, shift_row):
    row_mean = jnp.mean(token_rows, axis=-1, keepdims=True)
    centered = token_rows - row_mean
    variance = jnp.mean(centered * centered, axis=-1, keepdims=True)
    return centered * lax.rsqrt(variance + 1e-05) * gain_row + shift_row


def body(
    tokens, norm_gain, norm_shift, w_up, w_value, w_back, w_down, mode_coef, skip_gain, cotangent
):
    gain_full, shift_full, up_full, value_full = (
        lax.all_gather(norm_gain, ("item", "tok"), axis=0, tiled=True),
        lax.all_gather(norm_shift, ("item", "tok"), axis=0, tiled=True),
        lax.all_gather(w_up, ("item", "tok"), axis=0, tiled=True),
        lax.all_gather(w_value, ("item", "tok"), axis=0, tiled=True),
    )
    back_full, down_full = (
        lax.all_gather(w_back, ("item", "tok"), axis=0, tiled=True),
        lax.all_gather(w_down, ("item", "tok"), axis=0, tiled=True),
    )
    coef_full = lax.all_gather(mode_coef, "item", axis=1, tiled=True)
    token_rows = tokens.astype(jnp.float32)
    gain_float = gain_full.astype(jnp.float32)
    shift_float = shift_full.astype(jnp.float32)
    normed = layer_norm(token_rows, gain_float, shift_float).astype(jnp.bfloat16)
    up_pre = jnp.einsum("std,df->stf", normed, up_full, preferred_element_type=jnp.float32)
    value_pre = jnp.einsum("std,dh->sht", normed, value_full, preferred_element_type=jnp.float32)
    value = jax.nn.gelu(value_pre).astype(jnp.bfloat16)
    channel_values = lax.all_to_all(value, "tok", split_axis=1, concat_axis=2, tiled=True)
    length = channel_values.shape[-1]
    kernel = make_kernel(coef_full.astype(jnp.float32), length)
    signal = channel_values.astype(jnp.float32)
    skip_column = skip_gain.astype(jnp.float32)[:, None]
    value_real, value_imag = spectrum(signal)
    kernel_real, kernel_imag = spectrum(kernel)
    conv_out = inverse(
        value_real * kernel_real - value_imag * kernel_imag,
        value_real * kernel_imag + value_imag * kernel_real,
    )
    mixed_channels = (conv_out + skip_column * signal).astype(jnp.bfloat16)
    mixed = lax.all_to_all(mixed_channels, "tok", split_axis=2, concat_axis=1, tiled=True)
    gate = jnp.einsum("sht,hf->stf", mixed, back_full, preferred_element_type=jnp.float32)
    up_act = jax.nn.gelu(up_pre)
    hidden = (up_act * gate).astype(jnp.bfloat16)
    branch = jnp.einsum("stf,fd->std", hidden, down_full, preferred_element_type=jnp.float32)
    result = (token_rows + branch).astype(jnp.bfloat16)
    grad_w_down = jnp.einsum("stf,std->fd", hidden, cotangent, preferred_element_type=jnp.float32)
    grad_hidden = jnp.einsum(
        "std,fd->stf", cotangent, down_full, preferred_element_type=jnp.float32
    )
    grad_gate = (grad_hidden * up_act).astype(jnp.bfloat16)
    grad_up_act = grad_hidden * gate
    grad_w_back = jnp.einsum("sht,stf->hf", mixed, grad_gate, preferred_element_type=jnp.float32)
    grad_mixed = jnp.einsum(
        "stf,hf->sht", grad_gate, back_full, preferred_element_type=jnp.float32
    ).astype(jnp.bfloat16)
    grad_channels = lax.all_to_all(grad_mixed, "tok", split_axis=1, concat_axis=2, tiled=True)
    grad_signal = grad_channels.astype(jnp.float32)
    grad_real, grad_imag = spectrum(grad_signal)
    grad_value_channels = inverse(
        kernel_real * grad_real + kernel_imag * grad_imag,
        kernel_real * grad_imag - kernel_imag * grad_real,
    )
    grad_value_channels = (grad_value_channels + skip_column * grad_signal).astype(jnp.bfloat16)
    grad_kernel = inverse(
        jnp.sum(grad_real * value_real + grad_imag * value_imag, axis=0),
        jnp.sum(grad_imag * value_real - grad_real * value_imag, axis=0),
    )
    grad_skip_part = jnp.sum(grad_signal * signal, axis=(0, 2))
    grad_coef_part = coef_gradient(grad_kernel, coef_full.shape[1] // 2)
    grad_mode_coef = lax.psum_scatter(grad_coef_part, "item", scatter_dimension=1, tiled=True)
    grad_skip_gain = lax.psum(grad_skip_part, "item")
    grad_value = lax.all_to_all(grad_value_channels, "tok", split_axis=2, concat_axis=1, tiled=True)
    gelu_value_back = jax.vjp(jax.nn.gelu, value_pre)[1]
    grad_value_pre = gelu_value_back(grad_value.astype(jnp.float32))[0].astype(jnp.bfloat16)
    gelu_up_back = jax.vjp(jax.nn.gelu, up_pre)[1]
    grad_up_pre = gelu_up_back(grad_up_act)[0].astype(jnp.bfloat16)
    grad_w_up = jnp.einsum("std,stf->df", normed, grad_up_pre, preferred_element_type=jnp.float32)
    grad_w_value = jnp.einsum(
        "std,sht->dh", normed, grad_value_pre, preferred_element_type=jnp.float32
    )
    grad_normed = jnp.einsum(
        "stf,df->std", grad_up_pre, up_full, preferred_element_type=jnp.float32
    )
    grad_normed = grad_normed + jnp.einsum(
        "sht,dh->std", grad_value_pre, value_full, preferred_element_type=jnp.float32
    )
    norm_back = jax.vjp(layer_norm, token_rows, gain_float, shift_float)[1]
    grad_rows, grad_gain_part, grad_shift_part = norm_back(grad_normed)
    grad_tokens = cotangent.astype(jnp.float32) + grad_rows
    owners = lax.axis_size("item") * lax.axis_size("tok")
    norm_flat = jnp.concatenate(
        [grad_gain_part.reshape(owners, -1), grad_shift_part.reshape(owners, -1)], axis=1
    )
    up_flat = grad_w_up.reshape(owners, -1)
    value_flat = grad_w_value.reshape(owners, -1)
    back_flat = grad_w_back.reshape(owners, -1)
    down_flat = grad_w_down.reshape(owners, -1)
    summed = (
        lax.psum_scatter(norm_flat, ("item", "tok"), scatter_dimension=0, tiled=True),
        lax.psum_scatter(up_flat, ("item", "tok"), scatter_dimension=0, tiled=True),
        lax.psum_scatter(value_flat, ("item", "tok"), scatter_dimension=0, tiled=True),
        lax.psum_scatter(back_flat, ("item", "tok"), scatter_dimension=0, tiled=True),
        lax.psum_scatter(down_flat, ("item", "tok"), scatter_dimension=0, tiled=True),
    )
    gain_count = norm_gain.shape[0]
    norm_row = summed[0].reshape(-1)
    grad_norm_gain = norm_row[:gain_count]
    grad_norm_shift = norm_row[gain_count:]
    grad_up_out = summed[1].reshape(w_up.shape)
    grad_value_out = summed[2].reshape(w_value.shape)
    grad_back_out = summed[3].reshape(w_back.shape)
    grad_down_out = summed[4].reshape(w_down.shape)
    return (
        result,
        grad_tokens,
        grad_norm_gain,
        grad_norm_shift,
        grad_up_out,
        grad_value_out,
        grad_back_out,
        grad_down_out,
        grad_mode_coef,
        grad_skip_gain,
    )


MESH_ID = pl.DeviceIdType.MESH
bf16, f32 = jnp.bfloat16, jnp.float32
NT = (((1,), (1,)), ((), ()))
GC = math.sqrt(2.0 / math.pi)


def dot(a, b):
    return jnp.dot(a, b, preferred_element_type=f32)


def dot_nt(a, b):
    return lax.dot_general(a, b, NT, preferred_element_type=f32)


def gelu_parts(v):
    t = jnp.tanh(GC * (v + 0.044715 * v * v * v))
    half = 0.5 * (1.0 + t)
    slope = half + 0.5 * v * (1.0 - t * t) * (GC * (1.0 + 3 * 0.044715 * v * v))
    return v * half, slope


def split(v):
    high = v.astype(bf16)
    return high, (v - high.astype(f32)).astype(bf16)


def mode_tables(states, length):
    n = np.arange(states)
    rates = np.exp(np.log(1.0 / 32.0) + (n * 41 % states) / states * np.log(32.0 / (4.0 * length)))

    def table(places):
        decay = np.exp(-rates[:, None] * places[None, :])
        turn = (n[:, None] * places[None, :] % (2 * states)) * (np.pi / states)
        return decay * np.cos(turn), decay * np.sin(turn)

    far_re, far_im = table(np.arange(0, length, 128))
    near = np.concatenate(table(np.arange(128)), axis=0).astype(np.float32)
    high = near.astype(ml_dtypes.bfloat16)
    low = (near - high.astype(np.float32)).astype(ml_dtypes.bfloat16)
    return (
        far_re.T.astype(np.float32).copy(),
        far_im.T.astype(np.float32).copy(),
        high,
        low,
        high.T[::-1].copy(),
        low.T[::-1].copy(),
    )


class Links:
    def __init__(self, send_sems, recv_sems, place):
        self.send_sems, self.recv_sems, self.place = send_sems, recv_sems, place
        self.count = 0
        self.pending = []

    def take(self, n=1):
        first = self.count
        self.count += n
        return first

    def make(self, src, dst, ssem, rsem, to):
        return pltpu.make_async_remote_copy(
            src_ref=src,
            dst_ref=dst,
            send_sem=self.send_sems.at[ssem],
            recv_sem=self.recv_sems.at[rsem],
            device_id=to,
            device_id_type=MESH_ID,
        )

    def put(self, src, dst, to):
        slot = self.take()
        copy = self.make(src, dst, slot, slot, to)
        copy.start()
        self.pending.append((copy, None))
        return slot

    def got(self, slot, region):
        self.make(region, region, slot, slot, self.place).wait_recv()

    def put_or_keep(self, src, dst, ssem, rsem, to, here):
        remote = self.make(src, dst, ssem, rsem, to)
        local = pltpu.make_async_copy(src, dst, self.recv_sems.at[rsem])
        away = jnp.logical_not(here)
        pl.when(here)(local.start)
        pl.when(away)(remote.start)
        self.pending.append((remote, away))

    def finish(self):
        for copy, away in self.pending:
            if away is None:
                copy.wait_send()
            else:
                pl.when(away)(copy.wait_send)


N_SEMS = 200


def layer_kernel(names, *refs):
    r_ = dict(zip(names, refs))
    g = types.SimpleNamespace(**r_)
    x = lax.axis_index("item")
    tok = lax.axis_index("tok")
    z, y, c = tok // 4, (tok // 2) % 2, tok % 2
    n = tok // 2
    r = 2 * x + c

    def dev(x_, z_, y_, c_):
        return (x_, z_ * 4 + y_ * 2 + c_)

    def zo(k):
        return lax.rem(z + k, 4)

    def zb(k):
        return lax.rem(z + 4 - k, 4)

    def node(z_, y_):
        return 2 * z_ + y_

    sib, xn, diag = dev(x, z, y, 1 - c), dev(1 - x, z, y, c), dev(1 - x, z, y, 1 - c)
    r_sib, r_xn, r_diag = 2 * x + 1 - c, 2 * (1 - x) + c, 2 * (1 - x) + 1 - c
    members = ((sib, x, 1 - c, r_sib), (xn, 1 - x, c, r_xn), (diag, 1 - x, 1 - c, r_diag))
    ynb = dev(x, z, 1 - y, c)
    lk = Links(g.ssem, g.rsem, ynb)
    aligned = pl.multiple_of

    barrier = pltpu.get_barrier_semaphore()
    partners = [m[0] for m in members]
    for k in range(1, 4):
        partners += [dev(x, zo(k), y, c), dev(x, zo(k), 1 - y, c), dev(x, zo(k), y, 1 - c)]
    partners.append(ynb)
    for p in partners:
        pl.semaphore_signal(barrier, inc=1, device_id=p, device_id_type=MESH_ID)

    eye = lax.broadcasted_iota(jnp.int32, (32, 128), 0) == lax.broadcasted_iota(
        jnp.int32, (32, 128), 1
    )
    eye = eye.astype(bf16)
    ch_i = lax.broadcasted_iota(jnp.int32, (512, 128), 0)
    p_i = lax.broadcasted_iota(jnp.int32, (512, 128), 1)
    row16 = lax.broadcasted_iota(jnp.int32, (16, 128), 0)
    gain_row = dot(g.norm_gain[...], eye)
    shift_row = dot(g.norm_shift[...], eye)
    norm_pack = jnp.where(
        row16 == 0,
        jnp.broadcast_to(gain_row, (16, 128)),
        jnp.where(row16 == 1, jnp.broadcast_to(shift_row, (16, 128)), 0.0),
    ).astype(bf16)
    for rr in range(4):
        pick = ch_i == 64 * (p_i // 16) + 32 * (rr % 2) + 16 * (rr // 2) + p_i % 16
        pick = pick.astype(bf16)
        g.perm[:, 128 * rr : 128 * rr + 128] = pick
        g.pk_send[rr, 0:32, :] = dot(g.w_value[...], pick).astype(bf16)
        g.pk_send[rr, 32:48, :] = norm_pack
    pl.semaphore_wait(barrier, len(partners))

    pk_s, up_s, back_s = [], [], []
    for to, xm, cm, rm in members:
        pk_s.append(lk.put(g.pk_send.at[rm], g.pk.at[x, n, c], to))
    coef_s = lk.put(g.mode_coef.at[pl.ds(aligned(16 * (1 - x), 16), 16), :], g.coef.at[x], xn)
    tok_x = lk.put(g.tokens, g.tok_all.at[r], xn)
    my_back = g.w_back_all.at[c, y, x, z]

    def cols(rm):
        return pl.ds(aligned(768 * rm, 128), 768)

    for to, xm, cm, rm in members:
        up_s.append(lk.put(g.w_up.at[:, cols(rm)], g.w_up_all.at[x, n, c], to))
    for to, xm, cm, rm in members:
        back_s.append(lk.put(g.w_back.at[:, cols(rm)], my_back, to))
    tok_sib = lk.put(g.tokens, g.tok_all.at[r], sib)
    cot_x = lk.put(g.cot, g.cot_all.at[r], xn)
    cot_sib = lk.put(g.cot, g.cot_all.at[r], sib)
    g.pk[x, n, c] = g.pk_send[r]
    g.w_up_all[x, n, c] = g.w_up[:, cols(r)]
    g.w_back_all[c, y, x, z] = g.w_back[:, cols(r)]
    g.cot_all[r] = g.cot[...]
    g.coef[x] = g.mode_coef[pl.ds(aligned(16 * x, 16), 16), :]

    def gather_start(region):
        slots = {}
        for k in (1, 2, 3):
            slots[k] = lk.put(region(z, y), region(z, y), dev(x, zo(k), y, c))
        slots[4] = lk.put(region(z, y), region(z, y), ynb)
        return slots

    def gather_pass(slots, region, k):
        lk.got(slots[k], region(zb(k), y))
        slots[4 + k] = lk.put(region(zb(k), y), region(zb(k), y), ynb)

    def gather_end(slots, region):
        for k in range(4):
            lk.got(slots[4 + k], region(zb(k), 1 - y))

    def pk_region(z_, y_):
        return g.pk.at[:, node(z_, y_)]

    def up_region(z_, y_):
        return g.w_up_all.at[:, node(z_, y_)]

    def back_region(z_, y_):
        return g.w_back_all.at[:, y_, :, z_]

    for i, (to, xm, cm, rm) in enumerate(members):
        lk.got(pk_s[i], g.pk.at[xm, n, cm])
    pk_g = gather_start(pk_region)

    def line(region, has):
        right, left, across = lk.take(3), lk.take(3), lk.take(4)
        passes = lk.take(3)

        def send(zs, ssem, rsem, to, when):
            copy = lk.make(region(zs, y), region(zs, y), ssem, rsem, to)
            pl.when(when)(copy.start)
            lk.pending.append((copy, when))

        def also(when, zs):
            return when if has is None else jnp.logical_and(when, has(zs))

        def step(k):
            for way, base in ((-1, right), (1, left)):
                if k == 0 and way == 1:
                    continue
                zs = z + way * k
                there = also(z >= k if way == -1 else z + k <= 3, zs)
                if k:
                    slot = base + k - 1
                    block = region(lax.rem(zs + 4, 4), y)
                    wait = lk.make(block, block, slot, slot, ynb)
                    pl.when(there)(wait.wait_recv)
                zs = lax.rem(zs + 4, 4)
                if k < 3 and (way == -1 or k == 0):
                    on = jnp.logical_and(there, z < 3)
                    send(zs, right + k, right + k, dev(x, zo(1), y, c), on)
                if k < 3 and (way == 1 or k == 0):
                    on = jnp.logical_and(there, z > 0)
                    send(zs, left + k, left + k, dev(x, zb(1), y, c), on)
                ssem = across + k if way == -1 else passes + k - 1
                send(zs, ssem, across + zs, ynb, there)

        def end():
            for zs in range(4):
                block = region(zs, 1 - y)
                wait = lk.make(block, block, across + zs, across + zs, ynb)
                if has is None:
                    wait.wait_recv()
                else:
                    pl.when(has(zs))(wait.wait_recv)

        return step, end

    def down_region(z_, y_):
        return g.w_down_all.at[lax.rem(z_, 2), y_]

    def down_has(z_):
        return (z_ + 4) // 2 == c + 2

    owner = z // 2
    dn_own = lk.take()
    dst = g.w_down_all.at[lax.rem(z, 2), y, c]
    dn_copy = lk.make(g.w_down, dst, dn_own, dn_own, sib)
    pl.when(owner != c)(dn_copy.start)
    lk.pending.append((dn_copy, owner != c))

    @pl.when(owner == c)
    def _():
        g.w_down_all[lax.rem(z, 2), y, c] = g.w_down[...]
        block = g.w_down_all.at[lax.rem(z, 2), y, 1 - c]
        lk.make(block, block, dn_own, dn_own, sib).wait_recv()

    down_step, down_end = line(down_region, down_has)
    up_step, up_end = line(up_region, None)
    back_step, back_end = line(back_region, None)
    down_step(0)

    lk.got(coef_s, g.coef.at[1 - x])
    cc = g.coef[0].astype(f32)
    sc = g.coef[1].astype(f32)

    def far(p, _):
        hr = g.far_re[pl.ds(p, 1), :]
        hi = g.far_im[pl.ds(p, 1), :]
        rows = pl.ds(aligned(16 * p, 16), 16)
        g.state[rows, 0:512] = cc * hr + sc * hi
        g.state[rows, 512:1024] = sc * hr - cc * hi
        return 0

    lax.fori_loop(0, 16, far, 0)
    for half in range(2):
        rows = slice(128 * half, 128 * half + 128)
        hi_, lo_ = split(g.state[rows, :])
        g.kern[rows, :] = (
            dot(hi_, g.near_hi[...]) + dot(lo_, g.near_hi[...]) + dot(hi_, g.near_lo[...])
        )
    for k in (1, 2, 3):
        gather_pass(pk_g, pk_region, k)
    down_step(1)
    ii = lax.broadcasted_iota(jnp.int32, (128, 128), 0)
    jj = lax.broadcasted_iota(jnp.int32, (128, 128), 1)
    flip = (ii + jj == 127).astype(bf16)

    def toeplitz(h, _):
        prev = jnp.zeros((128, 128), f32)
        for k in range(16):
            row = jnp.broadcast_to(g.kern[pl.ds(16 * k + h, 1), :], (128, 128))
            turned = pltpu.roll(row, 0, 1, stride=1, stride_axis=0)
            g.toep[h, k] = jnp.where(jj >= ii, turned, prev).astype(bf16)
            prev = turned
        return 0

    lax.fori_loop(0, 16, toeplitz, 0, unroll=2)

    gather_end(pk_g, pk_region)
    e_i = lax.broadcasted_iota(jnp.int32, (128, 1024), 0)
    e_j = lax.broadcasted_iota(jnp.int32, (128, 1024), 1)
    spread = jnp.logical_and(e_i < 32, lax.rem(e_j, 32) == e_i).astype(bf16)
    blk = lax.broadcasted_iota(jnp.int32, (16, 1024), 1) // 32
    acc = jnp.zeros((16, 1024), f32)
    for xm in range(2):
        for nm in range(8):
            for cm in range(2):
                rows = g.pk[xm, nm, cm, 32:48, :]
                acc = acc + jnp.where(
                    blk == 16 * xm + 2 * nm + cm, dot(rows, spread), 0.0
                )
    gain = acc[0:1, :]
    shift = acc[1:2, :]
    g.norm_rows[0:1, :] = gain
    g.norm_rows[1:2, :] = shift
    wv = g.pk[:, :, :, 0:32, :].reshape(1024, 128)
    g.w_val[...] = wv
    wvt = wv.T
    for t in range(8):
        at = 256 * (t % 4) + 128 * (t // 4)
        g.w_val_t[:, at : at + 128] = wvt[:, 128 * t : 128 * t + 128]

    def norm_block(read, q):
        def part(s_, _):
            rows = read(s_).astype(f32)
            mean = jnp.mean(rows, axis=-1, keepdims=True)
            cen = rows - mean
            var = jnp.mean(cen * cen, axis=-1, keepdims=True)
            out = (cen * lax.rsqrt(var + 1e-5) * g.norm_rows[0:1, :] + g.norm_rows[1:2, :]).astype(
                bf16
            )
            at = aligned(256 * q + 128 * s_, 128)
            g.normed[pl.ds(at, 128), :] = out
            for t in range(8):
                low = 256 * (t % 4) + 128 * (t // 4)
                g.normed_t[low : low + 128, pl.ds(at, 128)] = out[:, 128 * t : 128 * t + 128].T
            return 0

        lax.fori_loop(0, 2, part, 0)
        at = pl.ds(aligned(256 * q, 128), 256)
        pre = dot(g.w_val_t[...], g.normed_t[:, at])
        act, slope = gelu_parts(pre)
        g.val_slope[:, at] = slope
        g.val[:, at] = act.astype(bf16)

    norm_block(lambda s_: g.tokens[s_], r)
    lk.got(tok_sib, g.tok_all.at[r_sib])
    norm_block(lambda s_: g.tok_all[r_sib, s_], r_sib)
    down_step(2)
    lk.got(tok_x, g.tok_all.at[r_xn])
    tok_f = lk.put(g.tok_all.at[r_xn], g.tok_all.at[r_xn], sib)
    norm_block(lambda s_: g.tok_all[r_xn, s_], r_xn)
    lk.got(tok_f, g.tok_all.at[r_diag])
    norm_block(lambda s_: g.tok_all[r_diag, s_], r_diag)

    def channel_send(src, landing):
        slots = []
        for k in range(1, 8):
            to = lax.rem(n + k, 8)
            slots.append(
                lk.put(
                    src.at[pl.ds(aligned(16 * to, 16), 16), :],
                    landing.at[n],
                    (x, 2 * to + c),
                )
            )
        return slots

    def channel_got(slots, landing):
        for k in range(1, 8):
            lk.got(slots[k - 1], landing.at[lax.rem(n + 8 - k, 8)])

    def unpack(landing, put):
        def one(nm, _):
            for tb in range(8):
                s_, cm = 2 * (tb // 4) + tb % 2, (tb // 2) % 2
                put(s_, 2 * nm + cm, landing[nm, :, 128 * tb : 128 * tb + 128].astype(f32))
            return 0

        lax.fori_loop(0, 8, one, 0)

    def put_val(s_, i, tile):
        g.v32[pl.ds(32 * s_ + 16 + i, 16, stride=128), :] = tile
        g.vr32[pl.ds(16 * s_ + 15 - i, 16, stride=64), :] = tile

    def put_grad(s_, i, tile):
        g.v32[pl.ds(32 * s_ + 31 - i, 16, stride=128), :] = tile

    val_s = channel_send(g.val, g.val_in)
    g.val_in[n] = g.val[pl.ds(aligned(16 * n, 16), 16), :]
    for i, (to, xm, cm, rm) in enumerate(members):
        lk.got(up_s[i], g.w_up_all.at[xm, n, cm])
    up_step(0)
    down_step(3)

    zero = jnp.zeros((16, 128), f32)
    for i in range(64):
        g.v32[32 * i : 32 * i + 16, :] = zero
    diag_i = lax.broadcasted_iota(jnp.int32, (32, 32), 0) == lax.broadcasted_iota(
        jnp.int32, (32, 32), 1
    )
    skip_row = jnp.broadcast_to(g.skip[...].astype(f32), (32, 32))
    g.skip_b[...] = dot(jnp.where(diag_i, skip_row, 0.0).astype(bf16), jnp.ones((32, 128), bf16))

    channel_got(val_s, g.val_in)
    unpack(g.val_in, put_val)
    up_step(1)

    def conv_rows(h, k):
        rows = [g.v32[pl.ds(128 * h + 32 * s_ + 16 - k, 16), :] for s_ in range(4)]
        return jnp.concatenate(rows, axis=0)

    def conv(h, _):
        parts = [conv_rows(h, k) for k in range(16)]
        out = g.skip_b[pl.ds(16 * x + h, 1), :] * parts[0]
        for kk in range(8):
            lhs = jnp.concatenate([parts[2 * kk], parts[2 * kk + 1]], axis=1).astype(bf16)
            out = out + dot(lhs, g.toep[h, 2 * kk : 2 * kk + 2].reshape(256, 128))
        g.o32[pl.ds(aligned(64 * h, 64), 64), :] = out
        return 0

    def pack(out, back):
        def one(nm, _):
            for tb in range(8):
                s_, cm = 2 * (tb // 4) + tb % 2, (tb // 2) % 2
                i = 2 * nm + cm
                at = pl.ds(16 * s_ + (15 - i if back else i), 16, stride=64)
                out[nm, :, 128 * tb : 128 * tb + 128] = g.o32[at, :].astype(bf16)
            return 0

        lax.fori_loop(0, 8, one, 0)

    def channel_back(src, landing):
        slots = []
        for k in range(1, 8):
            to = lax.rem(n + k, 8)
            slots.append(
                lk.put(src.at[to], landing.at[pl.ds(aligned(16 * n, 16), 16), :], (x, 2 * to + c))
            )
        return slots

    def channel_back_got(slots, landing):
        for k in range(1, 8):
            at = aligned(16 * lax.rem(n + 8 - k, 8), 16)
            lk.got(slots[k - 1], landing.at[pl.ds(at, 16), :])

    lax.fori_loop(0, 16, conv, 0, unroll=2)
    pack(g.mix_out, False)
    mix_s = channel_back(g.mix_out, g.mix.at[r])
    g.mix[r, pl.ds(aligned(16 * n, 16), 16), :] = g.mix_out[n]

    up_step(2)
    for i, (to, xm, cm, rm) in enumerate(members):
        lk.got(back_s[i], g.w_back_all.at[cm, y, xm, z])
    back_step(0)
    lk.got(cot_x, g.cot_all.at[r_xn])
    cot_f = lk.put(g.cot_all.at[r_xn], g.cot_all.at[r_xn], sib)
    down_end()
    lk.got(cot_sib, g.cot_all.at[r_sib])
    lk.got(cot_f, g.cot_all.at[r_diag])
    down2d = g.w_down_all.reshape(768, 1024)
    cot2d = g.cot_all.reshape(1024, 1024)

    def hidden_tile(q, _):
        rows = pl.ds(aligned(256 * q, 256), 256)
        g.slope[rows, :] = dot_nt(cot2d[rows, :], down2d[...])
        return 0

    lax.fori_loop(0, 4, hidden_tile, 0)
    up_step(3)
    back_step(1)
    channel_back_got(mix_s, g.mix.at[r])
    mix_x = lk.put(g.mix.at[r], g.mix.at[r], xn)
    mix_sib = lk.put(g.mix.at[r], g.mix.at[r], sib)
    back_step(2)

    up_end()
    up2d = g.w_up_all.reshape(1024, 768)

    def up_tile(q, _):
        rows = pl.ds(aligned(256 * q, 256), 256)
        act, slope = gelu_parts(dot(g.normed[rows, :], up2d[...]))
        gh = g.slope[rows, :]
        g.act[rows, :] = act
        g.g_gate[rows, :] = (gh * act).astype(bf16)
        g.slope[rows, :] = gh * slope
        return 0

    back_step(3)
    lax.fori_loop(0, 4, up_tile, 0)
    lk.got(mix_x, g.mix.at[r_xn])
    mix_f = lk.put(g.mix.at[r_xn], g.mix.at[r_xn], sib)
    back_end()
    back2d = g.w_back_all.reshape(512, 768)

    def mixed_part(ranks, q):
        w = [back2d[pl.ds(aligned(128 * rr, 128), 128), :] for rr in ranks]
        w = w[0] if len(w) == 1 else jnp.concatenate(w, axis=0)
        return dot_nt(w, g.g_gate[pl.ds(aligned(512 * q, 512), 512), :])

    def gm_sib(q, _):
        at = pl.ds(aligned(512 * q, 128), 512)
        both = mixed_part((1 - c, 2 + 1 - c), q).astype(bf16)
        g.gm_send[:, :, at] = both.reshape(2, 128, 512)
        return 0

    lax.fori_loop(0, 2, gm_sib, 0)
    gm_s = lk.put(g.gm_send, g.gm_in, sib)

    def gm_mine(q, _):
        at = pl.ds(aligned(512 * q, 128), 512)
        both = mixed_part((2 * (1 - x) + c, 2 * x + c), q)
        g.gm_x[:, at] = both[0:128, :].astype(bf16)
        g.gm_own[:, at] = both[128:256, :]
        return 0

    lax.fori_loop(0, 2, gm_mine, 0)
    lk.got(gm_s, g.gm_in)
    g.gm_x[...] = (g.gm_x[...].astype(f32) + g.gm_in[1 - x].astype(f32)).astype(bf16)
    gm_xs = lk.put(g.gm_x, g.gm_xin, xn)

    lk.got(mix_sib, g.mix.at[r_sib])
    lk.got(mix_f, g.mix.at[r_diag])

    def turn(i, _):
        rr, tb = i // 8, lax.rem(i, 8)
        rows = pl.ds(aligned(128 * tb, 128), 128)
        at = pl.ds(aligned(128 * rr, 128), 128)
        g.mix_tok[rows, at] = g.mix[rr, :, rows].T
        return 0

    lax.fori_loop(0, 32, turn, 0, unroll=4)

    def gate_tile(q, _):
        rows = pl.ds(aligned(256 * q, 256), 256)
        gate = dot(g.mix_tok[rows, :], back2d[...])
        hidden = (g.act[rows, :] * gate).astype(bf16)
        g.hidden[rows, :] = hidden
        g.hidden_t[:, rows] = hidden.T
        g.g_up[rows, :] = (g.slope[rows, :] * gate).astype(bf16)
        return 0

    lax.fori_loop(0, 4, gate_tile, 0)

    gd_y = []

    def down_grad(zl):
        def tile(i, _):
            at = pl.ds(aligned(512 * i, 512), 512)
            part = dot(g.hidden_t[384 * zl : 384 * zl + 384, :], cot2d[:, at]).astype(bf16)
            g.gd[zl, :, :, at] = part.reshape(2, 192, 512)
            return 0

        lax.fori_loop(0, 2, tile, 0)
        gd_y.append(lk.put(g.gd.at[zl, 1 - y], g.gd_y.at[zl], ynb))

    down_grad(0)

    lk.got(gm_xs, g.gm_xin)
    for tb in range(8):
        at = slice(128 * tb, 128 * tb + 128)
        total = g.gm_own[:, at] + g.gm_in[x, :, at].astype(f32) + g.gm_xin[:, at].astype(f32)
        g.gm[:, at] = dot(total.astype(bf16), flip).astype(bf16)
    gm_cs = channel_send(g.gm, g.gm_land)
    g.gm_land[n] = g.gm[pl.ds(aligned(16 * n, 16), 16), :]

    down_grad(1)
    gd_r = lk.take(4)

    def down_sum(zl):
        lk.got(gd_y[zl], g.gd_y.at[zl])
        for cm in range(2):
            part = pl.ds(96 * cm, 96)
            total = g.gd[zl, y, part, :].astype(f32) + g.gd_y[zl, part, :].astype(f32)
            g.gd[zl, y, part, :] = total.astype(bf16)
            z_d = 2 * c + zl
            here = jnp.logical_and(z_d == z, c == cm)
            lk.put_or_keep(
                g.gd.at[zl, y, part], g.gd_in.at[z], lk.take(), gd_r + z, dev(x, z_d, y, cm), here
            )

    other = pl.ds(aligned(64 * (1 - y), 64), 64)
    own64 = pl.ds(aligned(64 * y, 64), 64)
    up_y, gu_s = {}, {}

    def up_grad(k):
        z_d = zo(k)
        rows = pl.ds(aligned(256 * z_d, 256), 256)
        part = dot(g.normed_t[rows, :], g.g_up[...]).astype(bf16)
        g.gu[z_d] = part.reshape(2, 128, 768)
        up_y[k] = lk.put(g.gu.at[z_d, :, other], g.gu_y.at[z_d], ynb)

    def up_sum(k):
        z_d = zo(k)
        lk.got(up_y[k], g.gu_y.at[z_d])
        total = g.gu[z_d, :, own64, :].astype(f32) + g.gu_y[z_d].astype(f32)
        g.gu[z_d, :, own64, :] = total.astype(bf16)
        if k:
            gu_s[k] = lk.put(g.gu.at[z_d, :, own64], g.gu_in.at[k - 1], dev(x, z_d, y, c))

    up_grad(2)
    up_grad(1)

    channel_got(gm_cs, g.gm_land)
    unpack(g.gm_land, put_grad)
    down_sum(0)

    def conv_back(h, _):
        parts = [conv_rows(h, k) for k in range(16)]
        own = g.vr32[pl.ds(aligned(64 * h, 64), 64), :].T.astype(bf16)
        out = g.skip_b[pl.ds(16 * x + h, 1), :] * parts[0]
        lhs = []
        for kk in range(8):
            lhs.append(jnp.concatenate([parts[2 * kk], parts[2 * kk + 1]], axis=1).astype(bf16))
            out = out + dot(lhs[kk], g.toep[h, 2 * kk : 2 * kk + 2].reshape(256, 128))
        g.o32[pl.ds(aligned(64 * h, 64), 64), :] = out
        after = jnp.zeros((128, 128), f32)
        for kk in range(7, -1, -1):
            pair = dot(own, lhs[kk])
            for half in (1, 0):
                turned = pltpu.roll(
                    pair[:, 128 * half : 128 * half + 128], 0, 1, stride=1, stride_axis=0
                )
                lag = jnp.where(jj >= ii, turned, after)
                after = turned
                at = pl.ds(aligned((16 * (2 * kk + half) + h) * 8, 8), 8)
                g.gk8[at, :] = jnp.sum(lag.reshape(16, 8, 128), axis=0)
        return 0

    lax.fori_loop(0, 16, conv_back, 0)
    pack(g.gv_out, True)
    gv_s = channel_back(g.gv_out, g.g_val)
    g.g_val[pl.ds(aligned(16 * n, 16), 16), :] = g.gv_out[n]

    down_sum(1)
    up_sum(2)
    up_grad(3)
    up_grad(0)
    up_sum(1)

    mix2d = g.mix.reshape(512, 1024)

    def back_tile(i, _):
        at = pl.ds(aligned(384 * i, 128), 384)
        part = dot(mix2d[...], g.g_gate[:, at]).astype(bf16)
        g.gb[:, :, :, at] = part.reshape(2, 2, 128, 384)
        return 0

    lax.fori_loop(0, 2, back_tile, 0)
    gb_y = lk.put(g.gb.at[:, 1 - y], g.gb_y, ynb)

    tall = g.gk8[pl.ds(0, 256, stride=8), :]
    for s_ in range(1, 8):
        tall = tall + g.gk8[pl.ds(s_, 256, stride=8), :]
    for half in range(2):
        hi_, lo_ = split(tall[128 * half : 128 * half + 128, :])
        g.state[128 * half : 128 * half + 128, :] = (
            dot(hi_, g.near_t_hi[...]) + dot(lo_, g.near_t_hi[...]) + dot(hi_, g.near_t_lo[...])
        )
    g.skip_sum[...] = tall[0:16, :]

    def far_back(p, carry):
        gc, gs = carry
        hr = g.far_re[pl.ds(p, 1), :]
        hi = g.far_im[pl.ds(p, 1), :]
        rows = pl.ds(aligned(16 * p, 16), 16)
        ur = g.state[rows, 0:512]
        ui = g.state[rows, 512:1024]
        return gc + hr * ur - hi * ui, gs + hr * ui + hi * ur

    blank = jnp.zeros((16, 512), f32)
    gc, gs = lax.fori_loop(0, 16, far_back, (blank, blank))
    g.gcoef[0] = gc
    g.gcoef[1] = gs
    gcoef_s = lk.put(g.gcoef.at[1 - x], g.gcoef_in, xn)
    skip_s = lk.put(g.skip_sum, g.skip_in, xn)

    channel_back_got(gv_s, g.g_val)
    for tb in range(8):
        at = slice(128 * tb, 128 * tb + 128)
        back = dot(g.g_val[:, at], flip)
        g.gvp_t[at, :] = (back * g.val_slope[:, at]).astype(bf16).T
    part = dot(g.normed_t[...], g.gvp_t[...]).astype(bf16)
    g.gv[...] = part.reshape(4, 2, 128, 128)
    gv_y = lk.put(g.gv.at[:, :, other], g.gv_y, ynb)

    def group_sum(part, send, land, xsend, xland):
        for xm in range(2):
            send[xm] = part(xm, 1 - c).astype(bf16)
        first = lk.put(send, land, sib)
        mine = part(1 - x, c)
        lk.got(first, land)
        xsend[...] = (mine + land[1 - x].astype(f32)).astype(bf16)
        second = lk.put(xsend, xland, xn)

        def own():
            return part(x, c) + land[x].astype(f32) + xland[...].astype(f32)

        return second, own

    def branch_part(xm, cm):
        rows = pl.ds(aligned(256 * (2 * xm + cm), 256), 256)
        return dot(g.hidden[rows, :], down2d[...])

    def normed_part(xm, cm):
        rows = pl.ds(aligned(256 * (2 * xm + cm), 256), 256)
        return dot_nt(g.g_up[rows, :], up2d[...]) + dot_nt(g.gvp_t[rows, :], g.w_val[...])

    spare = g.normed.reshape(2, 2, 256, 1024)
    gn_s, gn_own = group_sum(
        normed_part, spare.at[1], g.gn_in, g.tok_all.at[r_sib].reshape(256, 1024), g.gn_xin
    )
    br_s, br_own = group_sum(
        branch_part, spare.at[0], g.br_in, g.tok_all.at[r].reshape(256, 1024), g.br_xin
    )
    up_sum(3)
    up_sum(0)

    lk.got(gb_y, g.gb_y)
    total = g.gb[:, y].astype(f32) + g.gb_y[...].astype(f32)
    g.gb_z[...] = total.astype(bf16).reshape(4, 4, 16, 768)
    gb_s = {}
    for k in (2, 1, 3):
        gb_s[k] = lk.put(g.gb_z.at[:, zo(k)], g.gb_in.at[k - 1], dev(x, zo(k), y, c))
    lk.got(gv_y, g.gv_y)
    g.gv_z[...] = (g.gv[:, :, own64, :].astype(f32) + g.gv_y[...].astype(f32)).astype(bf16)
    gv_zs = {}
    for k in (2, 1, 3):
        gv_zs[k] = lk.put(g.gv_z.at[zo(k)], g.gv_in.at[k - 1], dev(x, zo(k), y, c))

    lk.got(gn_s, g.gn_xin)
    g.state[...] = gn_own()

    def norm_back(i, carry):
        dg, ds = carry
        s_, part = i // 2, pl.ds(aligned(64 * lax.rem(i, 2), 64), 64)
        rows = g.tokens[s_, part, :].astype(f32)
        mean = jnp.mean(rows, axis=-1, keepdims=True)
        cen = rows - mean
        var = jnp.mean(cen * cen, axis=-1, keepdims=True)
        inv = lax.rsqrt(var + 1e-5)
        zn = cen * inv
        gn = g.state[pl.ds(aligned(64 * i, 64), 64), :]
        gg = gn * g.norm_rows[0:1, :]
        m1 = jnp.mean(gg, axis=-1, keepdims=True)
        m2 = jnp.mean(gg * zn, axis=-1, keepdims=True)
        g.g_tokens[s_, part, :] = g.cot[s_, part, :].astype(f32) + inv * (gg - m1 - zn * m2)
        dg = dg + jnp.sum(gn * zn, axis=0, keepdims=True)
        ds = ds + jnp.sum(gn, axis=0, keepdims=True)
        return dg, ds

    blank = jnp.zeros((1, 1024), f32)
    dg, ds = lax.fori_loop(0, 4, norm_back, (blank, blank))
    for zd in range(4):
        g.ng[zd, 0:1, :] = dg[:, 128 * zd : 128 * zd + 128]
        g.ng[zd, 1:2, :] = dg[:, 512 + 128 * zd : 640 + 128 * zd]
        g.ng[zd, 2:3, :] = ds[:, 128 * zd : 128 * zd + 128]
        g.ng[zd, 3:4, :] = ds[:, 512 + 128 * zd : 640 + 128 * zd]
        g.ng[zd, 4:8, :] = jnp.zeros((4, 128), f32)
    ng_s = []
    for k in range(1, 8):
        to = lax.rem(n + k, 8)
        ng_s.append(lk.put(g.ng.at[to // 2], g.ng_in.at[k - 1], (x, 2 * to + c)))

    lk.got(br_s, g.br_xin)
    out = br_own().reshape(2, 128, 1024) + g.tokens[...].astype(f32)
    g.result[...] = out.astype(bf16)

    for k in (2, 1, 3):
        lk.got(gu_s[k], g.gu_in.at[k - 1])
    total = g.gu[z, :, own64, :].astype(f32)
    for k in range(3):
        total = total + g.gu_in[k].astype(f32)
    g.gu_f[...] = total.reshape(2, 2, 32, 768).astype(bf16)
    fin_u = [lk.put(g.gu_f.at[xm, cm], g.fu_in.at[r], to) for to, xm, cm, rm in members]
    for k in (2, 1, 3):
        lk.got(gb_s[k], g.gb_in.at[k - 1])
    total = g.gb_z[:, z].astype(f32)
    for k in range(3):
        total = total + g.gb_in[k].astype(f32)
    g.gb_f[...] = total.astype(bf16)
    fin_b = [lk.put(g.gb_f.at[2 * cm + xm], g.fb_in.at[r], to) for to, xm, cm, rm in members]
    for k in (2, 1, 3):
        lk.got(gv_zs[k], g.gv_in.at[k - 1])
    total = g.gv_z[z].astype(f32)
    for k in range(3):
        total = total + g.gv_in[k].astype(f32)
    g.gv_f[...] = total.reshape(2, 2, 32, 128).astype(bf16)
    fin_v = [lk.put(g.gv_f.at[xm, cm], g.fv_in.at[r], to) for to, xm, cm, rm in members]
    g.fu_in[r] = g.gu_f[x, c]
    g.fb_in[r] = g.gb_f[2 * c + x]
    g.fv_in[r] = g.gv_f[x, c]

    for zs in range(4):
        region = g.gd_in.at[zs]
        pltpu.make_async_copy(region, region, lk.recv_sems.at[gd_r + zs]).wait()
    total = g.gd_in[0].astype(f32)
    for zs in range(1, 4):
        total = total + g.gd_in[zs].astype(f32)
    g.o_down[...] = total

    mine = pl.ds(aligned(16 * x, 16), 16)
    theirs = pl.ds(aligned(16 * (1 - x), 16), 16)
    lk.got(gcoef_s, g.gcoef_in)
    g.o_coef[mine, :] = g.gcoef[x]
    g.o_coef[theirs, :] = g.gcoef_in[...]
    lk.got(skip_s, g.skip_in)
    g.o_skip[mine, :] = g.skip_sum[...]
    g.o_skip[theirs, :] = g.skip_in[...]

    total = g.ng[z]
    for k in range(1, 8):
        lk.got(ng_s[k - 1], g.ng_in.at[k - 1])
        total = total + g.ng_in[k - 1]
    g.ng_f[...] = total
    ng_t = [lk.put(g.ng_f, g.ng_fin.at[i], to) for i, (to, xm, cm, rm) in enumerate(members)]

    for i, (to, xm, cm, rm) in enumerate(members):
        lk.got(fin_u[i], g.fu_in.at[rm])
        lk.got(fin_b[i], g.fb_in.at[rm])
        lk.got(fin_v[i], g.fv_in.at[rm])
    wide = jnp.concatenate([g.fv_in[rr] for rr in range(4)], axis=1)
    g.o_value[...] = dot_nt(wide, g.perm[...])
    for i in range(3):
        lk.got(ng_t[i], g.ng_fin.at[i])
        total = total + g.ng_fin[i]
    total = jnp.where(x == 0, total, pltpu.roll(total, 7, 0))
    g.o_norm[...] = pltpu.roll(total, 128 - (64 * y + 32 * c), 1)
    lk.finish()
    assert lk.count <= N_SEMS


def start_of(copy):
    copy.start()
    return copy


def fast_body(
    tokens, norm_gain, norm_shift, w_up, w_value, w_back, w_down, mode_coef, skip_gain, cotangent
):
    states = 512
    length = tokens.shape[1] * lax.axis_size("tok")
    far_re, far_im, near_hi, near_lo, near_t_hi, near_t_lo = mode_tables(states, length)
    ins = dict(
        tokens=tokens,
        norm_gain=norm_gain.reshape(1, -1),
        norm_shift=norm_shift.reshape(1, -1),
        w_up=w_up,
        w_value=w_value,
        w_back=w_back,
        w_down=w_down,
        mode_coef=mode_coef,
        skip=skip_gain.reshape(1, -1),
        cot=cotangent,
        far_re=far_re,
        far_im=far_im,
        near_hi=near_hi,
        near_lo=near_lo,
        near_t_hi=near_t_hi,
        near_t_lo=near_t_lo,
    )
    outs = dict(
        result=((2, 128, 1024), bf16),
        g_tokens=((2, 128, 1024), f32),
        o_norm=((8, 128), f32),
        fu_in=((4, 32, 768), bf16),
        o_value=((32, 512), f32),
        fb_in=((4, 16, 768), bf16),
        o_down=((96, 1024), f32),
        o_coef=((32, 512), f32),
        o_skip=((32, 128), f32),
    )
    scratch = dict(
        perm=((512, 512), bf16),
        pk_send=((4, 48, 128), bf16),
        pk=((2, 8, 2, 48, 128), bf16),
        coef=((2, 16, 512), bf16),
        w_up_all=((2, 8, 2, 32, 768), bf16),
        w_back_all=((2, 2, 2, 4, 16, 768), bf16),
        w_down_all=((2, 2, 2, 96, 1024), bf16),
        tok_all=((4, 2, 128, 1024), bf16),
        cot_all=((4, 2, 128, 1024), bf16),
        state=((256, 1024), f32),
        kern=((256, 128), f32),
        toep=((16, 16, 128, 128), bf16),
        norm_rows=((8, 1024), f32),
        w_val=((1024, 128), bf16),
        w_val_t=((128, 1024), bf16),
        normed=((1024, 1024), bf16),
        normed_t=((1024, 1024), bf16),
        val_slope=((128, 1024), f32),
        val=((128, 1024), bf16),
        val_in=((8, 16, 1024), bf16),
        v32=((2048, 128), f32),
        vr32=((1024, 128), f32),
        o32=((1024, 128), f32),
        skip_b=((32, 128), f32),
        mix_out=((8, 16, 1024), bf16),
        mix=((4, 128, 1024), bf16),
        act=((1024, 768), f32),
        slope=((1024, 768), f32),
        g_gate=((1024, 768), bf16),
        gm_send=((2, 128, 1024), bf16),
        gm_in=((2, 128, 1024), bf16),
        gm_x=((128, 1024), bf16),
        gm_xin=((128, 1024), bf16),
        gm=((128, 1024), bf16),
        gm_land=((8, 16, 1024), bf16),
        mix_tok=((1024, 512), bf16),
        hidden=((1024, 768), bf16),
        hidden_t=((768, 1024), bf16),
        g_up=((1024, 768), bf16),
        gd=((2, 2, 192, 1024), bf16),
        gd_y=((2, 192, 1024), bf16),
        gd_in=((4, 96, 1024), bf16),
        gu=((4, 2, 128, 768), bf16),
        gu_y=((4, 2, 64, 768), bf16),
        gu_in=((3, 2, 64, 768), bf16),
        fv_in=((4, 32, 128), bf16),
        gu_f=((2, 2, 32, 768), bf16),
        gb=((2, 2, 128, 768), bf16),
        gb_y=((2, 128, 768), bf16),
        gb_z=((4, 4, 16, 768), bf16),
        gb_in=((3, 4, 16, 768), bf16),
        gb_f=((4, 16, 768), bf16),
        gv=((4, 2, 128, 128), bf16),
        gv_y=((4, 2, 64, 128), bf16),
        gv_z=((4, 2, 64, 128), bf16),
        gv_in=((3, 2, 64, 128), bf16),
        gv_f=((2, 2, 32, 128), bf16),
        gk8=((2048, 128), f32),
        gm_own=((128, 1024), f32),
        skip_sum=((16, 128), f32),
        skip_in=((16, 128), f32),
        gcoef=((2, 16, 512), f32),
        gcoef_in=((16, 512), f32),
        gv_out=((8, 16, 1024), bf16),
        g_val=((128, 1024), bf16),
        gvp_t=((1024, 128), bf16),
        br_in=((2, 256, 1024), bf16),
        br_xin=((256, 1024), bf16),
        gn_in=((2, 256, 1024), bf16),
        gn_xin=((256, 1024), bf16),
        ng=((4, 8, 128), f32),
        ng_in=((7, 8, 128), f32),
        ng_f=((8, 128), f32),
        ng_fin=((3, 8, 128), f32),
    )
    names = list(ins) + list(outs) + list(scratch) + ["ssem", "rsem"]
    vmem = pl.BlockSpec(memory_space=pltpu.VMEM)
    got = pl.pallas_call(
        functools.partial(layer_kernel, names),
        out_shape=[jax.ShapeDtypeStruct(s, t) for s, t in outs.values()],
        in_specs=[vmem] * len(ins),
        out_specs=[vmem] * len(outs),
        scratch_shapes=[pltpu.VMEM(s, t) for s, t in scratch.values()]
        + [pltpu.SemaphoreType.DMA((N_SEMS,)), pltpu.SemaphoreType.DMA((N_SEMS,))],
        compiler_params=pltpu.CompilerParams(
            collective_id=0, has_side_effects=True, vmem_limit_bytes=64 << 20
        ),
    )(*ins.values())
    up_rows, back_rows = w_up.shape[0], w_back.shape[0]
    final = [
        jax.ShapeDtypeStruct((2, 128, 1024), bf16),
        jax.ShapeDtypeStruct((2, 128, 1024), f32),
        jax.ShapeDtypeStruct((1, 32), f32),
        jax.ShapeDtypeStruct((1, 32), f32),
        jax.ShapeDtypeStruct((up_rows, 3072), f32),
        jax.ShapeDtypeStruct((up_rows, 512), f32),
        jax.ShapeDtypeStruct((back_rows, 3072), f32),
        jax.ShapeDtypeStruct((96, 1024), f32),
        jax.ShapeDtypeStruct((32, 512), f32),
        jax.ShapeDtypeStruct((1, 32), f32),
    ]
    out = pl.pallas_call(
        last_kernel,
        out_shape=final,
        in_specs=[vmem] * len(outs),
        out_specs=[vmem] * len(final),
        compiler_params=pltpu.CompilerParams(vmem_limit_bytes=32 << 20),
    )(*got)
    return tuple(v.reshape(-1) if v.shape[0] == 1 else v for v in out)


def last_kernel(*refs):
    (result, g_tokens, norm, up, value, back, down, coef, skip), out = refs[:9], refs[9:]
    out[0][...] = result[...]
    out[1][...] = g_tokens[...]
    out[2][...] = norm[0:1, 0:32]
    out[3][...] = norm[2:3, 0:32]
    for rr in range(4):
        out[4][:, 768 * rr : 768 * rr + 768] = up[rr].astype(f32)
        out[6][:, 768 * rr : 768 * rr + 768] = back[rr].astype(f32)
    out[5][...] = value[...]
    out[7][...] = down[...]
    out[8][...] = coef[...]
    same = lax.broadcasted_iota(jnp.int32, (32, 32), 0) == lax.broadcasted_iota(
        jnp.int32, (32, 32), 1
    )
    column = jnp.broadcast_to(skip[:, 127:128], (32, 32))
    out[9][...] = jnp.sum(jnp.where(same, column, 0.0), axis=0, keepdims=True)


def run(tokens, *rest):
    sizes = (lax.axis_size("item"), lax.axis_size("tok"), tokens.shape)
    if sizes == (2, 16, (2, 128, 1024)):
        return fast_body(tokens, *rest)
    return body(tokens, *rest)


def solution(mesh):
    in_specs = (
        P("item", "tok", None),
        P(("item", "tok")),
        P(("item", "tok")),
        P(("item", "tok"), None),
        P(("item", "tok"), None),
        P(("item", "tok"), None),
        P(("item", "tok"), None),
        P("tok", "item"),
        P("tok"),
        P("item", "tok", None),
    )
    out_specs = (
        P("item", "tok", None),
        P("item", "tok", None),
        P(("item", "tok")),
        P(("item", "tok")),
        P(("item", "tok"), None),
        P(("item", "tok"), None),
        P(("item", "tok"), None),
        P(("item", "tok"), None),
        P("tok", "item"),
        P("tok"),
    )
    return jax.shard_map(run, mesh=mesh, in_specs=in_specs, out_specs=out_specs, check_vma=False)
```

```python
import functools
import math
import types

import jax
import jax.numpy as jnp
import ml_dtypes
import numpy as np
from jax import lax
from jax.experimental import pallas as pl
from jax.experimental.pallas import tpu as pltpu
from jax.sharding import PartitionSpec as P

highest = lax.Precision.HIGHEST


def basis_block(start_index, block_width, length, states):
    places = start_index + jnp.arange(block_width, dtype=jnp.int32)
    mode_ids = jnp.arange(states, dtype=jnp.int32)
    fraction = (mode_ids * 41 % states).astype(jnp.float32) / states
    mode_rates = jnp.exp(jnp.log(1.0 / 32.0) + fraction * jnp.log(32.0 / (4.0 * length)))
    decays = jnp.exp(-mode_rates[:, None] * places[None, :].astype(jnp.float32))
    phase_turns = (mode_ids[:, None] * places[None, :] % (2 * states)).astype(jnp.float32) * (
        jnp.pi / states
    )
    return jnp.concatenate([decays * jnp.cos(phase_turns), decays * jnp.sin(phase_turns)], axis=0)


def make_kernel(coef_full, length):
    states = coef_full.shape[1] // 2
    block_width = math.gcd(length, 2048)
    block_count = length // block_width

    def one_block(block_index):
        table = basis_block(block_index * block_width, block_width, length, states)
        return jnp.dot(coef_full, table, precision=highest)

    pieces = lax.map(one_block, jnp.arange(block_count, dtype=jnp.int32))
    return jnp.transpose(pieces, (1, 0, 2)).reshape(coef_full.shape[0], length)


def coef_gradient(grad_kernel, states):
    channels, length = grad_kernel.shape
    block_width = math.gcd(length, 2048)
    block_count = length // block_width
    slabs = grad_kernel.reshape(channels, block_count, block_width)

    def add_block(running, block_index):
        slab_part = lax.dynamic_index_in_dim(slabs, block_index, 1, keepdims=False)
        table = basis_block(block_index * block_width, block_width, length, states)
        return (running + jnp.dot(slab_part, table.T, precision=highest), None)

    start_total = jnp.zeros((channels, 2 * states), jnp.float32)
    summed, unused = lax.scan(add_block, start_total, jnp.arange(block_count, dtype=jnp.int32))
    return summed


def unit_tables(row_count, column_count, period):
    row_ids = jnp.arange(row_count, dtype=jnp.int32)[:, None]
    column_ids = jnp.arange(column_count, dtype=jnp.int32)[None, :]
    phase_turns = (row_ids * column_ids % period).astype(jnp.float32) * (2.0 * jnp.pi / period)
    return (jnp.cos(phase_turns), jnp.sin(phase_turns))


def right_product(left_part, table):
    return jnp.einsum("...kq,qm->...km", left_part, table, precision=highest)


def spectrum(signal):
    length = signal.shape[-1]
    padded_size = 2 * length
    outer_size = padded_size // 128
    half_size = outer_size // 2
    folded = signal.reshape(signal.shape[:-1] + (half_size, 128))
    cos_outer, sin_outer = unit_tables(outer_size, half_size, outer_size)
    section_real = jnp.einsum("kp,...pq->...kq", cos_outer, folded, precision=highest)
    section_imag = -jnp.einsum("kp,...pq->...kq", sin_outer, folded, precision=highest)
    twist_cos, twist_sin = unit_tables(outer_size, 128, padded_size)
    turned_real = section_real * twist_cos + section_imag * twist_sin
    turned_imag = section_imag * twist_cos - section_real * twist_sin
    cos_inner, sin_inner = unit_tables(128, 128, 128)
    out_real = right_product(turned_real, cos_inner) + right_product(turned_imag, sin_inner)
    out_imag = right_product(turned_imag, cos_inner) - right_product(turned_real, sin_inner)
    return (out_real, out_imag)


def inverse(spec_real, spec_imag):
    outer_size = spec_real.shape[-2]
    padded_size = outer_size * 128
    half_size = outer_size // 2
    cos_inner, sin_inner = unit_tables(128, 128, 128)
    back_real = right_product(spec_real, cos_inner) - right_product(spec_imag, sin_inner)
    back_imag = right_product(spec_real, sin_inner) + right_product(spec_imag, cos_inner)
    twist_cos, twist_sin = unit_tables(outer_size, 128, padded_size)
    turned_real = back_real * twist_cos - back_imag * twist_sin
    turned_imag = back_real * twist_sin + back_imag * twist_cos
    cos_outer, sin_outer = unit_tables(half_size, outer_size, outer_size)
    signal = jnp.einsum("pk,...kq->...pq", cos_outer, turned_real, precision=highest)
    signal = signal - jnp.einsum("pk,...kq->...pq", sin_outer, turned_imag, precision=highest)
    return signal.reshape(signal.shape[:-2] + (half_size * 128,)) / padded_size


def layer_norm(token_rows, gain_row, shift_row):
    row_mean = jnp.mean(token_rows, axis=-1, keepdims=True)
    centered = token_rows - row_mean
    variance = jnp.mean(centered * centered, axis=-1, keepdims=True)
    return centered * lax.rsqrt(variance + 1e-05) * gain_row + shift_row


def body(
    tokens, norm_gain, norm_shift, w_up, w_value, w_back, w_down, mode_coef, skip_gain, cotangent
):
    gain_full, shift_full, up_full, value_full = (
        lax.all_gather(norm_gain, ("item", "tok"), axis=0, tiled=True),
        lax.all_gather(norm_shift, ("item", "tok"), axis=0, tiled=True),
        lax.all_gather(w_up, ("item", "tok"), axis=0, tiled=True),
        lax.all_gather(w_value, ("item", "tok"), axis=0, tiled=True),
    )
    back_full, down_full = (
        lax.all_gather(w_back, ("item", "tok"), axis=0, tiled=True),
        lax.all_gather(w_down, ("item", "tok"), axis=0, tiled=True),
    )
    coef_full = lax.all_gather(mode_coef, "item", axis=1, tiled=True)
    token_rows = tokens.astype(jnp.float32)
    gain_float = gain_full.astype(jnp.float32)
    shift_float = shift_full.astype(jnp.float32)
    normed = layer_norm(token_rows, gain_float, shift_float).astype(jnp.bfloat16)
    up_pre = jnp.einsum("std,df->stf", normed, up_full, preferred_element_type=jnp.float32)
    value_pre = jnp.einsum("std,dh->sht", normed, value_full, preferred_element_type=jnp.float32)
    value = jax.nn.gelu(value_pre).astype(jnp.bfloat16)
    channel_values = lax.all_to_all(value, "tok", split_axis=1, concat_axis=2, tiled=True)
    length = channel_values.shape[-1]
    kernel = make_kernel(coef_full.astype(jnp.float32), length)
    signal = channel_values.astype(jnp.float32)
    skip_column = skip_gain.astype(jnp.float32)[:, None]
    value_real, value_imag = spectrum(signal)
    kernel_real, kernel_imag = spectrum(kernel)
    conv_out = inverse(
        value_real * kernel_real - value_imag * kernel_imag,
        value_real * kernel_imag + value_imag * kernel_real,
    )
    mixed_channels = (conv_out + skip_column * signal).astype(jnp.bfloat16)
    mixed = lax.all_to_all(mixed_channels, "tok", split_axis=2, concat_axis=1, tiled=True)
    gate = jnp.einsum("sht,hf->stf", mixed, back_full, preferred_element_type=jnp.float32)
    up_act = jax.nn.gelu(up_pre)
    hidden = (up_act * gate).astype(jnp.bfloat16)
    branch = jnp.einsum("stf,fd->std", hidden, down_full, preferred_element_type=jnp.float32)
    result = (token_rows + branch).astype(jnp.bfloat16)
    grad_w_down = jnp.einsum("stf,std->fd", hidden, cotangent, preferred_element_type=jnp.float32)
    grad_hidden = jnp.einsum(
        "std,fd->stf", cotangent, down_full, preferred_element_type=jnp.float32
    )
    grad_gate = (grad_hidden * up_act).astype(jnp.bfloat16)
    grad_up_act = grad_hidden * gate
    grad_w_back = jnp.einsum("sht,stf->hf", mixed, grad_gate, preferred_element_type=jnp.float32)
    grad_mixed = jnp.einsum(
        "stf,hf->sht", grad_gate, back_full, preferred_element_type=jnp.float32
    ).astype(jnp.bfloat16)
    grad_channels = lax.all_to_all(grad_mixed, "tok", split_axis=1, concat_axis=2, tiled=True)
    grad_signal = grad_channels.astype(jnp.float32)
    grad_real, grad_imag = spectrum(grad_signal)
    grad_value_channels = inverse(
        kernel_real * grad_real + kernel_imag * grad_imag,
        kernel_real * grad_imag - kernel_imag * grad_real,
    )
    grad_value_channels = (grad_value_channels + skip_column * grad_signal).astype(jnp.bfloat16)
    grad_kernel = inverse(
        jnp.sum(grad_real * value_real + grad_imag * value_imag, axis=0),
        jnp.sum(grad_imag * value_real - grad_real * value_imag, axis=0),
    )
    grad_skip_part = jnp.sum(grad_signal * signal, axis=(0, 2))
    grad_coef_part = coef_gradient(grad_kernel, coef_full.shape[1] // 2)
    grad_mode_coef = lax.psum_scatter(grad_coef_part, "item", scatter_dimension=1, tiled=True)
    grad_skip_gain = lax.psum(grad_skip_part, "item")
    grad_value = lax.all_to_all(grad_value_channels, "tok", split_axis=2, concat_axis=1, tiled=True)
    gelu_value_back = jax.vjp(jax.nn.gelu, value_pre)[1]
    grad_value_pre = gelu_value_back(grad_value.astype(jnp.float32))[0].astype(jnp.bfloat16)
    gelu_up_back = jax.vjp(jax.nn.gelu, up_pre)[1]
    grad_up_pre = gelu_up_back(grad_up_act)[0].astype(jnp.bfloat16)
    grad_w_up = jnp.einsum("std,stf->df", normed, grad_up_pre, preferred_element_type=jnp.float32)
    grad_w_value = jnp.einsum(
        "std,sht->dh", normed, grad_value_pre, preferred_element_type=jnp.float32
    )
    grad_normed = jnp.einsum(
        "stf,df->std", grad_up_pre, up_full, preferred_element_type=jnp.float32
    )
    grad_normed = grad_normed + jnp.einsum(
        "sht,dh->std", grad_value_pre, value_full, preferred_element_type=jnp.float32
    )
    norm_back = jax.vjp(layer_norm, token_rows, gain_float, shift_float)[1]
    grad_rows, grad_gain_part, grad_shift_part = norm_back(grad_normed)
    grad_tokens = cotangent.astype(jnp.float32) + grad_rows
    owners = lax.axis_size("item") * lax.axis_size("tok")
    norm_flat = jnp.concatenate(
        [grad_gain_part.reshape(owners, -1), grad_shift_part.reshape(owners, -1)], axis=1
    )
    up_flat = grad_w_up.reshape(owners, -1)
    value_flat = grad_w_value.reshape(owners, -1)
    back_flat = grad_w_back.reshape(owners, -1)
    down_flat = grad_w_down.reshape(owners, -1)
    summed = (
        lax.psum_scatter(norm_flat, ("item", "tok"), scatter_dimension=0, tiled=True),
        lax.psum_scatter(up_flat, ("item", "tok"), scatter_dimension=0, tiled=True),
        lax.psum_scatter(value_flat, ("item", "tok"), scatter_dimension=0, tiled=True),
        lax.psum_scatter(back_flat, ("item", "tok"), scatter_dimension=0, tiled=True),
        lax.psum_scatter(down_flat, ("item", "tok"), scatter_dimension=0, tiled=True),
    )
    gain_count = norm_gain.shape[0]
    norm_row = summed[0].reshape(-1)
    grad_norm_gain = norm_row[:gain_count]
    grad_norm_shift = norm_row[gain_count:]
    grad_up_out = summed[1].reshape(w_up.shape)
    grad_value_out = summed[2].reshape(w_value.shape)
    grad_back_out = summed[3].reshape(w_back.shape)
    grad_down_out = summed[4].reshape(w_down.shape)
    return (
        result,
        grad_tokens,
        grad_norm_gain,
        grad_norm_shift,
        grad_up_out,
        grad_value_out,
        grad_back_out,
        grad_down_out,
        grad_mode_coef,
        grad_skip_gain,
    )


MESH_ID = pl.DeviceIdType.MESH
bf16, f32 = jnp.bfloat16, jnp.float32
NT = (((1,), (1,)), ((), ()))
GC = math.sqrt(2.0 / math.pi)


def dot(a, b):
    return jnp.dot(a, b, preferred_element_type=f32)


def dot_nt(a, b):
    return lax.dot_general(a, b, NT, preferred_element_type=f32)


def gelu_parts(v):
    t = jnp.tanh(GC * (v + 0.044715 * v * v * v))
    half = 0.5 * (1.0 + t)
    slope = half + 0.5 * v * (1.0 - t * t) * (GC * (1.0 + 3 * 0.044715 * v * v))
    return v * half, slope


def split(v):
    high = v.astype(bf16)
    return high, (v - high.astype(f32)).astype(bf16)


def mode_tables(states, length):
    n = np.arange(states)
    rates = np.exp(np.log(1.0 / 32.0) + (n * 41 % states) / states * np.log(32.0 / (4.0 * length)))

    def table(places):
        decay = np.exp(-rates[:, None] * places[None, :])
        turn = (n[:, None] * places[None, :] % (2 * states)) * (np.pi / states)
        return decay * np.cos(turn), decay * np.sin(turn)

    far_re, far_im = table(np.arange(0, length, 128))
    near = np.concatenate(table(np.arange(128)), axis=0).astype(np.float32)
    high = near.astype(ml_dtypes.bfloat16)
    low = (near - high.astype(np.float32)).astype(ml_dtypes.bfloat16)
    return (
        far_re.T.astype(np.float32).copy(),
        far_im.T.astype(np.float32).copy(),
        high,
        low,
        high.T[::-1].copy(),
        low.T[::-1].copy(),
    )


class Links:
    def __init__(self, send_sems, recv_sems, place):
        self.send_sems, self.recv_sems, self.place = send_sems, recv_sems, place
        self.count = 0
        self.pending = []

    def take(self, n=1):
        first = self.count
        self.count += n
        return first

    def make(self, src, dst, ssem, rsem, to):
        return pltpu.make_async_remote_copy(
            src_ref=src,
            dst_ref=dst,
            send_sem=self.send_sems.at[ssem],
            recv_sem=self.recv_sems.at[rsem],
            device_id=to,
            device_id_type=MESH_ID,
        )

    def put(self, src, dst, to):
        slot = self.take()
        copy = self.make(src, dst, slot, slot, to)
        copy.start()
        self.pending.append((copy, None))
        return slot

    def got(self, slot, region):
        self.make(region, region, slot, slot, self.place).wait_recv()

    def put_or_keep(self, src, dst, ssem, rsem, to, here):
        remote = self.make(src, dst, ssem, rsem, to)
        local = pltpu.make_async_copy(src, dst, self.recv_sems.at[rsem])
        away = jnp.logical_not(here)
        pl.when(here)(local.start)
        pl.when(away)(remote.start)
        self.pending.append((remote, away))

    def finish(self):
        for copy, away in self.pending:
            if away is None:
                copy.wait_send()
            else:
                pl.when(away)(copy.wait_send)


N_SEMS = 200


def layer_kernel(names, *refs):
    r_ = dict(zip(names, refs))
    g = types.SimpleNamespace(**r_)
    x = lax.axis_index("item")
    tok = lax.axis_index("tok")
    z, y, c = tok // 4, (tok // 2) % 2, tok % 2
    n = tok // 2
    r = 2 * x + c

    def dev(x_, z_, y_, c_):
        return (x_, z_ * 4 + y_ * 2 + c_)

    def zo(k):
        return lax.rem(z + k, 4)

    def zb(k):
        return lax.rem(z + 4 - k, 4)

    def node(z_, y_):
        return 2 * z_ + y_

    sib, xn, diag = dev(x, z, y, 1 - c), dev(1 - x, z, y, c), dev(1 - x, z, y, 1 - c)
    r_sib, r_xn, r_diag = 2 * x + 1 - c, 2 * (1 - x) + c, 2 * (1 - x) + 1 - c
    members = ((sib, x, 1 - c, r_sib), (xn, 1 - x, c, r_xn), (diag, 1 - x, 1 - c, r_diag))
    ynb = dev(x, z, 1 - y, c)
    lk = Links(g.ssem, g.rsem, ynb)
    aligned = pl.multiple_of

    barrier = pltpu.get_barrier_semaphore()
    partners = [m[0] for m in members]
    for k in range(1, 4):
        partners += [dev(x, zo(k), y, c), dev(x, zo(k), 1 - y, c), dev(x, zo(k), y, 1 - c)]
    partners.append(ynb)
    for p in partners:
        pl.semaphore_signal(barrier, inc=1, device_id=p, device_id_type=MESH_ID)

    eye = lax.broadcasted_iota(jnp.int32, (32, 128), 0) == lax.broadcasted_iota(
        jnp.int32, (32, 128), 1
    )
    eye = eye.astype(bf16)
    ch_i = lax.broadcasted_iota(jnp.int32, (512, 128), 0)
    p_i = lax.broadcasted_iota(jnp.int32, (512, 128), 1)
    row16 = lax.broadcasted_iota(jnp.int32, (16, 128), 0)
    gain_row = dot(g.norm_gain[...], eye)
    shift_row = dot(g.norm_shift[...], eye)
    norm_pack = jnp.where(
        row16 == 0,
        jnp.broadcast_to(gain_row, (16, 128)),
        jnp.where(row16 == 1, jnp.broadcast_to(shift_row, (16, 128)), 0.0),
    ).astype(bf16)
    for rr in range(4):
        pick = ch_i == 64 * (p_i // 16) + 32 * (rr % 2) + 16 * (rr // 2) + p_i % 16
        pick = pick.astype(bf16)
        g.perm[:, 128 * rr : 128 * rr + 128] = pick
        g.pk_send[rr, 0:32, :] = dot(g.w_value[...], pick).astype(bf16)
        g.pk_send[rr, 32:48, :] = norm_pack
    pl.semaphore_wait(barrier, len(partners))

    pk_s, up_s, back_s = [], [], []
    for to, xm, cm, rm in members:
        pk_s.append(lk.put(g.pk_send.at[rm], g.pk.at[x, n, c], to))
    coef_s = lk.put(g.mode_coef.at[pl.ds(aligned(16 * (1 - x), 16), 16), :], g.coef.at[x], xn)
    tok_x = lk.put(g.tokens, g.tok_all.at[r], xn)
    my_back = g.w_back_all.at[c, y, x, z]

    def cols(rm):
        return pl.ds(aligned(768 * rm, 128), 768)

    for to, xm, cm, rm in members:
        up_s.append(lk.put(g.w_up.at[:, cols(rm)], g.w_up_all.at[x, n, c], to))
    for to, xm, cm, rm in members:
        back_s.append(lk.put(g.w_back.at[:, cols(rm)], my_back, to))
    tok_sib = lk.put(g.tokens, g.tok_all.at[r], sib)
    cot_x = lk.put(g.cot, g.cot_all.at[r], xn)
    cot_sib = lk.put(g.cot, g.cot_all.at[r], sib)
    g.pk[x, n, c] = g.pk_send[r]
    g.w_up_all[x, n, c] = g.w_up[:, cols(r)]
    g.w_back_all[c, y, x, z] = g.w_back[:, cols(r)]
    g.cot_all[r] = g.cot[...]
    g.coef[x] = g.mode_coef[pl.ds(aligned(16 * x, 16), 16), :]

    def gather_start(region):
        slots = {}
        for k in (1, 2, 3):
            slots[k] = lk.put(region(z, y), region(z, y), dev(x, zo(k), y, c))
        slots[4] = lk.put(region(z, y), region(z, y), ynb)
        return slots

    def gather_pass(slots, region, k):
        lk.got(slots[k], region(zb(k), y))
        slots[4 + k] = lk.put(region(zb(k), y), region(zb(k), y), ynb)

    def gather_end(slots, region):
        for k in range(4):
            lk.got(slots[4 + k], region(zb(k), 1 - y))

    def pk_region(z_, y_):
        return g.pk.at[:, node(z_, y_)]

    def up_region(z_, y_):
        return g.w_up_all.at[:, node(z_, y_)]

    def back_region(z_, y_):
        return g.w_back_all.at[:, y_, :, z_]

    for i, (to, xm, cm, rm) in enumerate(members):
        lk.got(pk_s[i], g.pk.at[xm, n, cm])
    pk_g = gather_start(pk_region)

    def line(region, has):
        right, left, across = lk.take(3), lk.take(3), lk.take(4)
        passes = lk.take(3)

        def send(zs, ssem, rsem, to, when):
            copy = lk.make(region(zs, y), region(zs, y), ssem, rsem, to)
            pl.when(when)(copy.start)
            lk.pending.append((copy, when))

        def also(when, zs):
            return when if has is None else jnp.logical_and(when, has(zs))

        def step(k):
            for way, base in ((-1, right), (1, left)):
                if k == 0 and way == 1:
                    continue
                zs = z + way * k
                there = also(z >= k if way == -1 else z + k <= 3, zs)
                if k:
                    slot = base + k - 1
                    block = region(lax.rem(zs + 4, 4), y)
                    wait = lk.make(block, block, slot, slot, ynb)
                    pl.when(there)(wait.wait_recv)
                zs = lax.rem(zs + 4, 4)
                if k < 3 and (way == -1 or k == 0):
                    on = jnp.logical_and(there, z < 3)
                    send(zs, right + k, right + k, dev(x, zo(1), y, c), on)
                if k < 3 and (way == 1 or k == 0):
                    on = jnp.logical_and(there, z > 0)
                    send(zs, left + k, left + k, dev(x, zb(1), y, c), on)
                ssem = across + k if way == -1 else passes + k - 1
                send(zs, ssem, across + zs, ynb, there)

        def end():
            for zs in range(4):
                block = region(zs, 1 - y)
                wait = lk.make(block, block, across + zs, across + zs, ynb)
                if has is None:
                    wait.wait_recv()
                else:
                    pl.when(has(zs))(wait.wait_recv)

        return step, end

    def down_region(z_, y_):
        return g.w_down_all.at[lax.rem(z_, 2), y_]

    def down_has(z_):
        return (z_ + 4) // 2 == c + 2

    owner = z // 2
    dn_own = lk.take()
    dst = g.w_down_all.at[lax.rem(z, 2), y, c]
    dn_copy = lk.make(g.w_down, dst, dn_own, dn_own, sib)
    pl.when(owner != c)(dn_copy.start)
    lk.pending.append((dn_copy, owner != c))

    @pl.when(owner == c)
    def _():
        g.w_down_all[lax.rem(z, 2), y, c] = g.w_down[...]
        block = g.w_down_all.at[lax.rem(z, 2), y, 1 - c]
        lk.make(block, block, dn_own, dn_own, sib).wait_recv()

    down_step, down_end = line(down_region, down_has)
    up_step, up_end = line(up_region, None)
    back_step, back_end = line(back_region, None)
    down_step(0)

    lk.got(coef_s, g.coef.at[1 - x])
    cc = g.coef[0].astype(f32)
    sc = g.coef[1].astype(f32)

    def far(p, _):
        hr = g.far_re[pl.ds(p, 1), :]
        hi = g.far_im[pl.ds(p, 1), :]
        rows = pl.ds(aligned(16 * p, 16), 16)
        g.state[rows, 0:512] = cc * hr + sc * hi
        g.state[rows, 512:1024] = sc * hr - cc * hi
        return 0

    lax.fori_loop(0, 16, far, 0)
    for half in range(2):
        rows = slice(128 * half, 128 * half + 128)
        hi_, lo_ = split(g.state[rows, :])
        g.kern[rows, :] = (
            dot(hi_, g.near_hi[...]) + dot(lo_, g.near_hi[...]) + dot(hi_, g.near_lo[...])
        )
    for k in (1, 2, 3):
        gather_pass(pk_g, pk_region, k)
    ii = lax.broadcasted_iota(jnp.int32, (128, 128), 0)
    jj = lax.broadcasted_iota(jnp.int32, (128, 128), 1)
    flip = (ii + jj == 127).astype(bf16)

    def toeplitz(h, _):
        prev = jnp.zeros((128, 128), f32)
        for k in range(16):
            row = jnp.broadcast_to(g.kern[pl.ds(16 * k + h, 1), :], (128, 128))
            turned = pltpu.roll(row, 0, 1, stride=1, stride_axis=0)
            g.toep[h, k] = jnp.where(jj >= ii, turned, prev).astype(bf16)
            prev = turned
        return 0

    lax.fori_loop(0, 16, toeplitz, 0, unroll=2)
    down_step(1)

    gather_end(pk_g, pk_region)
    e_i = lax.broadcasted_iota(jnp.int32, (128, 1024), 0)
    e_j = lax.broadcasted_iota(jnp.int32, (128, 1024), 1)
    spread = jnp.logical_and(e_i < 32, lax.rem(e_j, 32) == e_i).astype(bf16)
    blk = lax.broadcasted_iota(jnp.int32, (16, 1024), 1) // 32
    acc = jnp.zeros((16, 1024), f32)
    for xm in range(2):
        for nm in range(8):
            for cm in range(2):
                rows = g.pk[xm, nm, cm, 32:48, :]
                acc = acc + jnp.where(
                    blk == 16 * xm + 2 * nm + cm, dot(rows, spread), 0.0
                )
    gain = acc[0:1, :]
    shift = acc[1:2, :]
    g.norm_rows[0:1, :] = gain
    g.norm_rows[1:2, :] = shift
    wv = g.pk[:, :, :, 0:32, :].reshape(1024, 128)
    g.w_val[...] = wv
    wvt = wv.T
    for t in range(8):
        at = 256 * (t % 4) + 128 * (t // 4)
        g.w_val_t[:, at : at + 128] = wvt[:, 128 * t : 128 * t + 128]

    def norm_block(read, q):
        def part(s_, _):
            rows = read(s_).astype(f32)
            mean = jnp.mean(rows, axis=-1, keepdims=True)
            cen = rows - mean
            var = jnp.mean(cen * cen, axis=-1, keepdims=True)
            out = (cen * lax.rsqrt(var + 1e-5) * g.norm_rows[0:1, :] + g.norm_rows[1:2, :]).astype(
                bf16
            )
            at = aligned(256 * q + 128 * s_, 128)
            g.normed[pl.ds(at, 128), :] = out
            for t in range(8):
                low = 256 * (t % 4) + 128 * (t // 4)
                g.normed_t[low : low + 128, pl.ds(at, 128)] = out[:, 128 * t : 128 * t + 128].T
            return 0

        lax.fori_loop(0, 2, part, 0)
        at = pl.ds(aligned(256 * q, 128), 256)
        pre = dot(g.w_val_t[...], g.normed_t[:, at])
        act, slope = gelu_parts(pre)
        g.val_slope[:, at] = slope
        g.val[:, at] = act.astype(bf16)

    norm_block(lambda s_: g.tokens[s_], r)
    lk.got(tok_sib, g.tok_all.at[r_sib])
    norm_block(lambda s_: g.tok_all[r_sib, s_], r_sib)
    lk.got(tok_x, g.tok_all.at[r_xn])
    tok_f = lk.put(g.tok_all.at[r_xn], g.tok_all.at[r_xn], sib)
    norm_block(lambda s_: g.tok_all[r_xn, s_], r_xn)
    lk.got(tok_f, g.tok_all.at[r_diag])
    norm_block(lambda s_: g.tok_all[r_diag, s_], r_diag)

    def channel_send(src, landing):
        slots = []
        for k in range(1, 8):
            to = lax.rem(n + k, 8)
            slots.append(
                lk.put(
                    src.at[pl.ds(aligned(16 * to, 16), 16), :],
                    landing.at[n],
                    (x, 2 * to + c),
                )
            )
        return slots

    def channel_got(slots, landing):
        for k in range(1, 8):
            lk.got(slots[k - 1], landing.at[lax.rem(n + 8 - k, 8)])

    def unpack(landing, put):
        def one(nm, _):
            for tb in range(8):
                s_, cm = 2 * (tb // 4) + tb % 2, (tb // 2) % 2
                put(s_, 2 * nm + cm, landing[nm, :, 128 * tb : 128 * tb + 128].astype(f32))
            return 0

        lax.fori_loop(0, 8, one, 0)

    def put_val(s_, i, tile):
        g.v32[pl.ds(32 * s_ + 16 + i, 16, stride=128), :] = tile
        g.vr32[pl.ds(16 * s_ + 15 - i, 16, stride=64), :] = tile

    def put_grad(s_, i, tile):
        g.v32[pl.ds(32 * s_ + 31 - i, 16, stride=128), :] = tile

    val_s = channel_send(g.val, g.val_in)
    g.val_in[n] = g.val[pl.ds(aligned(16 * n, 16), 16), :]
    down_step(2)
    for i, (to, xm, cm, rm) in enumerate(members):
        lk.got(up_s[i], g.w_up_all.at[xm, n, cm])
    up_step(0)
    down_step(3)

    zero = jnp.zeros((16, 128), f32)
    for i in range(64):
        g.v32[32 * i : 32 * i + 16, :] = zero
    diag_i = lax.broadcasted_iota(jnp.int32, (32, 32), 0) == lax.broadcasted_iota(
        jnp.int32, (32, 32), 1
    )
    skip_row = jnp.broadcast_to(g.skip[...].astype(f32), (32, 32))
    g.skip_b[...] = dot(jnp.where(diag_i, skip_row, 0.0).astype(bf16), jnp.ones((32, 128), bf16))

    channel_got(val_s, g.val_in)
    unpack(g.val_in, put_val)
    up_step(1)

    def conv_rows(h, k):
        rows = [g.v32[pl.ds(128 * h + 32 * s_ + 16 - k, 16), :] for s_ in range(4)]
        return jnp.concatenate(rows, axis=0)

    def conv(h, _):
        parts = [conv_rows(h, k) for k in range(16)]
        out = g.skip_b[pl.ds(16 * x + h, 1), :] * parts[0]
        for kk in range(8):
            lhs = jnp.concatenate([parts[2 * kk], parts[2 * kk + 1]], axis=1).astype(bf16)
            out = out + dot(lhs, g.toep[h, 2 * kk : 2 * kk + 2].reshape(256, 128))
        g.o32[pl.ds(aligned(64 * h, 64), 64), :] = out
        return 0

    def pack(out, back):
        def one(nm, _):
            for tb in range(8):
                s_, cm = 2 * (tb // 4) + tb % 2, (tb // 2) % 2
                i = 2 * nm + cm
                at = pl.ds(16 * s_ + (15 - i if back else i), 16, stride=64)
                out[nm, :, 128 * tb : 128 * tb + 128] = g.o32[at, :].astype(bf16)
            return 0

        lax.fori_loop(0, 8, one, 0)

    def channel_back(src, landing):
        slots = []
        for k in range(1, 8):
            to = lax.rem(n + k, 8)
            slots.append(
                lk.put(src.at[to], landing.at[pl.ds(aligned(16 * n, 16), 16), :], (x, 2 * to + c))
            )
        return slots

    def channel_back_got(slots, landing):
        for k in range(1, 8):
            at = aligned(16 * lax.rem(n + 8 - k, 8), 16)
            lk.got(slots[k - 1], landing.at[pl.ds(at, 16), :])

    lax.fori_loop(0, 16, conv, 0, unroll=2)
    pack(g.mix_out, False)
    mix_s = channel_back(g.mix_out, g.mix.at[r])
    g.mix[r, pl.ds(aligned(16 * n, 16), 16), :] = g.mix_out[n]

    up_step(2)
    for i, (to, xm, cm, rm) in enumerate(members):
        lk.got(back_s[i], g.w_back_all.at[cm, y, xm, z])
    back_step(0)
    lk.got(cot_x, g.cot_all.at[r_xn])
    cot_f = lk.put(g.cot_all.at[r_xn], g.cot_all.at[r_xn], sib)
    down_end()
    lk.got(cot_sib, g.cot_all.at[r_sib])
    lk.got(cot_f, g.cot_all.at[r_diag])
    down2d = g.w_down_all.reshape(768, 1024)
    cot2d = g.cot_all.reshape(1024, 1024)

    def hidden_tile(q, _):
        rows = pl.ds(aligned(256 * q, 256), 256)
        g.slope[rows, :] = dot_nt(cot2d[rows, :], down2d[...])
        return 0

    lax.fori_loop(0, 4, hidden_tile, 0)
    up_step(3)
    back_step(1)
    channel_back_got(mix_s, g.mix.at[r])
    mix_x = lk.put(g.mix.at[r], g.mix.at[r], xn)
    mix_sib = lk.put(g.mix.at[r], g.mix.at[r], sib)
    back_step(2)

    up_end()
    up2d = g.w_up_all.reshape(1024, 768)

    def up_tile(q, _):
        rows = pl.ds(aligned(256 * q, 256), 256)
        act, slope = gelu_parts(dot(g.normed[rows, :], up2d[...]))
        gh = g.slope[rows, :]
        g.act[rows, :] = act
        g.g_gate[rows, :] = (gh * act).astype(bf16)
        g.slope[rows, :] = gh * slope
        return 0

    back_step(3)
    lax.fori_loop(0, 4, up_tile, 0)
    lk.got(mix_x, g.mix.at[r_xn])
    mix_f = lk.put(g.mix.at[r_xn], g.mix.at[r_xn], sib)
    back_end()
    back2d = g.w_back_all.reshape(512, 768)

    def mixed_part(ranks, q):
        w = [back2d[pl.ds(aligned(128 * rr, 128), 128), :] for rr in ranks]
        w = w[0] if len(w) == 1 else jnp.concatenate(w, axis=0)
        return dot_nt(w, g.g_gate[pl.ds(aligned(512 * q, 512), 512), :])

    def gm_sib(q, _):
        at = pl.ds(aligned(512 * q, 128), 512)
        both = mixed_part((1 - c, 2 + 1 - c), q).astype(bf16)
        g.gm_send[:, :, at] = both.reshape(2, 128, 512)
        return 0

    lax.fori_loop(0, 2, gm_sib, 0)
    gm_s = lk.put(g.gm_send, g.gm_in, sib)
    lk.got(mix_sib, g.mix.at[r_sib])
    lk.got(mix_f, g.mix.at[r_diag])

    mix2d = g.mix.reshape(512, 1024)

    def back_tile(i, _):
        at = pl.ds(aligned(384 * i, 128), 384)
        part = dot(mix2d[...], g.g_gate[:, at]).astype(bf16)
        g.gb[:, :, :, at] = part.reshape(2, 2, 128, 384)
        return 0

    lax.fori_loop(0, 2, back_tile, 0)
    gb_y = lk.put(g.gb.at[:, 1 - y], g.gb_y, ynb)


    def gm_mine(q, _):
        at = pl.ds(aligned(512 * q, 128), 512)
        both = mixed_part((2 * (1 - x) + c, 2 * x + c), q)
        g.gm_x[:, at] = both[0:128, :].astype(bf16)
        g.gm_own[:, at] = both[128:256, :]
        return 0

    lax.fori_loop(0, 2, gm_mine, 0)
    lk.got(gm_s, g.gm_in)
    g.gm_x[...] = (g.gm_x[...].astype(f32) + g.gm_in[1 - x].astype(f32)).astype(bf16)
    gm_xs = lk.put(g.gm_x, g.gm_xin, xn)


    def turn(i, _):
        rr, tb = i // 8, lax.rem(i, 8)
        rows = pl.ds(aligned(128 * tb, 128), 128)
        at = pl.ds(aligned(128 * rr, 128), 128)
        g.mix_tok[rows, at] = g.mix[rr, :, rows].T
        return 0

    lax.fori_loop(0, 32, turn, 0, unroll=4)

    def gate_tile(q, _):
        rows = pl.ds(aligned(256 * q, 256), 256)
        gate = dot(g.mix_tok[rows, :], back2d[...])
        hidden = (g.act[rows, :] * gate).astype(bf16)
        g.hidden[rows, :] = hidden
        g.hidden_t[:, rows] = hidden.T
        g.g_up[rows, :] = (g.slope[rows, :] * gate).astype(bf16)
        return 0

    lax.fori_loop(0, 4, gate_tile, 0)

    gd_y = []

    def down_grad(zl):
        def tile(i, _):
            at = pl.ds(aligned(512 * i, 512), 512)
            part = dot(g.hidden_t[384 * zl : 384 * zl + 384, :], cot2d[:, at]).astype(bf16)
            g.gd[zl, :, :, at] = part.reshape(2, 192, 512)
            return 0

        lax.fori_loop(0, 2, tile, 0)

    def down_send(zl):
        gd_y.append(lk.put(g.gd.at[zl, 1 - y], g.gd_y.at[zl], ynb))

    down_grad(0)
    down_grad(1)

    lk.got(gm_xs, g.gm_xin)
    for tb in range(8):
        at = slice(128 * tb, 128 * tb + 128)
        total = g.gm_own[:, at] + g.gm_in[x, :, at].astype(f32) + g.gm_xin[:, at].astype(f32)
        g.gm[:, at] = dot(total.astype(bf16), flip).astype(bf16)
    gm_cs = channel_send(g.gm, g.gm_land)
    g.gm_land[n] = g.gm[pl.ds(aligned(16 * n, 16), 16), :]

    down_send(0)

    gd_r = lk.take(4)

    def down_sum(zl):
        lk.got(gd_y[zl], g.gd_y.at[zl])
        for cm in range(2):
            part = pl.ds(96 * cm, 96)
            total = g.gd[zl, y, part, :].astype(f32) + g.gd_y[zl, part, :].astype(f32)
            g.gd[zl, y, part, :] = total.astype(bf16)
            z_d = 2 * c + zl
            here = jnp.logical_and(z_d == z, c == cm)
            lk.put_or_keep(
                g.gd.at[zl, y, part], g.gd_in.at[z], lk.take(), gd_r + z, dev(x, z_d, y, cm), here
            )

    def group_sum(part, send, land, xsend, xland):
        for xm in range(2):
            send[xm] = part(xm, 1 - c).astype(bf16)
        first = lk.put(send, land, sib)
        mine = part(1 - x, c)
        lk.got(first, land)
        xsend[...] = (mine + land[1 - x].astype(f32)).astype(bf16)
        second = lk.put(xsend, xland, xn)

        def own():
            return part(x, c) + land[x].astype(f32) + xland[...].astype(f32)

        return second, own

    def branch_part(xm, cm):
        rows = pl.ds(aligned(256 * (2 * xm + cm), 256), 256)
        return dot(g.hidden[rows, :], down2d[...])

    spare = g.normed.reshape(2, 2, 256, 1024)
    br_s, br_own = group_sum(
        branch_part, spare.at[0], g.br_in, g.tok_all.at[r].reshape(256, 1024), g.br_xin
    )

    other = pl.ds(aligned(64 * (1 - y), 64), 64)
    own64 = pl.ds(aligned(64 * y, 64), 64)
    up_y, gu_s = {}, {}

    def up_grad(k):
        z_d = zo(k)
        rows = pl.ds(aligned(256 * z_d, 256), 256)
        part = dot(g.normed_t[rows, :], g.g_up[...]).astype(bf16)
        g.gu[z_d] = part.reshape(2, 128, 768)
        up_y[k] = lk.put(g.gu.at[z_d, :, other], g.gu_y.at[z_d], ynb)

    def up_sum(k):
        z_d = zo(k)
        lk.got(up_y[k], g.gu_y.at[z_d])
        total = g.gu[z_d, :, own64, :].astype(f32) + g.gu_y[z_d].astype(f32)
        g.gu[z_d, :, own64, :] = total.astype(bf16)
        if k:
            gu_s[k] = lk.put(g.gu.at[z_d, :, own64], g.gu_in.at[k - 1], dev(x, z_d, y, c))


    lk.got(gb_y, g.gb_y)
    total = g.gb[:, y].astype(f32) + g.gb_y[...].astype(f32)
    g.gb_z[...] = total.astype(bf16).reshape(4, 4, 16, 768)
    gb_s = {}
    for k in (2, 1, 3):
        gb_s[k] = lk.put(g.gb_z.at[:, zo(k)], g.gb_in.at[k - 1], dev(x, zo(k), y, c))
    channel_got(gm_cs, g.gm_land)
    unpack(g.gm_land, put_grad)

    def conv_back(h, _):
        parts = [conv_rows(h, k) for k in range(16)]
        own = g.vr32[pl.ds(aligned(64 * h, 64), 64), :].T.astype(bf16)
        out = g.skip_b[pl.ds(16 * x + h, 1), :] * parts[0]
        lhs = []
        for kk in range(8):
            lhs.append(jnp.concatenate([parts[2 * kk], parts[2 * kk + 1]], axis=1).astype(bf16))
            out = out + dot(lhs[kk], g.toep[h, 2 * kk : 2 * kk + 2].reshape(256, 128))
        g.o32[pl.ds(aligned(64 * h, 64), 64), :] = out
        after = jnp.zeros((128, 128), f32)
        for kk in range(7, -1, -1):
            pair = dot(own, lhs[kk])
            for half in (1, 0):
                turned = pltpu.roll(
                    pair[:, 128 * half : 128 * half + 128], 0, 1, stride=1, stride_axis=0
                )
                lag = jnp.where(jj >= ii, turned, after)
                after = turned
                at = pl.ds(aligned((16 * (2 * kk + half) + h) * 8, 8), 8)
                g.gk8[at, :] = jnp.sum(lag.reshape(16, 8, 128), axis=0)
        return 0

    lax.fori_loop(0, 8, conv_back, 0, unroll=2)
    up_grad(2)
    lax.fori_loop(8, 16, conv_back, 0, unroll=2)
    pack(g.gv_out, True)
    gv_s = channel_back(g.gv_out, g.g_val)
    g.g_val[pl.ds(aligned(16 * n, 16), 16), :] = g.gv_out[n]

    down_send(1)
    down_sum(0)
    up_sum(2)

    tall = g.gk8[pl.ds(0, 256, stride=8), :]
    for s_ in range(1, 8):
        tall = tall + g.gk8[pl.ds(s_, 256, stride=8), :]
    for half in range(2):
        hi_, lo_ = split(tall[128 * half : 128 * half + 128, :])
        g.state[128 * half : 128 * half + 128, :] = (
            dot(hi_, g.near_t_hi[...]) + dot(lo_, g.near_t_hi[...]) + dot(hi_, g.near_t_lo[...])
        )
    g.skip_sum[...] = tall[0:16, :]

    def far_back(p, carry):
        gc, gs = carry
        hr = g.far_re[pl.ds(p, 1), :]
        hi = g.far_im[pl.ds(p, 1), :]
        rows = pl.ds(aligned(16 * p, 16), 16)
        ur = g.state[rows, 0:512]
        ui = g.state[rows, 512:1024]
        return gc + hr * ur - hi * ui, gs + hr * ui + hi * ur

    blank = jnp.zeros((16, 512), f32)
    gc, gs = lax.fori_loop(0, 16, far_back, (blank, blank))
    g.gcoef[0] = gc
    g.gcoef[1] = gs
    gcoef_s = lk.put(g.gcoef.at[1 - x], g.gcoef_in, xn)
    skip_s = lk.put(g.skip_sum, g.skip_in, xn)

    channel_back_got(gv_s, g.g_val)
    for tb in range(8):
        at = slice(128 * tb, 128 * tb + 128)
        back = dot(g.g_val[:, at], flip)
        g.gvp_t[at, :] = (back * g.val_slope[:, at]).astype(bf16).T
    part = dot(g.normed_t[...], g.gvp_t[...]).astype(bf16)
    g.gv[...] = part.reshape(4, 2, 128, 128)
    gv_y = lk.put(g.gv.at[:, :, other], g.gv_y, ynb)

    def normed_part(xm, cm):
        rows = pl.ds(aligned(256 * (2 * xm + cm), 256), 256)
        return dot_nt(g.g_up[rows, :], up2d[...]) + dot_nt(g.gvp_t[rows, :], g.w_val[...])

    gn_s, gn_own = group_sum(
        normed_part, spare.at[1], g.gn_in, g.tok_all.at[r_sib].reshape(256, 1024), g.gn_xin
    )
    up_grad(1)
    up_grad(3)
    up_grad(0)
    down_sum(1)

    lk.got(gv_y, g.gv_y)
    g.gv_z[...] = (g.gv[:, :, own64, :].astype(f32) + g.gv_y[...].astype(f32)).astype(bf16)
    gv_zs = {}
    for k in (2, 1, 3):
        gv_zs[k] = lk.put(g.gv_z.at[zo(k)], g.gv_in.at[k - 1], dev(x, zo(k), y, c))

    up_sum(1)

    lk.got(gn_s, g.gn_xin)
    up_sum(3)
    g.state[...] = gn_own()

    def norm_back(i, carry):
        dg, ds = carry
        s_, part = i // 2, pl.ds(aligned(64 * lax.rem(i, 2), 64), 64)
        rows = g.tokens[s_, part, :].astype(f32)
        mean = jnp.mean(rows, axis=-1, keepdims=True)
        cen = rows - mean
        var = jnp.mean(cen * cen, axis=-1, keepdims=True)
        inv = lax.rsqrt(var + 1e-5)
        zn = cen * inv
        gn = g.state[pl.ds(aligned(64 * i, 64), 64), :]
        gg = gn * g.norm_rows[0:1, :]
        m1 = jnp.mean(gg, axis=-1, keepdims=True)
        m2 = jnp.mean(gg * zn, axis=-1, keepdims=True)
        g.g_tokens[s_, part, :] = g.cot[s_, part, :].astype(f32) + inv * (gg - m1 - zn * m2)
        dg = dg + jnp.sum(gn * zn, axis=0, keepdims=True)
        ds = ds + jnp.sum(gn, axis=0, keepdims=True)
        return dg, ds

    blank = jnp.zeros((1, 1024), f32)
    dg, ds = lax.fori_loop(0, 4, norm_back, (blank, blank))
    for zd in range(4):
        g.ng[zd, 0:1, :] = dg[:, 128 * zd : 128 * zd + 128]
        g.ng[zd, 1:2, :] = dg[:, 512 + 128 * zd : 640 + 128 * zd]
        g.ng[zd, 2:3, :] = ds[:, 128 * zd : 128 * zd + 128]
        g.ng[zd, 3:4, :] = ds[:, 512 + 128 * zd : 640 + 128 * zd]
        g.ng[zd, 4:8, :] = jnp.zeros((4, 128), f32)
    ng_s = []
    for k in range(1, 8):
        to = lax.rem(n + k, 8)
        ng_s.append(lk.put(g.ng.at[to // 2], g.ng_in.at[k - 1], (x, 2 * to + c)))

    lk.got(br_s, g.br_xin)
    out = br_own().reshape(2, 128, 1024) + g.tokens[...].astype(f32)
    g.result[...] = out.astype(bf16)

    up_sum(0)

    for k in (2, 1, 3):
        lk.got(gu_s[k], g.gu_in.at[k - 1])
    total = g.gu[z, :, own64, :].astype(f32)
    for k in range(3):
        total = total + g.gu_in[k].astype(f32)
    g.gu_f[...] = total.reshape(2, 2, 32, 768).astype(bf16)
    fin_u = [lk.put(g.gu_f.at[xm, cm], g.fu_in.at[r], to) for to, xm, cm, rm in members]
    for k in (2, 1, 3):
        lk.got(gb_s[k], g.gb_in.at[k - 1])
    total = g.gb_z[:, z].astype(f32)
    for k in range(3):
        total = total + g.gb_in[k].astype(f32)
    g.gb_f[...] = total.astype(bf16)
    fin_b = [lk.put(g.gb_f.at[2 * cm + xm], g.fb_in.at[r], to) for to, xm, cm, rm in members]
    for k in (2, 1, 3):
        lk.got(gv_zs[k], g.gv_in.at[k - 1])
    total = g.gv_z[z].astype(f32)
    for k in range(3):
        total = total + g.gv_in[k].astype(f32)
    g.gv_f[...] = total.reshape(2, 2, 32, 128).astype(bf16)
    fin_v = [lk.put(g.gv_f.at[xm, cm], g.fv_in.at[r], to) for to, xm, cm, rm in members]
    g.fu_in[r] = g.gu_f[x, c]
    g.fb_in[r] = g.gb_f[2 * c + x]
    g.fv_in[r] = g.gv_f[x, c]

    for zs in range(4):
        region = g.gd_in.at[zs]
        pltpu.make_async_copy(region, region, lk.recv_sems.at[gd_r + zs]).wait()
    total = g.gd_in[0].astype(f32)
    for zs in range(1, 4):
        total = total + g.gd_in[zs].astype(f32)
    g.o_down[...] = total

    mine = pl.ds(aligned(16 * x, 16), 16)
    theirs = pl.ds(aligned(16 * (1 - x), 16), 16)
    lk.got(gcoef_s, g.gcoef_in)
    g.o_coef[mine, :] = g.gcoef[x]
    g.o_coef[theirs, :] = g.gcoef_in[...]
    lk.got(skip_s, g.skip_in)
    g.o_skip[mine, :] = g.skip_sum[...]
    g.o_skip[theirs, :] = g.skip_in[...]

    total = g.ng[z]
    for k in range(1, 8):
        lk.got(ng_s[k - 1], g.ng_in.at[k - 1])
        total = total + g.ng_in[k - 1]
    g.ng_f[...] = total
    ng_t = [lk.put(g.ng_f, g.ng_fin.at[i], to) for i, (to, xm, cm, rm) in enumerate(members)]

    for i, (to, xm, cm, rm) in enumerate(members):
        lk.got(fin_u[i], g.fu_in.at[rm])
        lk.got(fin_b[i], g.fb_in.at[rm])
        lk.got(fin_v[i], g.fv_in.at[rm])
    wide = jnp.concatenate([g.fv_in[rr] for rr in range(4)], axis=1)
    g.o_value[...] = dot_nt(wide, g.perm[...])
    for i in range(3):
        lk.got(ng_t[i], g.ng_fin.at[i])
        total = total + g.ng_fin[i]
    total = jnp.where(x == 0, total, pltpu.roll(total, 7, 0))
    g.o_norm[...] = pltpu.roll(total, 128 - (64 * y + 32 * c), 1)
    lk.finish()
    assert lk.count <= N_SEMS


def start_of(copy):
    copy.start()
    return copy


def fast_body(
    tokens, norm_gain, norm_shift, w_up, w_value, w_back, w_down, mode_coef, skip_gain, cotangent
):
    states = 512
    length = tokens.shape[1] * lax.axis_size("tok")
    far_re, far_im, near_hi, near_lo, near_t_hi, near_t_lo = mode_tables(states, length)
    ins = dict(
        tokens=tokens,
        norm_gain=norm_gain.reshape(1, -1),
        norm_shift=norm_shift.reshape(1, -1),
        w_up=w_up,
        w_value=w_value,
        w_back=w_back,
        w_down=w_down,
        mode_coef=mode_coef,
        skip=skip_gain.reshape(1, -1),
        cot=cotangent,
        far_re=far_re,
        far_im=far_im,
        near_hi=near_hi,
        near_lo=near_lo,
        near_t_hi=near_t_hi,
        near_t_lo=near_t_lo,
    )
    outs = dict(
        result=((2, 128, 1024), bf16),
        g_tokens=((2, 128, 1024), f32),
        o_norm=((8, 128), f32),
        fu_in=((4, 32, 768), bf16),
        o_value=((32, 512), f32),
        fb_in=((4, 16, 768), bf16),
        o_down=((96, 1024), f32),
        o_coef=((32, 512), f32),
        o_skip=((32, 128), f32),
    )
    scratch = dict(
        perm=((512, 512), bf16),
        pk_send=((4, 48, 128), bf16),
        pk=((2, 8, 2, 48, 128), bf16),
        coef=((2, 16, 512), bf16),
        w_up_all=((2, 8, 2, 32, 768), bf16),
        w_back_all=((2, 2, 2, 4, 16, 768), bf16),
        w_down_all=((2, 2, 2, 96, 1024), bf16),
        tok_all=((4, 2, 128, 1024), bf16),
        cot_all=((4, 2, 128, 1024), bf16),
        state=((256, 1024), f32),
        kern=((256, 128), f32),
        toep=((16, 16, 128, 128), bf16),
        norm_rows=((8, 1024), f32),
        w_val=((1024, 128), bf16),
        w_val_t=((128, 1024), bf16),
        normed=((1024, 1024), bf16),
        normed_t=((1024, 1024), bf16),
        val_slope=((128, 1024), f32),
        val=((128, 1024), bf16),
        val_in=((8, 16, 1024), bf16),
        v32=((2048, 128), f32),
        vr32=((1024, 128), f32),
        o32=((1024, 128), f32),
        skip_b=((32, 128), f32),
        mix_out=((8, 16, 1024), bf16),
        mix=((4, 128, 1024), bf16),
        act=((1024, 768), f32),
        slope=((1024, 768), f32),
        g_gate=((1024, 768), bf16),
        gm_send=((2, 128, 1024), bf16),
        gm_in=((2, 128, 1024), bf16),
        gm_x=((128, 1024), bf16),
        gm_xin=((128, 1024), bf16),
        gm=((128, 1024), bf16),
        gm_land=((8, 16, 1024), bf16),
        mix_tok=((1024, 512), bf16),
        hidden=((1024, 768), bf16),
        hidden_t=((768, 1024), bf16),
        g_up=((1024, 768), bf16),
        gd=((2, 2, 192, 1024), bf16),
        gd_y=((2, 192, 1024), bf16),
        gd_in=((4, 96, 1024), bf16),
        gu=((4, 2, 128, 768), bf16),
        gu_y=((4, 2, 64, 768), bf16),
        gu_in=((3, 2, 64, 768), bf16),
        fv_in=((4, 32, 128), bf16),
        gu_f=((2, 2, 32, 768), bf16),
        gb=((2, 2, 128, 768), bf16),
        gb_y=((2, 128, 768), bf16),
        gb_z=((4, 4, 16, 768), bf16),
        gb_in=((3, 4, 16, 768), bf16),
        gb_f=((4, 16, 768), bf16),
        gv=((4, 2, 128, 128), bf16),
        gv_y=((4, 2, 64, 128), bf16),
        gv_z=((4, 2, 64, 128), bf16),
        gv_in=((3, 2, 64, 128), bf16),
        gv_f=((2, 2, 32, 128), bf16),
        gk8=((2048, 128), f32),
        gm_own=((128, 1024), f32),
        skip_sum=((16, 128), f32),
        skip_in=((16, 128), f32),
        gcoef=((2, 16, 512), f32),
        gcoef_in=((16, 512), f32),
        gv_out=((8, 16, 1024), bf16),
        g_val=((128, 1024), bf16),
        gvp_t=((1024, 128), bf16),
        br_in=((2, 256, 1024), bf16),
        br_xin=((256, 1024), bf16),
        gn_in=((2, 256, 1024), bf16),
        gn_xin=((256, 1024), bf16),
        ng=((4, 8, 128), f32),
        ng_in=((7, 8, 128), f32),
        ng_f=((8, 128), f32),
        ng_fin=((3, 8, 128), f32),
    )
    names = list(ins) + list(outs) + list(scratch) + ["ssem", "rsem"]
    vmem = pl.BlockSpec(memory_space=pltpu.VMEM)
    got = pl.pallas_call(
        functools.partial(layer_kernel, names),
        out_shape=[jax.ShapeDtypeStruct(s, t) for s, t in outs.values()],
        in_specs=[vmem] * len(ins),
        out_specs=[vmem] * len(outs),
        scratch_shapes=[pltpu.VMEM(s, t) for s, t in scratch.values()]
        + [pltpu.SemaphoreType.DMA((N_SEMS,)), pltpu.SemaphoreType.DMA((N_SEMS,))],
        compiler_params=pltpu.CompilerParams(
            collective_id=0, has_side_effects=True, vmem_limit_bytes=64 << 20
        ),
    )(*ins.values())
    up_rows, back_rows = w_up.shape[0], w_back.shape[0]
    final = [
        jax.ShapeDtypeStruct((2, 128, 1024), bf16),
        jax.ShapeDtypeStruct((2, 128, 1024), f32),
        jax.ShapeDtypeStruct((1, 32), f32),
        jax.ShapeDtypeStruct((1, 32), f32),
        jax.ShapeDtypeStruct((up_rows, 3072), f32),
        jax.ShapeDtypeStruct((up_rows, 512), f32),
        jax.ShapeDtypeStruct((back_rows, 3072), f32),
        jax.ShapeDtypeStruct((96, 1024), f32),
        jax.ShapeDtypeStruct((32, 512), f32),
        jax.ShapeDtypeStruct((1, 32), f32),
    ]
    out = pl.pallas_call(
        last_kernel,
        out_shape=final,
        in_specs=[vmem] * len(outs),
        out_specs=[vmem] * len(final),
        compiler_params=pltpu.CompilerParams(vmem_limit_bytes=63 << 20),
    )(*got)
    return tuple(v.reshape(-1) if v.shape[0] == 1 else v for v in out)


def last_kernel(*refs):
    (result, g_tokens, norm, up, value, back, down, coef, skip), out = refs[:9], refs[9:]
    out[0][...] = result[...]
    out[1][...] = g_tokens[...]
    out[2][...] = norm[0:1, 0:32]
    out[3][...] = norm[2:3, 0:32]
    for rr in range(4):
        out[4][:, 768 * rr : 768 * rr + 768] = up[rr].astype(f32)
        out[6][:, 768 * rr : 768 * rr + 768] = back[rr].astype(f32)
    out[5][...] = value[...]
    out[7][...] = down[...]
    out[8][...] = coef[...]
    same = lax.broadcasted_iota(jnp.int32, (32, 32), 0) == lax.broadcasted_iota(
        jnp.int32, (32, 32), 1
    )
    column = jnp.broadcast_to(skip[:, 127:128], (32, 32))
    out[9][...] = jnp.sum(jnp.where(same, column, 0.0), axis=0, keepdims=True)


def run(tokens, *rest):
    sizes = (lax.axis_size("item"), lax.axis_size("tok"), tokens.shape)
    if sizes == (2, 16, (2, 128, 1024)):
        return fast_body(tokens, *rest)
    return body(tokens, *rest)


def solution(mesh):
    in_specs = (
        P("item", "tok", None),
        P(("item", "tok")),
        P(("item", "tok")),
        P(("item", "tok"), None),
        P(("item", "tok"), None),
        P(("item", "tok"), None),
        P(("item", "tok"), None),
        P("tok", "item"),
        P("tok"),
        P("item", "tok", None),
    )
    out_specs = (
        P("item", "tok", None),
        P("item", "tok", None),
        P(("item", "tok")),
        P(("item", "tok")),
        P(("item", "tok"), None),
        P(("item", "tok"), None),
        P(("item", "tok"), None),
        P(("item", "tok"), None),
        P("tok", "item"),
        P("tok"),
    )
    return jax.shard_map(run, mesh=mesh, in_specs=in_specs, out_specs=out_specs, check_vma=False)
```

```python
import functools
import math
import types

import jax
import jax.numpy as jnp
import ml_dtypes
import numpy as np
from jax import lax
from jax.experimental import pallas as pl
from jax.experimental.pallas import tpu as pltpu
from jax.sharding import PartitionSpec as P

highest = lax.Precision.HIGHEST


def basis_block(start_index, block_width, length, states):
    places = start_index + jnp.arange(block_width, dtype=jnp.int32)
    mode_ids = jnp.arange(states, dtype=jnp.int32)
    fraction = (mode_ids * 41 % states).astype(jnp.float32) / states
    mode_rates = jnp.exp(jnp.log(1.0 / 32.0) + fraction * jnp.log(32.0 / (4.0 * length)))
    decays = jnp.exp(-mode_rates[:, None] * places[None, :].astype(jnp.float32))
    phase_turns = (mode_ids[:, None] * places[None, :] % (2 * states)).astype(jnp.float32) * (
        jnp.pi / states
    )
    return jnp.concatenate([decays * jnp.cos(phase_turns), decays * jnp.sin(phase_turns)], axis=0)


def make_kernel(coef_full, length):
    states = coef_full.shape[1] // 2
    block_width = math.gcd(length, 2048)
    block_count = length // block_width

    def one_block(block_index):
        table = basis_block(block_index * block_width, block_width, length, states)
        return jnp.dot(coef_full, table, precision=highest)

    pieces = lax.map(one_block, jnp.arange(block_count, dtype=jnp.int32))
    return jnp.transpose(pieces, (1, 0, 2)).reshape(coef_full.shape[0], length)


def coef_gradient(grad_kernel, states):
    channels, length = grad_kernel.shape
    block_width = math.gcd(length, 2048)
    block_count = length // block_width
    slabs = grad_kernel.reshape(channels, block_count, block_width)

    def add_block(running, block_index):
        slab_part = lax.dynamic_index_in_dim(slabs, block_index, 1, keepdims=False)
        table = basis_block(block_index * block_width, block_width, length, states)
        return (running + jnp.dot(slab_part, table.T, precision=highest), None)

    start_total = jnp.zeros((channels, 2 * states), jnp.float32)
    summed, unused = lax.scan(add_block, start_total, jnp.arange(block_count, dtype=jnp.int32))
    return summed


def unit_tables(row_count, column_count, period):
    row_ids = jnp.arange(row_count, dtype=jnp.int32)[:, None]
    column_ids = jnp.arange(column_count, dtype=jnp.int32)[None, :]
    phase_turns = (row_ids * column_ids % period).astype(jnp.float32) * (2.0 * jnp.pi / period)
    return (jnp.cos(phase_turns), jnp.sin(phase_turns))


def right_product(left_part, table):
    return jnp.einsum("...kq,qm->...km", left_part, table, precision=highest)


def spectrum(signal):
    length = signal.shape[-1]
    padded_size = 2 * length
    outer_size = padded_size // 128
    half_size = outer_size // 2
    folded = signal.reshape(signal.shape[:-1] + (half_size, 128))
    cos_outer, sin_outer = unit_tables(outer_size, half_size, outer_size)
    section_real = jnp.einsum("kp,...pq->...kq", cos_outer, folded, precision=highest)
    section_imag = -jnp.einsum("kp,...pq->...kq", sin_outer, folded, precision=highest)
    twist_cos, twist_sin = unit_tables(outer_size, 128, padded_size)
    turned_real = section_real * twist_cos + section_imag * twist_sin
    turned_imag = section_imag * twist_cos - section_real * twist_sin
    cos_inner, sin_inner = unit_tables(128, 128, 128)
    out_real = right_product(turned_real, cos_inner) + right_product(turned_imag, sin_inner)
    out_imag = right_product(turned_imag, cos_inner) - right_product(turned_real, sin_inner)
    return (out_real, out_imag)


def inverse(spec_real, spec_imag):
    outer_size = spec_real.shape[-2]
    padded_size = outer_size * 128
    half_size = outer_size // 2
    cos_inner, sin_inner = unit_tables(128, 128, 128)
    back_real = right_product(spec_real, cos_inner) - right_product(spec_imag, sin_inner)
    back_imag = right_product(spec_real, sin_inner) + right_product(spec_imag, cos_inner)
    twist_cos, twist_sin = unit_tables(outer_size, 128, padded_size)
    turned_real = back_real * twist_cos - back_imag * twist_sin
    turned_imag = back_real * twist_sin + back_imag * twist_cos
    cos_outer, sin_outer = unit_tables(half_size, outer_size, outer_size)
    signal = jnp.einsum("pk,...kq->...pq", cos_outer, turned_real, precision=highest)
    signal = signal - jnp.einsum("pk,...kq->...pq", sin_outer, turned_imag, precision=highest)
    return signal.reshape(signal.shape[:-2] + (half_size * 128,)) / padded_size


def layer_norm(token_rows, gain_row, shift_row):
    row_mean = jnp.mean(token_rows, axis=-1, keepdims=True)
    centered = token_rows - row_mean
    variance = jnp.mean(centered * centered, axis=-1, keepdims=True)
    return centered * lax.rsqrt(variance + 1e-05) * gain_row + shift_row


def body(
    tokens, norm_gain, norm_shift, w_up, w_value, w_back, w_down, mode_coef, skip_gain, cotangent
):
    gain_full, shift_full, up_full, value_full = (
        lax.all_gather(norm_gain, ("item", "tok"), axis=0, tiled=True),
        lax.all_gather(norm_shift, ("item", "tok"), axis=0, tiled=True),
        lax.all_gather(w_up, ("item", "tok"), axis=0, tiled=True),
        lax.all_gather(w_value, ("item", "tok"), axis=0, tiled=True),
    )
    back_full, down_full = (
        lax.all_gather(w_back, ("item", "tok"), axis=0, tiled=True),
        lax.all_gather(w_down, ("item", "tok"), axis=0, tiled=True),
    )
    coef_full = lax.all_gather(mode_coef, "item", axis=1, tiled=True)
    token_rows = tokens.astype(jnp.float32)
    gain_float = gain_full.astype(jnp.float32)
    shift_float = shift_full.astype(jnp.float32)
    normed = layer_norm(token_rows, gain_float, shift_float).astype(jnp.bfloat16)
    up_pre = jnp.einsum("std,df->stf", normed, up_full, preferred_element_type=jnp.float32)
    value_pre = jnp.einsum("std,dh->sht", normed, value_full, preferred_element_type=jnp.float32)
    value = jax.nn.gelu(value_pre).astype(jnp.bfloat16)
    channel_values = lax.all_to_all(value, "tok", split_axis=1, concat_axis=2, tiled=True)
    length = channel_values.shape[-1]
    kernel = make_kernel(coef_full.astype(jnp.float32), length)
    signal = channel_values.astype(jnp.float32)
    skip_column = skip_gain.astype(jnp.float32)[:, None]
    value_real, value_imag = spectrum(signal)
    kernel_real, kernel_imag = spectrum(kernel)
    conv_out = inverse(
        value_real * kernel_real - value_imag * kernel_imag,
        value_real * kernel_imag + value_imag * kernel_real,
    )
    mixed_channels = (conv_out + skip_column * signal).astype(jnp.bfloat16)
    mixed = lax.all_to_all(mixed_channels, "tok", split_axis=2, concat_axis=1, tiled=True)
    gate = jnp.einsum("sht,hf->stf", mixed, back_full, preferred_element_type=jnp.float32)
    up_act = jax.nn.gelu(up_pre)
    hidden = (up_act * gate).astype(jnp.bfloat16)
    branch = jnp.einsum("stf,fd->std", hidden, down_full, preferred_element_type=jnp.float32)
    result = (token_rows + branch).astype(jnp.bfloat16)
    grad_w_down = jnp.einsum("stf,std->fd", hidden, cotangent, preferred_element_type=jnp.float32)
    grad_hidden = jnp.einsum(
        "std,fd->stf", cotangent, down_full, preferred_element_type=jnp.float32
    )
    grad_gate = (grad_hidden * up_act).astype(jnp.bfloat16)
    grad_up_act = grad_hidden * gate
    grad_w_back = jnp.einsum("sht,stf->hf", mixed, grad_gate, preferred_element_type=jnp.float32)
    grad_mixed = jnp.einsum(
        "stf,hf->sht", grad_gate, back_full, preferred_element_type=jnp.float32
    ).astype(jnp.bfloat16)
    grad_channels = lax.all_to_all(grad_mixed, "tok", split_axis=1, concat_axis=2, tiled=True)
    grad_signal = grad_channels.astype(jnp.float32)
    grad_real, grad_imag = spectrum(grad_signal)
    grad_value_channels = inverse(
        kernel_real * grad_real + kernel_imag * grad_imag,
        kernel_real * grad_imag - kernel_imag * grad_real,
    )
    grad_value_channels = (grad_value_channels + skip_column * grad_signal).astype(jnp.bfloat16)
    grad_kernel = inverse(
        jnp.sum(grad_real * value_real + grad_imag * value_imag, axis=0),
        jnp.sum(grad_imag * value_real - grad_real * value_imag, axis=0),
    )
    grad_skip_part = jnp.sum(grad_signal * signal, axis=(0, 2))
    grad_coef_part = coef_gradient(grad_kernel, coef_full.shape[1] // 2)
    grad_mode_coef = lax.psum_scatter(grad_coef_part, "item", scatter_dimension=1, tiled=True)
    grad_skip_gain = lax.psum(grad_skip_part, "item")
    grad_value = lax.all_to_all(grad_value_channels, "tok", split_axis=2, concat_axis=1, tiled=True)
    gelu_value_back = jax.vjp(jax.nn.gelu, value_pre)[1]
    grad_value_pre = gelu_value_back(grad_value.astype(jnp.float32))[0].astype(jnp.bfloat16)
    gelu_up_back = jax.vjp(jax.nn.gelu, up_pre)[1]
    grad_up_pre = gelu_up_back(grad_up_act)[0].astype(jnp.bfloat16)
    grad_w_up = jnp.einsum("std,stf->df", normed, grad_up_pre, preferred_element_type=jnp.float32)
    grad_w_value = jnp.einsum(
        "std,sht->dh", normed, grad_value_pre, preferred_element_type=jnp.float32
    )
    grad_normed = jnp.einsum(
        "stf,df->std", grad_up_pre, up_full, preferred_element_type=jnp.float32
    )
    grad_normed = grad_normed + jnp.einsum(
        "sht,dh->std", grad_value_pre, value_full, preferred_element_type=jnp.float32
    )
    norm_back = jax.vjp(layer_norm, token_rows, gain_float, shift_float)[1]
    grad_rows, grad_gain_part, grad_shift_part = norm_back(grad_normed)
    grad_tokens = cotangent.astype(jnp.float32) + grad_rows
    owners = lax.axis_size("item") * lax.axis_size("tok")
    norm_flat = jnp.concatenate(
        [grad_gain_part.reshape(owners, -1), grad_shift_part.reshape(owners, -1)], axis=1
    )
    up_flat = grad_w_up.reshape(owners, -1)
    value_flat = grad_w_value.reshape(owners, -1)
    back_flat = grad_w_back.reshape(owners, -1)
    down_flat = grad_w_down.reshape(owners, -1)
    summed = (
        lax.psum_scatter(norm_flat, ("item", "tok"), scatter_dimension=0, tiled=True),
        lax.psum_scatter(up_flat, ("item", "tok"), scatter_dimension=0, tiled=True),
        lax.psum_scatter(value_flat, ("item", "tok"), scatter_dimension=0, tiled=True),
        lax.psum_scatter(back_flat, ("item", "tok"), scatter_dimension=0, tiled=True),
        lax.psum_scatter(down_flat, ("item", "tok"), scatter_dimension=0, tiled=True),
    )
    gain_count = norm_gain.shape[0]
    norm_row = summed[0].reshape(-1)
    grad_norm_gain = norm_row[:gain_count]
    grad_norm_shift = norm_row[gain_count:]
    grad_up_out = summed[1].reshape(w_up.shape)
    grad_value_out = summed[2].reshape(w_value.shape)
    grad_back_out = summed[3].reshape(w_back.shape)
    grad_down_out = summed[4].reshape(w_down.shape)
    return (
        result,
        grad_tokens,
        grad_norm_gain,
        grad_norm_shift,
        grad_up_out,
        grad_value_out,
        grad_back_out,
        grad_down_out,
        grad_mode_coef,
        grad_skip_gain,
    )


MESH_ID = pl.DeviceIdType.MESH
bf16, f32 = jnp.bfloat16, jnp.float32
NT = (((1,), (1,)), ((), ()))
GC = math.sqrt(2.0 / math.pi)


def dot(a, b):
    return jnp.dot(a, b, preferred_element_type=f32)


def dot_nt(a, b):
    return lax.dot_general(a, b, NT, preferred_element_type=f32)


def gelu_parts(v):
    t = jnp.tanh(GC * (v + 0.044715 * v * v * v))
    half = 0.5 * (1.0 + t)
    slope = half + 0.5 * v * (1.0 - t * t) * (GC * (1.0 + 3 * 0.044715 * v * v))
    return v * half, slope


def split(v):
    high = v.astype(bf16)
    return high, (v - high.astype(f32)).astype(bf16)


def mode_tables(states, length):
    n = np.arange(states)
    rates = np.exp(np.log(1.0 / 32.0) + (n * 41 % states) / states * np.log(32.0 / (4.0 * length)))

    def table(places):
        decay = np.exp(-rates[:, None] * places[None, :])
        turn = (n[:, None] * places[None, :] % (2 * states)) * (np.pi / states)
        return decay * np.cos(turn), decay * np.sin(turn)

    far_re, far_im = table(np.arange(0, length, 128))
    near = np.concatenate(table(np.arange(128)), axis=0).astype(np.float32)
    high = near.astype(ml_dtypes.bfloat16)
    low = (near - high.astype(np.float32)).astype(ml_dtypes.bfloat16)
    return (
        far_re.T.astype(np.float32).copy(),
        far_im.T.astype(np.float32).copy(),
        high,
        low,
        high.T[::-1].copy(),
        low.T[::-1].copy(),
    )


class Links:
    def __init__(self, send_sems, recv_sems, place):
        self.send_sems, self.recv_sems, self.place = send_sems, recv_sems, place
        self.count = 0
        self.pending = []

    def take(self, n=1):
        first = self.count
        self.count += n
        return first

    def make(self, src, dst, ssem, rsem, to):
        return pltpu.make_async_remote_copy(
            src_ref=src,
            dst_ref=dst,
            send_sem=self.send_sems.at[ssem],
            recv_sem=self.recv_sems.at[rsem],
            device_id=to,
            device_id_type=MESH_ID,
        )

    def put(self, src, dst, to):
        slot = self.take()
        copy = self.make(src, dst, slot, slot, to)
        copy.start()
        self.pending.append((copy, None))
        return slot

    def got(self, slot, region):
        self.make(region, region, slot, slot, self.place).wait_recv()

    def put_or_keep(self, src, dst, ssem, rsem, to, here):
        remote = self.make(src, dst, ssem, rsem, to)
        local = pltpu.make_async_copy(src, dst, self.recv_sems.at[rsem])
        away = jnp.logical_not(here)
        pl.when(here)(local.start)
        pl.when(away)(remote.start)
        self.pending.append((remote, away))

    def finish(self):
        for copy, away in self.pending:
            if away is None:
                copy.wait_send()
            else:
                pl.when(away)(copy.wait_send)


N_SEMS = 200


def channels_of(rr):
    ch = lax.broadcasted_iota(jnp.int32, (512, 128), 0)
    p = lax.broadcasted_iota(jnp.int32, (512, 128), 1)
    return (ch == 64 * (p // 16) + 32 * (rr % 2) + 16 * (rr // 2) + p % 16).astype(bf16)


def layer_kernel(names, *refs):
    r_ = dict(zip(names, refs))
    g = types.SimpleNamespace(**r_)
    x = lax.axis_index("item")
    tok = lax.axis_index("tok")
    z, y, c = tok // 4, (tok // 2) % 2, tok % 2
    n = tok // 2
    r = 2 * x + c

    def dev(x_, z_, y_, c_):
        return (x_, z_ * 4 + y_ * 2 + c_)

    def zo(k):
        return lax.rem(z + k, 4)

    def zb(k):
        return lax.rem(z + 4 - k, 4)

    def node(z_, y_):
        return 2 * z_ + y_

    sib, xn, diag = dev(x, z, y, 1 - c), dev(1 - x, z, y, c), dev(1 - x, z, y, 1 - c)
    r_sib, r_xn, r_diag = 2 * x + 1 - c, 2 * (1 - x) + c, 2 * (1 - x) + 1 - c
    members = ((sib, x, 1 - c, r_sib), (xn, 1 - x, c, r_xn), (diag, 1 - x, 1 - c, r_diag))
    ynb = dev(x, z, 1 - y, c)
    lk = Links(g.ssem, g.rsem, ynb)
    aligned = pl.multiple_of

    barrier = pltpu.get_barrier_semaphore()
    partners = [m[0] for m in members]
    for k in range(1, 4):
        partners += [dev(x, zo(k), y, c), dev(x, zo(k), 1 - y, c), dev(x, zo(k), y, 1 - c)]
    partners.append(ynb)
    for p in partners:
        pl.semaphore_signal(barrier, inc=1, device_id=p, device_id_type=MESH_ID)

    eye = lax.broadcasted_iota(jnp.int32, (32, 128), 0) == lax.broadcasted_iota(
        jnp.int32, (32, 128), 1
    )
    eye = eye.astype(bf16)
    row16 = lax.broadcasted_iota(jnp.int32, (16, 128), 0)
    gain_row = dot(g.norm_gain[...], eye)
    shift_row = dot(g.norm_shift[...], eye)
    norm_pack = jnp.where(
        row16 == 0,
        jnp.broadcast_to(gain_row, (16, 128)),
        jnp.where(row16 == 1, jnp.broadcast_to(shift_row, (16, 128)), 0.0),
    ).astype(bf16)
    for rr in range(4):
        pick = channels_of(rr)
        g.pk_send[rr, 0:32, :] = dot(g.w_value[...], pick).astype(bf16)
        g.pk_send[rr, 32:48, :] = norm_pack
    pl.semaphore_wait(barrier, len(partners))

    pk_s, up_s, back_s = [], [], []
    for to, xm, cm, rm in members:
        pk_s.append(lk.put(g.pk_send.at[rm], g.pk.at[x, n, c], to))
    coef_s = lk.put(g.mode_coef.at[pl.ds(aligned(16 * (1 - x), 16), 16), :], g.coef.at[x], xn)
    tok_x = lk.put(g.tokens, g.tok_all.at[r], xn)
    my_back = g.w_back_all.at[c, y, x, z]

    def cols(rm):
        return pl.ds(aligned(768 * rm, 128), 768)

    for to, xm, cm, rm in members:
        up_s.append(lk.put(g.w_up.at[:, cols(rm)], g.w_up_all.at[x, n, c], to))
    for to, xm, cm, rm in members:
        back_s.append(lk.put(g.w_back.at[:, cols(rm)], my_back, to))
    tok_sib = lk.put(g.tokens, g.tok_all.at[r], sib)
    cot_x = lk.put(g.cot, g.cot_all.at[r], xn)
    cot_sib = lk.put(g.cot, g.cot_all.at[r], sib)
    g.pk[x, n, c] = g.pk_send[r]
    g.w_up_all[x, n, c] = g.w_up[:, cols(r)]
    g.w_back_all[c, y, x, z] = g.w_back[:, cols(r)]
    g.cot_all[r] = g.cot[...]
    g.coef[x] = g.mode_coef[pl.ds(aligned(16 * x, 16), 16), :]

    def gather_start(region):
        slots = {}
        for k in (1, 2, 3):
            slots[k] = lk.put(region(z, y), region(z, y), dev(x, zo(k), y, c))
        slots[4] = lk.put(region(z, y), region(z, y), ynb)
        return slots

    def gather_pass(slots, region, k):
        lk.got(slots[k], region(zb(k), y))
        slots[4 + k] = lk.put(region(zb(k), y), region(zb(k), y), ynb)

    def gather_end(slots, region):
        for k in range(4):
            lk.got(slots[4 + k], region(zb(k), 1 - y))

    def pk_region(z_, y_):
        return g.pk.at[:, node(z_, y_)]

    def up_region(z_, y_):
        return g.w_up_all.at[:, node(z_, y_)]

    def back_region(z_, y_):
        return g.w_back_all.at[:, y_, :, z_]

    for i, (to, xm, cm, rm) in enumerate(members):
        lk.got(pk_s[i], g.pk.at[xm, n, cm])
    pk_g = gather_start(pk_region)

    def line(region, has):
        right, left, across = lk.take(3), lk.take(3), lk.take(4)
        passes = lk.take(3)

        def send(zs, ssem, rsem, to, when):
            copy = lk.make(region(zs, y), region(zs, y), ssem, rsem, to)
            pl.when(when)(copy.start)
            lk.pending.append((copy, when))

        def also(when, zs):
            return when if has is None else jnp.logical_and(when, has(zs))

        def step(k):
            for way, base in ((-1, right), (1, left)):
                if k == 0 and way == 1:
                    continue
                zs = z + way * k
                there = also(z >= k if way == -1 else z + k <= 3, zs)
                if k:
                    slot = base + k - 1
                    block = region(lax.rem(zs + 4, 4), y)
                    wait = lk.make(block, block, slot, slot, ynb)
                    pl.when(there)(wait.wait_recv)
                zs = lax.rem(zs + 4, 4)
                if k < 3 and (way == -1 or k == 0):
                    on = jnp.logical_and(there, z < 3)
                    send(zs, right + k, right + k, dev(x, zo(1), y, c), on)
                if k < 3 and (way == 1 or k == 0):
                    on = jnp.logical_and(there, z > 0)
                    send(zs, left + k, left + k, dev(x, zb(1), y, c), on)
                ssem = across + k if way == -1 else passes + k - 1
                send(zs, ssem, across + zs, ynb, there)

        def end():
            for zs in range(4):
                block = region(zs, 1 - y)
                wait = lk.make(block, block, across + zs, across + zs, ynb)
                if has is None:
                    wait.wait_recv()
                else:
                    pl.when(has(zs))(wait.wait_recv)

        return step, end

    def down_region(z_, y_):
        return g.w_down_all.at[lax.rem(z_, 2), y_]

    def down_has(z_):
        return (z_ + 4) // 2 == c + 2

    owner = z // 2
    dn_own = lk.take()
    dst = g.w_down_all.at[lax.rem(z, 2), y, c]
    dn_copy = lk.make(g.w_down, dst, dn_own, dn_own, sib)
    pl.when(owner != c)(dn_copy.start)
    lk.pending.append((dn_copy, owner != c))

    @pl.when(owner == c)
    def _():
        g.w_down_all[lax.rem(z, 2), y, c] = g.w_down[...]
        block = g.w_down_all.at[lax.rem(z, 2), y, 1 - c]
        lk.make(block, block, dn_own, dn_own, sib).wait_recv()

    down_step, down_end = line(down_region, down_has)
    up_step, up_end = line(up_region, None)
    back_step, back_end = line(back_region, None)
    down_step(0)

    lk.got(coef_s, g.coef.at[1 - x])
    cc = g.coef[0].astype(f32)
    sc = g.coef[1].astype(f32)

    def far(p, _):
        hr = g.far_re[pl.ds(p, 1), :]
        hi = g.far_im[pl.ds(p, 1), :]
        rows = pl.ds(aligned(16 * p, 16), 16)
        g.state[rows, 0:512] = cc * hr + sc * hi
        g.state[rows, 512:1024] = sc * hr - cc * hi
        return 0

    lax.fori_loop(0, 16, far, 0)
    for half in range(2):
        rows = slice(128 * half, 128 * half + 128)
        hi_, lo_ = split(g.state[rows, :])
        g.kern[rows, :] = (
            dot(hi_, g.near_hi[...]) + dot(lo_, g.near_hi[...]) + dot(hi_, g.near_lo[...])
        )
    for k in (1, 2, 3):
        gather_pass(pk_g, pk_region, k)
    ii = lax.broadcasted_iota(jnp.int32, (128, 128), 0)
    jj = lax.broadcasted_iota(jnp.int32, (128, 128), 1)
    flip = (ii + jj == 127).astype(bf16)

    def toeplitz(h, _):
        prev = jnp.zeros((128, 128), f32)
        for k in range(16):
            row = jnp.broadcast_to(g.kern[pl.ds(16 * k + h, 1), :], (128, 128))
            turned = pltpu.roll(row, 0, 1, stride=1, stride_axis=0)
            g.toep[h, k] = jnp.where(jj >= ii, turned, prev).astype(bf16)
            prev = turned
        return 0

    lax.fori_loop(0, 16, toeplitz, 0, unroll=2)
    down_step(1)

    gather_end(pk_g, pk_region)
    e_i = lax.broadcasted_iota(jnp.int32, (128, 1024), 0)
    e_j = lax.broadcasted_iota(jnp.int32, (128, 1024), 1)
    spread = jnp.logical_and(e_i < 32, lax.rem(e_j, 32) == e_i).astype(bf16)
    blk = lax.broadcasted_iota(jnp.int32, (16, 1024), 1) // 32
    acc = jnp.zeros((16, 1024), f32)
    for xm in range(2):
        for nm in range(8):
            for cm in range(2):
                rows = g.pk[xm, nm, cm, 32:48, :]
                acc = acc + jnp.where(
                    blk == 16 * xm + 2 * nm + cm, dot(rows, spread), 0.0
                )
    gain = acc[0:1, :]
    shift = acc[1:2, :]
    g.norm_rows[0:1, :] = gain
    g.norm_rows[1:2, :] = shift
    wv = g.pk[:, :, :, 0:32, :].reshape(1024, 128)
    g.w_val[...] = wv
    wvt = wv.T
    for t in range(8):
        at = 256 * (t % 4) + 128 * (t // 4)
        g.w_val_t[:, at : at + 128] = wvt[:, 128 * t : 128 * t + 128]

    def norm_block(read, q):
        def part(s_, _):
            rows = read(s_).astype(f32)
            mean = jnp.mean(rows, axis=-1, keepdims=True)
            cen = rows - mean
            var = jnp.mean(cen * cen, axis=-1, keepdims=True)
            out = (cen * lax.rsqrt(var + 1e-5) * g.norm_rows[0:1, :] + g.norm_rows[1:2, :]).astype(
                bf16
            )
            at = aligned(256 * q + 128 * s_, 128)
            g.normed[pl.ds(at, 128), :] = out
            for t in range(8):
                low = 256 * (t % 4) + 128 * (t // 4)
                g.normed_t[low : low + 128, pl.ds(at, 128)] = out[:, 128 * t : 128 * t + 128].T
            return 0

        lax.fori_loop(0, 2, part, 0)
        at = pl.ds(aligned(256 * q, 128), 256)
        pre = dot(g.w_val_t[...], g.normed_t[:, at])
        act, slope = gelu_parts(pre)
        g.val_slope[:, at] = slope
        g.val[:, at] = act.astype(bf16)

    norm_block(lambda s_: g.tokens[s_], r)
    lk.got(tok_sib, g.tok_all.at[r_sib])
    norm_block(lambda s_: g.tok_all[r_sib, s_], r_sib)
    lk.got(tok_x, g.tok_all.at[r_xn])
    tok_f = lk.put(g.tok_all.at[r_xn], g.tok_all.at[r_xn], sib)
    norm_block(lambda s_: g.tok_all[r_xn, s_], r_xn)
    lk.got(tok_f, g.tok_all.at[r_diag])
    norm_block(lambda s_: g.tok_all[r_diag, s_], r_diag)

    def channel_send(src, landing):
        slots = []
        for k in range(1, 8):
            to = lax.rem(n + k, 8)
            slots.append(
                lk.put(
                    src.at[pl.ds(aligned(16 * to, 16), 16), :],
                    landing.at[n],
                    (x, 2 * to + c),
                )
            )
        return slots

    def channel_got(slots, landing):
        for k in range(1, 8):
            lk.got(slots[k - 1], landing.at[lax.rem(n + 8 - k, 8)])

    def unpack(landing, put):
        def one(nm, _):
            for tb in range(8):
                s_, cm = 2 * (tb // 4) + tb % 2, (tb // 2) % 2
                put(s_, 2 * nm + cm, landing[nm, :, 128 * tb : 128 * tb + 128].astype(f32))
            return 0

        lax.fori_loop(0, 8, one, 0)

    def put_val(s_, i, tile):
        g.v32[pl.ds(32 * s_ + 16 + i, 16, stride=128), :] = tile
        g.vr32[pl.ds(16 * s_ + 15 - i, 16, stride=64), :] = tile

    def put_grad(s_, i, tile):
        g.v32[pl.ds(32 * s_ + 31 - i, 16, stride=128), :] = tile

    val_s = channel_send(g.val, g.val_in)
    g.val_in[n] = g.val[pl.ds(aligned(16 * n, 16), 16), :]
    down_step(2)
    for i, (to, xm, cm, rm) in enumerate(members):
        lk.got(up_s[i], g.w_up_all.at[xm, n, cm])
    up_step(0)
    down_step(3)

    zero = jnp.zeros((16, 128), f32)
    for i in range(64):
        g.v32[32 * i : 32 * i + 16, :] = zero
    diag_i = lax.broadcasted_iota(jnp.int32, (32, 32), 0) == lax.broadcasted_iota(
        jnp.int32, (32, 32), 1
    )
    skip_row = jnp.broadcast_to(g.skip[...].astype(f32), (32, 32))
    g.skip_b[...] = dot(jnp.where(diag_i, skip_row, 0.0).astype(bf16), jnp.ones((32, 128), bf16))

    channel_got(val_s, g.val_in)
    unpack(g.val_in, put_val)
    up_step(1)

    def conv_rows(h, k):
        rows = [g.v32[pl.ds(128 * h + 32 * s_ + 16 - k, 16), :] for s_ in range(4)]
        return jnp.concatenate(rows, axis=0)

    def conv(h, _):
        parts = [conv_rows(h, k) for k in range(16)]
        out = g.skip_b[pl.ds(16 * x + h, 1), :] * parts[0]
        for kk in range(8):
            lhs = jnp.concatenate([parts[2 * kk], parts[2 * kk + 1]], axis=1).astype(bf16)
            out = out + dot(lhs, g.toep[h, 2 * kk : 2 * kk + 2].reshape(256, 128))
        g.o32[pl.ds(aligned(64 * h, 64), 64), :] = out
        return 0

    def pack(out, back):
        def one(nm, _):
            for tb in range(8):
                s_, cm = 2 * (tb // 4) + tb % 2, (tb // 2) % 2
                i = 2 * nm + cm
                at = pl.ds(16 * s_ + (15 - i if back else i), 16, stride=64)
                out[nm, :, 128 * tb : 128 * tb + 128] = g.o32[at, :].astype(bf16)
            return 0

        lax.fori_loop(0, 8, one, 0)

    def channel_back(src, landing):
        slots = []
        for k in range(1, 8):
            to = lax.rem(n + k, 8)
            slots.append(
                lk.put(src.at[to], landing.at[pl.ds(aligned(16 * n, 16), 16), :], (x, 2 * to + c))
            )
        return slots

    def channel_back_got(slots, landing):
        for k in range(1, 8):
            at = aligned(16 * lax.rem(n + 8 - k, 8), 16)
            lk.got(slots[k - 1], landing.at[pl.ds(at, 16), :])

    lax.fori_loop(0, 16, conv, 0, unroll=2)
    pack(g.mix_out, False)
    mix_s = channel_back(g.mix_out, g.mix.at[r])
    g.mix[r, pl.ds(aligned(16 * n, 16), 16), :] = g.mix_out[n]

    up_step(2)
    for i, (to, xm, cm, rm) in enumerate(members):
        lk.got(back_s[i], g.w_back_all.at[cm, y, xm, z])
    back_step(0)
    lk.got(cot_x, g.cot_all.at[r_xn])
    cot_f = lk.put(g.cot_all.at[r_xn], g.cot_all.at[r_xn], sib)
    down_end()
    lk.got(cot_sib, g.cot_all.at[r_sib])
    lk.got(cot_f, g.cot_all.at[r_diag])
    down2d = g.w_down_all.reshape(768, 1024)
    cot2d = g.cot_all.reshape(1024, 1024)

    def hidden_tile(q, _):
        rows = pl.ds(aligned(256 * q, 256), 256)
        g.slope[rows, :] = dot_nt(cot2d[rows, :], down2d[...])
        return 0

    lax.fori_loop(0, 4, hidden_tile, 0)
    up_step(3)
    back_step(1)
    channel_back_got(mix_s, g.mix.at[r])
    mix_x = lk.put(g.mix.at[r], g.mix.at[r], xn)
    mix_sib = lk.put(g.mix.at[r], g.mix.at[r], sib)
    back_step(2)

    up_end()
    up2d = g.w_up_all.reshape(1024, 768)

    def up_tile(q, _):
        rows = pl.ds(aligned(256 * q, 256), 256)
        act, slope = gelu_parts(dot(g.normed[rows, :], up2d[...]))
        gh = g.slope[rows, :]
        g.act[rows, :] = act
        g.g_gate[rows, :] = (gh * act).astype(bf16)
        g.slope[rows, :] = gh * slope
        return 0

    back_step(3)
    lax.fori_loop(0, 4, up_tile, 0)
    lk.got(mix_x, g.mix.at[r_xn])
    mix_f = lk.put(g.mix.at[r_xn], g.mix.at[r_xn], sib)
    back_end()
    back2d = g.w_back_all.reshape(512, 768)

    def mixed_part(ranks, q):
        w = [back2d[pl.ds(aligned(128 * rr, 128), 128), :] for rr in ranks]
        w = w[0] if len(w) == 1 else jnp.concatenate(w, axis=0)
        return dot_nt(w, g.g_gate[pl.ds(aligned(512 * q, 512), 512), :])

    gm_s, gm_xs = [], []
    for q in range(2):
        at = slice(512 * q, 512 * q + 512)
        both = mixed_part((1 - c, 2 + 1 - c), q).astype(bf16)
        g.gm_send[:, :, at] = both.reshape(2, 128, 512)
        gm_s.append(lk.put(g.gm_send.at[:, :, at], g.gm_in.at[:, :, at], sib))
    lk.got(mix_sib, g.mix.at[r_sib])
    lk.got(mix_f, g.mix.at[r_diag])

    mix2d = g.mix.reshape(512, 1024)

    def back_tile(i, _):
        at = pl.ds(aligned(384 * i, 128), 384)
        part = dot(mix2d[...], g.g_gate[:, at]).astype(bf16)
        g.gb[:, :, :, at] = part.reshape(2, 2, 128, 384)
        return 0

    lax.fori_loop(0, 2, back_tile, 0)
    gb_y = lk.put(g.gb.at[:, 1 - y], g.gb_y, ynb)


    for q in range(2):
        at = slice(512 * q, 512 * q + 512)
        both = mixed_part((2 * (1 - x) + c, 2 * x + c), q)
        g.state[0:128, at] = both[128:256, :]
        lk.got(gm_s[q], g.gm_in.at[:, :, at])
        g.gm_x[:, at] = (both[0:128, :] + g.gm_in[1 - x, :, at].astype(f32)).astype(bf16)
        gm_xs.append(lk.put(g.gm_x.at[:, at], g.gm_xin.at[:, at], xn))


    def turn(i, _):
        rr, tb = i // 8, lax.rem(i, 8)
        rows = pl.ds(aligned(128 * tb, 128), 128)
        at = pl.ds(aligned(128 * rr, 128), 128)
        g.mix_tok[rows, at] = g.mix[rr, :, rows].T
        return 0

    lax.fori_loop(0, 32, turn, 0, unroll=4)

    def gate_tile(q, _):
        rows = pl.ds(aligned(256 * q, 256), 256)
        gate = dot(g.mix_tok[rows, :], back2d[...])
        hidden = (g.act[rows, :] * gate).astype(bf16)
        g.hidden[rows, :] = hidden
        g.hidden_t[:, rows] = hidden.T
        g.g_up[rows, :] = (g.slope[rows, :] * gate).astype(bf16)
        return 0

    lax.fori_loop(0, 4, gate_tile, 0)

    gd_y = []

    def down_grad(zl):
        def tile(i, _):
            at = pl.ds(aligned(512 * i, 512), 512)
            part = dot(g.hidden_t[384 * zl : 384 * zl + 384, :], cot2d[:, at]).astype(bf16)
            g.gd[zl, :, :, at] = part.reshape(2, 192, 512)
            return 0

        lax.fori_loop(0, 2, tile, 0)

    def down_send(zl):
        gd_y.append(lk.put(g.gd.at[zl, 1 - y], g.gd_y.at[zl], ynb))

    down_grad(0)
    down_grad(1)

    for tb in range(8):
        if tb % 4 == 0:
            half = slice(128 * tb, 128 * tb + 512)
            lk.got(gm_xs[tb // 4], g.gm_xin.at[:, half])
        at = slice(128 * tb, 128 * tb + 128)
        total = g.state[0:128, at] + g.gm_in[x, :, at].astype(f32) + g.gm_xin[:, at].astype(f32)
        g.w_val_t[:, at] = dot(total.astype(bf16), flip).astype(bf16)
    gm_cs = channel_send(g.w_val_t, g.gm_land)
    g.gm_land[n] = g.w_val_t[pl.ds(aligned(16 * n, 16), 16), :]

    down_send(0)
    down_send(1)

    z1 = z + 1 - 2 * lax.rem(z, 2)
    z2 = zo(2)
    z3 = 3 - z

    def put_add(mine, pair):
        return (mine[...].astype(f32) + pair[...].astype(f32)).astype(bf16)

    near_half = z // 2 == c
    gd_r = lk.take(3)
    d_pair = (lk.take(), lk.take())

    def down_owner(zl, when, zd, place):
        for cm in range(2):
            src = g.gd.at[zl, y, pl.ds(96 * cm, 96)]
            copy = lk.make(src, g.gd_in.at[place], lk.take(), gd_r + place, dev(x, zd, y, cm))
            pl.when(when)(copy.start)
            lk.pending.append((copy, when))

    def down_sum(zl):
        lk.got(gd_y[zl], g.gd_y.at[zl])
        total = g.gd[zl, y].astype(f32) + g.gd_y[zl].astype(f32)
        g.gd[zl, y] = total.astype(bf16)
        same = lax.rem(z, 2) == zl
        down_owner(zl, jnp.logical_and(near_half, jnp.logical_not(same)), z1, 1)
        copy = lk.make(g.gd.at[zl, y], g.gd_p, d_pair[zl], d_pair[zl], dev(x, z1, y, c))
        sends = jnp.logical_and(jnp.logical_not(near_half), jnp.logical_not(same))
        pl.when(sends)(copy.start)
        lk.pending.append((copy, sends))
        own = jnp.logical_and(near_half, same)

        @pl.when(own)
        def _():
            g.gd_in[0] = g.gd[zl, y, pl.ds(aligned(96 * c, 32), 96), :]

        other = g.gd.at[zl, y, pl.ds(aligned(96 * (1 - c), 32), 96)]
        copy = lk.make(other, g.gd_in.at[0], lk.take(), gd_r, sib)
        pl.when(own)(copy.start)
        lk.pending.append((copy, own))

    def down_far(zl):
        adds = jnp.logical_and(jnp.logical_not(near_half), lax.rem(z, 2) == zl)

        @pl.when(adds)
        def _():
            lk.make(g.gd_p, g.gd_p, d_pair[zl], d_pair[zl], ynb).wait_recv()
            g.gd[zl, y] = put_add(g.gd.at[zl, y], g.gd_p)

        down_owner(zl, adds, z2, 2)

    def back_pairs():
        near = lk.put(g.gb_z.at[:, z1], g.gb_in.at[0], dev(x, z1, y, c))
        pair = lk.put(g.gb_z.at[:, z3], g.gb_in.at[1], dev(x, z1, y, c))
        return near, pair

    def back_far(pair):
        lk.got(pair, g.gb_in.at[1])
        g.gb_z[:, z2] = put_add(g.gb_z.at[:, z2], g.gb_in.at[1])
        return lk.put(g.gb_z.at[:, z2], g.gb_in.at[2], dev(x, z2, y, c))

    def group_sum(part, send, land, xsend, xland):
        for xm in range(2):
            send[xm] = part(xm, 1 - c).astype(bf16)
        first = lk.put(send, land, sib)
        mine = part(1 - x, c)
        lk.got(first, land)
        xsend[...] = (mine + land[1 - x].astype(f32)).astype(bf16)
        second = lk.put(xsend, xland, xn)

        def own():
            return part(x, c) + land[x].astype(f32) + xland[...].astype(f32)

        return second, own

    def branch_part(xm, cm):
        rows = pl.ds(aligned(256 * (2 * xm + cm), 256), 256)
        return dot(g.hidden[rows, :], down2d[...])

    spare = g.normed.reshape(2, 2, 256, 1024)
    br_s, br_own = group_sum(
        branch_part, spare.at[0], g.br_in, g.tok_all.at[r].reshape(256, 1024), g.br_xin
    )

    other = pl.ds(aligned(64 * (1 - y), 64), 64)
    own64 = pl.ds(aligned(64 * y, 64), 64)
    up_y, gu_s = {}, {}
    up_to = {0: z, 1: z1, 2: z2, 3: z3}

    def up_grad(k):
        z_d = up_to[k]
        rows = pl.ds(aligned(256 * z_d, 256), 256)
        part = dot(g.normed_t[rows, :], g.g_up[...]).astype(bf16)
        g.gu[z_d] = part.reshape(2, 128, 768)
        up_y[k] = lk.put(g.gu.at[z_d, :, other], g.gu_y.at[z_d], ynb)

    def up_sum(k):
        z_d = up_to[k]
        lk.got(up_y[k], g.gu_y.at[z_d])
        total = g.gu[z_d, :, own64, :].astype(f32) + g.gu_y[z_d].astype(f32)
        if k == 2:
            lk.got(gu_s[3], g.gu_in.at[0])
            total = total + g.gu_in[0].astype(f32)
        g.gu[z_d, :, own64, :] = total.astype(bf16)
        if k:
            to = dev(x, up_to[2 if k == 2 else 1], y, c)
            gu_s[k] = lk.put(g.gu.at[z_d, :, own64], g.gu_in.at[(1, 2, 0)[k - 1]], to)

    lk.got(gb_y, g.gb_y)
    total = g.gb[:, y].astype(f32) + g.gb_y[...].astype(f32)
    g.gb_z[...] = total.astype(bf16).reshape(4, 4, 16, 768)
    gb_near, gb_pair = back_pairs()
    channel_got(gm_cs, g.gm_land)
    unpack(g.gm_land, put_grad)

    def conv_back(h, _):
        parts = [conv_rows(h, k) for k in range(16)]
        own = g.vr32[pl.ds(aligned(64 * h, 64), 64), :].T.astype(bf16)
        out = g.skip_b[pl.ds(16 * x + h, 1), :] * parts[0]
        lhs = []
        for kk in range(8):
            lhs.append(jnp.concatenate([parts[2 * kk], parts[2 * kk + 1]], axis=1).astype(bf16))
            out = out + dot(lhs[kk], g.toep[h, 2 * kk : 2 * kk + 2].reshape(256, 128))
        g.o32[pl.ds(aligned(64 * h, 64), 64), :] = out
        after = jnp.zeros((128, 128), f32)
        for kk in range(7, -1, -1):
            pair = dot(own, lhs[kk])
            for half in (1, 0):
                turned = pltpu.roll(
                    pair[:, 128 * half : 128 * half + 128], 0, 1, stride=1, stride_axis=0
                )
                lag = jnp.where(jj >= ii, turned, after)
                after = turned
                at = pl.ds(aligned((16 * (2 * kk + half) + h) * 8, 8), 8)
                g.gk8[at, :] = jnp.sum(lag.reshape(16, 8, 128), axis=0)
        return 0

    lax.fori_loop(0, 8, conv_back, 0, unroll=2)
    lax.fori_loop(8, 16, conv_back, 0, unroll=2)
    pack(g.gv_out, True)
    gv_s = channel_back(g.gv_out, g.g_val)
    g.g_val[pl.ds(aligned(16 * n, 16), 16), :] = g.gv_out[n]

    up_grad(3)
    down_sum(0)
    gb_far = back_far(gb_pair)
    down_sum(1)

    tall = g.gk8[pl.ds(0, 256, stride=8), :]
    for s_ in range(1, 8):
        tall = tall + g.gk8[pl.ds(s_, 256, stride=8), :]
    for half in range(2):
        hi_, lo_ = split(tall[128 * half : 128 * half + 128, :])
        g.state[128 * half : 128 * half + 128, :] = (
            dot(hi_, g.near_t_hi[...]) + dot(lo_, g.near_t_hi[...]) + dot(hi_, g.near_t_lo[...])
        )
    g.skip_sum[...] = tall[0:16, :]

    def far_back(p, carry):
        gc, gs = carry
        hr = g.far_re[pl.ds(p, 1), :]
        hi = g.far_im[pl.ds(p, 1), :]
        rows = pl.ds(aligned(16 * p, 16), 16)
        ur = g.state[rows, 0:512]
        ui = g.state[rows, 512:1024]
        return gc + hr * ur - hi * ui, gs + hr * ui + hi * ur

    blank = jnp.zeros((16, 512), f32)
    gc, gs = lax.fori_loop(0, 16, far_back, (blank, blank))
    g.gcoef[0] = gc
    g.gcoef[1] = gs
    gcoef_s = lk.put(g.gcoef.at[1 - x], g.gcoef_in, xn)
    skip_s = lk.put(g.skip_sum, g.skip_in, xn)

    channel_back_got(gv_s, g.g_val)
    for tb in range(8):
        at = slice(128 * tb, 128 * tb + 128)
        back = dot(g.g_val[:, at], flip)
        g.gvp_t[at, :] = (back * g.val_slope[:, at]).astype(bf16).T
    part = dot(g.normed_t[...], g.gvp_t[...]).astype(bf16)
    g.gv[...] = part.reshape(4, 2, 128, 128)
    gv_y = lk.put(g.gv.at[:, :, other], g.gv_y, ynb)

    def normed_part(xm, cm):
        rows = pl.ds(aligned(256 * (2 * xm + cm), 256), 256)
        return dot_nt(g.g_up[rows, :], up2d[...]) + dot_nt(g.gvp_t[rows, :], g.w_val[...])

    gn_s, gn_own = group_sum(
        normed_part, spare.at[1], g.gn_in, g.tok_all.at[r_sib].reshape(256, 1024), g.gn_xin
    )
    up_grad(2)
    up_grad(1)
    up_grad(0)
    up_sum(3)
    down_far(0)
    down_far(1)

    lk.got(gv_y, g.gv_y)
    g.gv_z[...] = (g.gv[:, :, own64, :].astype(f32) + g.gv_y[...].astype(f32)).astype(bf16)
    gv_zs = {}
    for k in (2, 1, 3):
        gv_zs[k] = lk.put(g.gv_z.at[zo(k)], g.gv_in.at[k - 1], dev(x, zo(k), y, c))

    up_sum(2)

    lk.got(gn_s, g.gn_xin)
    up_sum(1)
    g.state[...] = gn_own()

    def norm_back(i, carry):
        dg, ds = carry
        s_, part = i // 2, pl.ds(aligned(64 * lax.rem(i, 2), 64), 64)
        rows = g.tokens[s_, part, :].astype(f32)
        mean = jnp.mean(rows, axis=-1, keepdims=True)
        cen = rows - mean
        var = jnp.mean(cen * cen, axis=-1, keepdims=True)
        inv = lax.rsqrt(var + 1e-5)
        zn = cen * inv
        gn = g.state[pl.ds(aligned(64 * i, 64), 64), :]
        gg = gn * g.norm_rows[0:1, :]
        m1 = jnp.mean(gg, axis=-1, keepdims=True)
        m2 = jnp.mean(gg * zn, axis=-1, keepdims=True)
        g.g_tokens[s_, part, :] = g.cot[s_, part, :].astype(f32) + inv * (gg - m1 - zn * m2)
        dg = dg + jnp.sum(gn * zn, axis=0, keepdims=True)
        ds = ds + jnp.sum(gn, axis=0, keepdims=True)
        return dg, ds

    blank = jnp.zeros((1, 1024), f32)
    dg, ds = lax.fori_loop(0, 4, norm_back, (blank, blank))
    for zd in range(4):
        g.ng[zd, 0:1, :] = dg[:, 128 * zd : 128 * zd + 128]
        g.ng[zd, 1:2, :] = dg[:, 512 + 128 * zd : 640 + 128 * zd]
        g.ng[zd, 2:3, :] = ds[:, 128 * zd : 128 * zd + 128]
        g.ng[zd, 3:4, :] = ds[:, 512 + 128 * zd : 640 + 128 * zd]
        g.ng[zd, 4:8, :] = jnp.zeros((4, 128), f32)
    ng_s = []
    for k in range(1, 8):
        to = lax.rem(n + k, 8)
        ng_s.append(lk.put(g.ng.at[to // 2], g.ng_in.at[k - 1], (x, 2 * to + c)))

    lk.got(br_s, g.br_xin)
    out = br_own().reshape(2, 128, 1024) + g.tokens[...].astype(f32)
    g.result[...] = out.astype(bf16)

    up_sum(0)

    total = g.gu[z, :, own64, :].astype(f32)
    for k in (2, 1):
        lk.got(gu_s[k], g.gu_in.at[(1, 2, 0)[k - 1]])
        total = total + g.gu_in[(1, 2, 0)[k - 1]].astype(f32)
    g.gu_f[...] = total.reshape(2, 2, 32, 768).astype(bf16)
    fin_u = [lk.put(g.gu_f.at[xm, cm], g.fu_in.at[r], to) for to, xm, cm, rm in members]
    lk.got(gb_near, g.gb_in.at[0])
    lk.got(gb_far, g.gb_in.at[2])
    total = g.gb_z[:, z].astype(f32) + g.gb_in[0].astype(f32) + g.gb_in[2].astype(f32)
    g.gb_f[...] = total.astype(bf16)
    fin_b = [lk.put(g.gb_f.at[2 * cm + xm], g.fb_in.at[r], to) for to, xm, cm, rm in members]
    for k in (2, 1, 3):
        lk.got(gv_zs[k], g.gv_in.at[k - 1])
    total = g.gv_z[z].astype(f32)
    for k in range(3):
        total = total + g.gv_in[k].astype(f32)
    g.gv_f[...] = total.reshape(2, 2, 32, 128).astype(bf16)
    fin_v = [lk.put(g.gv_f.at[xm, cm], g.fv_in.at[r], to) for to, xm, cm, rm in members]
    g.fu_in[r] = g.gu_f[x, c]
    g.fb_in[r] = g.gb_f[2 * c + x]
    g.fv_in[r] = g.gv_f[x, c]

    from_sib = owner != c

    @pl.when(from_sib)
    def _():
        lk.make(g.gd_in.at[0], g.gd_in.at[0], gd_r, gd_r, sib).wait_recv()

    for place in (1, 2):
        region = g.gd_in.at[place]
        lk.make(region, region, gd_r + place, gd_r + place, sib).wait_recv()
    g.o_down[...] = (
        g.gd_in[0].astype(f32) + g.gd_in[1].astype(f32) + g.gd_in[2].astype(f32)
    )

    mine = pl.ds(aligned(16 * x, 16), 16)
    theirs = pl.ds(aligned(16 * (1 - x), 16), 16)
    lk.got(gcoef_s, g.gcoef_in)
    g.o_coef[mine, :] = g.gcoef[x]
    g.o_coef[theirs, :] = g.gcoef_in[...]
    lk.got(skip_s, g.skip_in)
    g.o_skip[mine, :] = g.skip_sum[...]
    g.o_skip[theirs, :] = g.skip_in[...]

    total = g.ng[z]
    for k in range(1, 8):
        lk.got(ng_s[k - 1], g.ng_in.at[k - 1])
        total = total + g.ng_in[k - 1]
    g.ng_f[...] = total
    ng_t = [lk.put(g.ng_f, g.ng_fin.at[i], to) for i, (to, xm, cm, rm) in enumerate(members)]

    for i, (to, xm, cm, rm) in enumerate(members):
        lk.got(fin_u[i], g.fu_in.at[rm])
        lk.got(fin_b[i], g.fb_in.at[rm])
        lk.got(fin_v[i], g.fv_in.at[rm])
    for i in range(3):
        lk.got(ng_t[i], g.ng_fin.at[i])
        total = total + g.ng_fin[i]
    total = jnp.where(x == 0, total, pltpu.roll(total, 7, 0))
    g.o_norm[...] = pltpu.roll(total, 128 - (64 * y + 32 * c), 1)
    lk.finish()
    assert lk.count <= N_SEMS


def start_of(copy):
    copy.start()
    return copy


def fast_body(
    tokens, norm_gain, norm_shift, w_up, w_value, w_back, w_down, mode_coef, skip_gain, cotangent
):
    states = 512
    length = tokens.shape[1] * lax.axis_size("tok")
    far_re, far_im, near_hi, near_lo, near_t_hi, near_t_lo = mode_tables(states, length)
    ins = dict(
        tokens=tokens,
        norm_gain=norm_gain.reshape(1, -1),
        norm_shift=norm_shift.reshape(1, -1),
        w_up=w_up,
        w_value=w_value,
        w_back=w_back,
        w_down=w_down,
        mode_coef=mode_coef,
        skip=skip_gain.reshape(1, -1),
        cot=cotangent,
        far_re=far_re,
        far_im=far_im,
        near_hi=near_hi,
        near_lo=near_lo,
        near_t_hi=near_t_hi,
        near_t_lo=near_t_lo,
    )
    outs = dict(
        result=((2, 128, 1024), bf16),
        g_tokens=((2, 128, 1024), f32),
        o_norm=((8, 128), f32),
        fu_in=((4, 32, 768), bf16),
        fv_in=((4, 32, 128), bf16),
        fb_in=((4, 16, 768), bf16),
        o_down=((96, 1024), f32),
        o_coef=((32, 512), f32),
        o_skip=((32, 128), f32),
    )
    scratch = dict(
        pk_send=((4, 48, 128), bf16),
        pk=((2, 8, 2, 48, 128), bf16),
        coef=((2, 16, 512), bf16),
        w_up_all=((2, 8, 2, 32, 768), bf16),
        w_back_all=((2, 2, 2, 4, 16, 768), bf16),
        w_down_all=((2, 2, 2, 96, 1024), bf16),
        tok_all=((4, 2, 128, 1024), bf16),
        cot_all=((4, 2, 128, 1024), bf16),
        state=((256, 1024), f32),
        kern=((256, 128), f32),
        toep=((16, 16, 128, 128), bf16),
        norm_rows=((8, 1024), f32),
        w_val=((1024, 128), bf16),
        w_val_t=((128, 1024), bf16),
        normed=((1024, 1024), bf16),
        normed_t=((1024, 1024), bf16),
        val_slope=((128, 1024), f32),
        val=((128, 1024), bf16),
        val_in=((8, 16, 1024), bf16),
        v32=((2048, 128), f32),
        vr32=((1024, 128), f32),
        o32=((1024, 128), f32),
        skip_b=((32, 128), f32),
        mix_out=((8, 16, 1024), bf16),
        mix=((4, 128, 1024), bf16),
        act=((1024, 768), f32),
        slope=((1024, 768), f32),
        g_gate=((1024, 768), bf16),
        gm_send=((2, 128, 1024), bf16),
        gm_in=((2, 128, 1024), bf16),
        gm_x=((128, 1024), bf16),
        gm_xin=((128, 1024), bf16),
        gm_land=((8, 16, 1024), bf16),
        mix_tok=((1024, 512), bf16),
        hidden=((1024, 768), bf16),
        hidden_t=((768, 1024), bf16),
        g_up=((1024, 768), bf16),
        gd=((2, 2, 192, 1024), bf16),
        gd_y=((2, 192, 1024), bf16),
        gd_in=((3, 96, 1024), bf16),
        gd_p=((192, 1024), bf16),
        gu=((4, 2, 128, 768), bf16),
        gu_y=((4, 2, 64, 768), bf16),
        gu_in=((3, 2, 64, 768), bf16),
        gu_f=((2, 2, 32, 768), bf16),
        gb=((2, 2, 128, 768), bf16),
        gb_y=((2, 128, 768), bf16),
        gb_z=((4, 4, 16, 768), bf16),
        gb_in=((3, 4, 16, 768), bf16),
        gb_f=((4, 16, 768), bf16),
        gv=((4, 2, 128, 128), bf16),
        gv_y=((4, 2, 64, 128), bf16),
        gv_z=((4, 2, 64, 128), bf16),
        gv_in=((3, 2, 64, 128), bf16),
        gv_f=((2, 2, 32, 128), bf16),
        gk8=((2048, 128), f32),
        skip_sum=((16, 128), f32),
        skip_in=((16, 128), f32),
        gcoef=((2, 16, 512), f32),
        gcoef_in=((16, 512), f32),
        gv_out=((8, 16, 1024), bf16),
        g_val=((128, 1024), bf16),
        gvp_t=((1024, 128), bf16),
        br_in=((2, 256, 1024), bf16),
        br_xin=((256, 1024), bf16),
        gn_in=((2, 256, 1024), bf16),
        gn_xin=((256, 1024), bf16),
        ng=((4, 8, 128), f32),
        ng_in=((7, 8, 128), f32),
        ng_f=((8, 128), f32),
        ng_fin=((3, 8, 128), f32),
    )
    names = list(ins) + list(outs) + list(scratch) + ["ssem", "rsem"]
    vmem = pl.BlockSpec(memory_space=pltpu.VMEM)
    got = pl.pallas_call(
        functools.partial(layer_kernel, names),
        out_shape=[jax.ShapeDtypeStruct(s, t) for s, t in outs.values()],
        in_specs=[vmem] * len(ins),
        out_specs=[vmem] * len(outs),
        scratch_shapes=[pltpu.VMEM(s, t) for s, t in scratch.values()]
        + [pltpu.SemaphoreType.DMA((N_SEMS,)), pltpu.SemaphoreType.DMA((N_SEMS,))],
        compiler_params=pltpu.CompilerParams(
            collective_id=0, has_side_effects=True, vmem_limit_bytes=64 << 20
        ),
    )(*ins.values())
    up_rows, back_rows = w_up.shape[0], w_back.shape[0]
    final = [
        jax.ShapeDtypeStruct((2, 128, 1024), bf16),
        jax.ShapeDtypeStruct((2, 128, 1024), f32),
        jax.ShapeDtypeStruct((1, 32), f32),
        jax.ShapeDtypeStruct((1, 32), f32),
        jax.ShapeDtypeStruct((up_rows, 3072), f32),
        jax.ShapeDtypeStruct((up_rows, 512), f32),
        jax.ShapeDtypeStruct((back_rows, 3072), f32),
        jax.ShapeDtypeStruct((96, 1024), f32),
        jax.ShapeDtypeStruct((32, 512), f32),
        jax.ShapeDtypeStruct((1, 32), f32),
    ]
    out = pl.pallas_call(
        last_kernel,
        out_shape=final,
        in_specs=[vmem] * len(outs),
        out_specs=[vmem] * len(final),
        compiler_params=pltpu.CompilerParams(vmem_limit_bytes=63 << 20),
    )(*got)
    return tuple(v.reshape(-1) if v.shape[0] == 1 else v for v in out)


def last_kernel(*refs):
    (result, g_tokens, norm, up, value, back, down, coef, skip), out = refs[:9], refs[9:]
    out[0][...] = result[...]
    out[1][...] = g_tokens[...]
    out[2][...] = norm[0:1, 0:32]
    out[3][...] = norm[2:3, 0:32]
    for rr in range(4):
        out[4][:, 768 * rr : 768 * rr + 768] = up[rr].astype(f32)
        out[6][:, 768 * rr : 768 * rr + 768] = back[rr].astype(f32)
    out[5][...] = sum(dot_nt(value[rr], channels_of(rr)) for rr in range(4))
    out[7][...] = down[...]
    out[8][...] = coef[...]
    same = lax.broadcasted_iota(jnp.int32, (32, 32), 0) == lax.broadcasted_iota(
        jnp.int32, (32, 32), 1
    )
    column = jnp.broadcast_to(skip[:, 127:128], (32, 32))
    out[9][...] = jnp.sum(jnp.where(same, column, 0.0), axis=0, keepdims=True)


def run(tokens, *rest):
    sizes = (lax.axis_size("item"), lax.axis_size("tok"), tokens.shape)
    if sizes == (2, 16, (2, 128, 1024)):
        return fast_body(tokens, *rest)
    return body(tokens, *rest)


def solution(mesh):
    in_specs = (
        P("item", "tok", None),
        P(("item", "tok")),
        P(("item", "tok")),
        P(("item", "tok"), None),
        P(("item", "tok"), None),
        P(("item", "tok"), None),
        P(("item", "tok"), None),
        P("tok", "item"),
        P("tok"),
        P("item", "tok", None),
    )
    out_specs = (
        P("item", "tok", None),
        P("item", "tok", None),
        P(("item", "tok")),
        P(("item", "tok")),
        P(("item", "tok"), None),
        P(("item", "tok"), None),
        P(("item", "tok"), None),
        P(("item", "tok"), None),
        P("tok", "item"),
        P("tok"),
    )
    return jax.shard_map(run, mesh=mesh, in_specs=in_specs, out_specs=out_specs, check_vma=False)
```

```python
import functools
import math
import types

import jax
import jax.numpy as jnp
import ml_dtypes
import numpy as np
from jax import lax
from jax.experimental import pallas as pl
from jax.experimental.pallas import tpu as pltpu
from jax.sharding import PartitionSpec as P

highest = lax.Precision.HIGHEST


def basis_block(start_index, block_width, length, states):
    places = start_index + jnp.arange(block_width, dtype=jnp.int32)
    mode_ids = jnp.arange(states, dtype=jnp.int32)
    fraction = (mode_ids * 41 % states).astype(jnp.float32) / states
    mode_rates = jnp.exp(jnp.log(1.0 / 32.0) + fraction * jnp.log(32.0 / (4.0 * length)))
    decays = jnp.exp(-mode_rates[:, None] * places[None, :].astype(jnp.float32))
    phase_turns = (mode_ids[:, None] * places[None, :] % (2 * states)).astype(jnp.float32) * (
        jnp.pi / states
    )
    return jnp.concatenate([decays * jnp.cos(phase_turns), decays * jnp.sin(phase_turns)], axis=0)


def make_kernel(coef_full, length):
    states = coef_full.shape[1] // 2
    block_width = math.gcd(length, 2048)
    block_count = length // block_width

    def one_block(block_index):
        table = basis_block(block_index * block_width, block_width, length, states)
        return jnp.dot(coef_full, table, precision=highest)

    pieces = lax.map(one_block, jnp.arange(block_count, dtype=jnp.int32))
    return jnp.transpose(pieces, (1, 0, 2)).reshape(coef_full.shape[0], length)


def coef_gradient(grad_kernel, states):
    channels, length = grad_kernel.shape
    block_width = math.gcd(length, 2048)
    block_count = length // block_width
    slabs = grad_kernel.reshape(channels, block_count, block_width)

    def add_block(running, block_index):
        slab_part = lax.dynamic_index_in_dim(slabs, block_index, 1, keepdims=False)
        table = basis_block(block_index * block_width, block_width, length, states)
        return (running + jnp.dot(slab_part, table.T, precision=highest), None)

    start_total = jnp.zeros((channels, 2 * states), jnp.float32)
    summed, unused = lax.scan(add_block, start_total, jnp.arange(block_count, dtype=jnp.int32))
    return summed


def unit_tables(row_count, column_count, period):
    row_ids = jnp.arange(row_count, dtype=jnp.int32)[:, None]
    column_ids = jnp.arange(column_count, dtype=jnp.int32)[None, :]
    phase_turns = (row_ids * column_ids % period).astype(jnp.float32) * (2.0 * jnp.pi / period)
    return (jnp.cos(phase_turns), jnp.sin(phase_turns))


def right_product(left_part, table):
    return jnp.einsum("...kq,qm->...km", left_part, table, precision=highest)


def spectrum(signal):
    length = signal.shape[-1]
    padded_size = 2 * length
    outer_size = padded_size // 128
    half_size = outer_size // 2
    folded = signal.reshape(signal.shape[:-1] + (half_size, 128))
    cos_outer, sin_outer = unit_tables(outer_size, half_size, outer_size)
    section_real = jnp.einsum("kp,...pq->...kq", cos_outer, folded, precision=highest)
    section_imag = -jnp.einsum("kp,...pq->...kq", sin_outer, folded, precision=highest)
    twist_cos, twist_sin = unit_tables(outer_size, 128, padded_size)
    turned_real = section_real * twist_cos + section_imag * twist_sin
    turned_imag = section_imag * twist_cos - section_real * twist_sin
    cos_inner, sin_inner = unit_tables(128, 128, 128)
    out_real = right_product(turned_real, cos_inner) + right_product(turned_imag, sin_inner)
    out_imag = right_product(turned_imag, cos_inner) - right_product(turned_real, sin_inner)
    return (out_real, out_imag)


def inverse(spec_real, spec_imag):
    outer_size = spec_real.shape[-2]
    padded_size = outer_size * 128
    half_size = outer_size // 2
    cos_inner, sin_inner = unit_tables(128, 128, 128)
    back_real = right_product(spec_real, cos_inner) - right_product(spec_imag, sin_inner)
    back_imag = right_product(spec_real, sin_inner) + right_product(spec_imag, cos_inner)
    twist_cos, twist_sin = unit_tables(outer_size, 128, padded_size)
    turned_real = back_real * twist_cos - back_imag * twist_sin
    turned_imag = back_real * twist_sin + back_imag * twist_cos
    cos_outer, sin_outer = unit_tables(half_size, outer_size, outer_size)
    signal = jnp.einsum("pk,...kq->...pq", cos_outer, turned_real, precision=highest)
    signal = signal - jnp.einsum("pk,...kq->...pq", sin_outer, turned_imag, precision=highest)
    return signal.reshape(signal.shape[:-2] + (half_size * 128,)) / padded_size


def layer_norm(token_rows, gain_row, shift_row):
    row_mean = jnp.mean(token_rows, axis=-1, keepdims=True)
    centered = token_rows - row_mean
    variance = jnp.mean(centered * centered, axis=-1, keepdims=True)
    return centered * lax.rsqrt(variance + 1e-05) * gain_row + shift_row


def body(
    tokens, norm_gain, norm_shift, w_up, w_value, w_back, w_down, mode_coef, skip_gain, cotangent
):
    gain_full, shift_full, up_full, value_full = (
        lax.all_gather(norm_gain, ("item", "tok"), axis=0, tiled=True),
        lax.all_gather(norm_shift, ("item", "tok"), axis=0, tiled=True),
        lax.all_gather(w_up, ("item", "tok"), axis=0, tiled=True),
        lax.all_gather(w_value, ("item", "tok"), axis=0, tiled=True),
    )
    back_full, down_full = (
        lax.all_gather(w_back, ("item", "tok"), axis=0, tiled=True),
        lax.all_gather(w_down, ("item", "tok"), axis=0, tiled=True),
    )
    coef_full = lax.all_gather(mode_coef, "item", axis=1, tiled=True)
    token_rows = tokens.astype(jnp.float32)
    gain_float = gain_full.astype(jnp.float32)
    shift_float = shift_full.astype(jnp.float32)
    normed = layer_norm(token_rows, gain_float, shift_float).astype(jnp.bfloat16)
    up_pre = jnp.einsum("std,df->stf", normed, up_full, preferred_element_type=jnp.float32)
    value_pre = jnp.einsum("std,dh->sht", normed, value_full, preferred_element_type=jnp.float32)
    value = jax.nn.gelu(value_pre).astype(jnp.bfloat16)
    channel_values = lax.all_to_all(value, "tok", split_axis=1, concat_axis=2, tiled=True)
    length = channel_values.shape[-1]
    kernel = make_kernel(coef_full.astype(jnp.float32), length)
    signal = channel_values.astype(jnp.float32)
    skip_column = skip_gain.astype(jnp.float32)[:, None]
    value_real, value_imag = spectrum(signal)
    kernel_real, kernel_imag = spectrum(kernel)
    conv_out = inverse(
        value_real * kernel_real - value_imag * kernel_imag,
        value_real * kernel_imag + value_imag * kernel_real,
    )
    mixed_channels = (conv_out + skip_column * signal).astype(jnp.bfloat16)
    mixed = lax.all_to_all(mixed_channels, "tok", split_axis=2, concat_axis=1, tiled=True)
    gate = jnp.einsum("sht,hf->stf", mixed, back_full, preferred_element_type=jnp.float32)
    up_act = jax.nn.gelu(up_pre)
    hidden = (up_act * gate).astype(jnp.bfloat16)
    branch = jnp.einsum("stf,fd->std", hidden, down_full, preferred_element_type=jnp.float32)
    result = (token_rows + branch).astype(jnp.bfloat16)
    grad_w_down = jnp.einsum("stf,std->fd", hidden, cotangent, preferred_element_type=jnp.float32)
    grad_hidden = jnp.einsum(
        "std,fd->stf", cotangent, down_full, preferred_element_type=jnp.float32
    )
    grad_gate = (grad_hidden * up_act).astype(jnp.bfloat16)
    grad_up_act = grad_hidden * gate
    grad_w_back = jnp.einsum("sht,stf->hf", mixed, grad_gate, preferred_element_type=jnp.float32)
    grad_mixed = jnp.einsum(
        "stf,hf->sht", grad_gate, back_full, preferred_element_type=jnp.float32
    ).astype(jnp.bfloat16)
    grad_channels = lax.all_to_all(grad_mixed, "tok", split_axis=1, concat_axis=2, tiled=True)
    grad_signal = grad_channels.astype(jnp.float32)
    grad_real, grad_imag = spectrum(grad_signal)
    grad_value_channels = inverse(
        kernel_real * grad_real + kernel_imag * grad_imag,
        kernel_real * grad_imag - kernel_imag * grad_real,
    )
    grad_value_channels = (grad_value_channels + skip_column * grad_signal).astype(jnp.bfloat16)
    grad_kernel = inverse(
        jnp.sum(grad_real * value_real + grad_imag * value_imag, axis=0),
        jnp.sum(grad_imag * value_real - grad_real * value_imag, axis=0),
    )
    grad_skip_part = jnp.sum(grad_signal * signal, axis=(0, 2))
    grad_coef_part = coef_gradient(grad_kernel, coef_full.shape[1] // 2)
    grad_mode_coef = lax.psum_scatter(grad_coef_part, "item", scatter_dimension=1, tiled=True)
    grad_skip_gain = lax.psum(grad_skip_part, "item")
    grad_value = lax.all_to_all(grad_value_channels, "tok", split_axis=2, concat_axis=1, tiled=True)
    gelu_value_back = jax.vjp(jax.nn.gelu, value_pre)[1]
    grad_value_pre = gelu_value_back(grad_value.astype(jnp.float32))[0].astype(jnp.bfloat16)
    gelu_up_back = jax.vjp(jax.nn.gelu, up_pre)[1]
    grad_up_pre = gelu_up_back(grad_up_act)[0].astype(jnp.bfloat16)
    grad_w_up = jnp.einsum("std,stf->df", normed, grad_up_pre, preferred_element_type=jnp.float32)
    grad_w_value = jnp.einsum(
        "std,sht->dh", normed, grad_value_pre, preferred_element_type=jnp.float32
    )
    grad_normed = jnp.einsum(
        "stf,df->std", grad_up_pre, up_full, preferred_element_type=jnp.float32
    )
    grad_normed = grad_normed + jnp.einsum(
        "sht,dh->std", grad_value_pre, value_full, preferred_element_type=jnp.float32
    )
    norm_back = jax.vjp(layer_norm, token_rows, gain_float, shift_float)[1]
    grad_rows, grad_gain_part, grad_shift_part = norm_back(grad_normed)
    grad_tokens = cotangent.astype(jnp.float32) + grad_rows
    owners = lax.axis_size("item") * lax.axis_size("tok")
    norm_flat = jnp.concatenate(
        [grad_gain_part.reshape(owners, -1), grad_shift_part.reshape(owners, -1)], axis=1
    )
    up_flat = grad_w_up.reshape(owners, -1)
    value_flat = grad_w_value.reshape(owners, -1)
    back_flat = grad_w_back.reshape(owners, -1)
    down_flat = grad_w_down.reshape(owners, -1)
    summed = (
        lax.psum_scatter(norm_flat, ("item", "tok"), scatter_dimension=0, tiled=True),
        lax.psum_scatter(up_flat, ("item", "tok"), scatter_dimension=0, tiled=True),
        lax.psum_scatter(value_flat, ("item", "tok"), scatter_dimension=0, tiled=True),
        lax.psum_scatter(back_flat, ("item", "tok"), scatter_dimension=0, tiled=True),
        lax.psum_scatter(down_flat, ("item", "tok"), scatter_dimension=0, tiled=True),
    )
    gain_count = norm_gain.shape[0]
    norm_row = summed[0].reshape(-1)
    grad_norm_gain = norm_row[:gain_count]
    grad_norm_shift = norm_row[gain_count:]
    grad_up_out = summed[1].reshape(w_up.shape)
    grad_value_out = summed[2].reshape(w_value.shape)
    grad_back_out = summed[3].reshape(w_back.shape)
    grad_down_out = summed[4].reshape(w_down.shape)
    return (
        result,
        grad_tokens,
        grad_norm_gain,
        grad_norm_shift,
        grad_up_out,
        grad_value_out,
        grad_back_out,
        grad_down_out,
        grad_mode_coef,
        grad_skip_gain,
    )


MESH_ID = pl.DeviceIdType.MESH
bf16, f32 = jnp.bfloat16, jnp.float32
NT = (((1,), (1,)), ((), ()))
GC = math.sqrt(2.0 / math.pi)


def dot(a, b):
    return jnp.dot(a, b, preferred_element_type=f32)


def dot_nt(a, b):
    return lax.dot_general(a, b, NT, preferred_element_type=f32)


def gelu_parts(v):
    t = jnp.tanh(GC * (v + 0.044715 * v * v * v))
    half = 0.5 * (1.0 + t)
    slope = half + 0.5 * v * (1.0 - t * t) * (GC * (1.0 + 3 * 0.044715 * v * v))
    return v * half, slope


def split(v):
    high = v.astype(bf16)
    return high, (v - high.astype(f32)).astype(bf16)


def mode_tables(states, length):
    n = np.arange(states)
    rates = np.exp(np.log(1.0 / 32.0) + (n * 41 % states) / states * np.log(32.0 / (4.0 * length)))

    def table(places):
        decay = np.exp(-rates[:, None] * places[None, :])
        turn = (n[:, None] * places[None, :] % (2 * states)) * (np.pi / states)
        return decay * np.cos(turn), decay * np.sin(turn)

    far_re, far_im = table(np.arange(0, length, 128))
    near = np.concatenate(table(np.arange(128)), axis=0).astype(np.float32)
    high = near.astype(ml_dtypes.bfloat16)
    low = (near - high.astype(np.float32)).astype(ml_dtypes.bfloat16)
    return (
        far_re.T.astype(np.float32).copy(),
        far_im.T.astype(np.float32).copy(),
        high,
        low,
        high.T[::-1].copy(),
        low.T[::-1].copy(),
    )


class Links:
    def __init__(self, send_sems, recv_sems, place):
        self.send_sems, self.recv_sems, self.place = send_sems, recv_sems, place
        self.count = 0
        self.pending = []

    def take(self, n=1):
        first = self.count
        self.count += n
        return first

    def make(self, src, dst, ssem, rsem, to):
        return pltpu.make_async_remote_copy(
            src_ref=src,
            dst_ref=dst,
            send_sem=self.send_sems.at[ssem],
            recv_sem=self.recv_sems.at[rsem],
            device_id=to,
            device_id_type=MESH_ID,
        )

    def put(self, src, dst, to):
        slot = self.take()
        copy = self.make(src, dst, slot, slot, to)
        copy.start()
        self.pending.append((copy, None))
        return slot

    def got(self, slot, region):
        self.make(region, region, slot, slot, self.place).wait_recv()

    def put_or_keep(self, src, dst, ssem, rsem, to, here):
        remote = self.make(src, dst, ssem, rsem, to)
        local = pltpu.make_async_copy(src, dst, self.recv_sems.at[rsem])
        away = jnp.logical_not(here)
        pl.when(here)(local.start)
        pl.when(away)(remote.start)
        self.pending.append((remote, away))

    def finish(self):
        for copy, away in self.pending:
            if away is None:
                copy.wait_send()
            else:
                pl.when(away)(copy.wait_send)


N_SEMS = 200


def channels_of(rr):
    ch = lax.broadcasted_iota(jnp.int32, (512, 128), 0)
    p = lax.broadcasted_iota(jnp.int32, (512, 128), 1)
    return (ch == 64 * (p // 16) + 32 * (rr % 2) + 16 * (rr // 2) + p % 16).astype(bf16)


def layer_kernel(names, *refs):
    r_ = dict(zip(names, refs))
    g = types.SimpleNamespace(**r_)
    x = lax.axis_index("item")
    tok = lax.axis_index("tok")
    z, y, c = tok // 4, (tok // 2) % 2, tok % 2
    n = tok // 2
    r = 2 * x + c

    def dev(x_, z_, y_, c_):
        return (x_, z_ * 4 + y_ * 2 + c_)

    def zo(k):
        return lax.rem(z + k, 4)

    def zb(k):
        return lax.rem(z + 4 - k, 4)

    def node(z_, y_):
        return 2 * z_ + y_

    sib, xn, diag = dev(x, z, y, 1 - c), dev(1 - x, z, y, c), dev(1 - x, z, y, 1 - c)
    r_sib, r_xn, r_diag = 2 * x + 1 - c, 2 * (1 - x) + c, 2 * (1 - x) + 1 - c
    members = ((sib, x, 1 - c, r_sib), (xn, 1 - x, c, r_xn), (diag, 1 - x, 1 - c, r_diag))
    ynb = dev(x, z, 1 - y, c)
    lk = Links(g.ssem, g.rsem, ynb)
    aligned = pl.multiple_of

    barrier = pltpu.get_barrier_semaphore()
    partners = [m[0] for m in members]
    for k in range(1, 4):
        partners += [dev(x, zo(k), y, c), dev(x, zo(k), 1 - y, c), dev(x, zo(k), y, 1 - c)]
    partners.append(ynb)
    for p in partners:
        pl.semaphore_signal(barrier, inc=1, device_id=p, device_id_type=MESH_ID)

    eye = lax.broadcasted_iota(jnp.int32, (32, 128), 0) == lax.broadcasted_iota(
        jnp.int32, (32, 128), 1
    )
    eye = eye.astype(bf16)
    row16 = lax.broadcasted_iota(jnp.int32, (16, 128), 0)
    gain_row = dot(g.norm_gain[...], eye)
    shift_row = dot(g.norm_shift[...], eye)
    norm_pack = jnp.where(
        row16 == 0,
        jnp.broadcast_to(gain_row, (16, 128)),
        jnp.where(row16 == 1, jnp.broadcast_to(shift_row, (16, 128)), 0.0),
    ).astype(bf16)
    for rr in range(4):
        pick = channels_of(rr)
        g.pk_send[rr, 0:32, :] = dot(g.w_value[...], pick).astype(bf16)
        g.pk_send[rr, 32:48, :] = norm_pack
    pl.semaphore_wait(barrier, len(partners))

    pk_s, up_s, back_s = [], [], []
    for to, xm, cm, rm in members:
        pk_s.append(lk.put(g.pk_send.at[rm], g.pk.at[x, n, c], to))
    coef_s = lk.put(g.mode_coef.at[pl.ds(aligned(16 * (1 - x), 16), 16), :], g.coef.at[x], xn)
    tok_x = lk.put(g.tokens, g.tok_all.at[r], xn)
    my_back = g.w_back_all.at[c, y, x, z]

    def cols(rm):
        return pl.ds(aligned(768 * rm, 128), 768)

    for to, xm, cm, rm in members:
        up_s.append(lk.put(g.w_up.at[:, cols(rm)], g.w_up_all.at[x, n, c], to))
    for to, xm, cm, rm in members:
        back_s.append(lk.put(g.w_back.at[:, cols(rm)], my_back, to))
    tok_sib = lk.put(g.tokens, g.tok_all.at[r], sib)
    cot_x = lk.put(g.cot, g.cot_all.at[r], xn)
    cot_sib = lk.put(g.cot, g.cot_all.at[r], sib)
    g.pk[x, n, c] = g.pk_send[r]
    g.w_up_all[x, n, c] = g.w_up[:, cols(r)]
    g.w_back_all[c, y, x, z] = g.w_back[:, cols(r)]
    g.cot_all[r] = g.cot[...]
    g.coef[x] = g.mode_coef[pl.ds(aligned(16 * x, 16), 16), :]

    def gather_start(region):
        slots = {}
        for k in (1, 2, 3):
            slots[k] = lk.put(region(z, y), region(z, y), dev(x, zo(k), y, c))
        slots[4] = lk.put(region(z, y), region(z, y), ynb)
        return slots

    def gather_pass(slots, region, k):
        lk.got(slots[k], region(zb(k), y))
        slots[4 + k] = lk.put(region(zb(k), y), region(zb(k), y), ynb)

    def gather_end(slots, region):
        for k in range(4):
            lk.got(slots[4 + k], region(zb(k), 1 - y))

    def pk_region(z_, y_):
        return g.pk.at[:, node(z_, y_)]

    def up_region(z_, y_):
        return g.w_up_all.at[:, node(z_, y_)]

    def back_region(z_, y_):
        return g.w_back_all.at[:, y_, :, z_]

    for i, (to, xm, cm, rm) in enumerate(members):
        lk.got(pk_s[i], g.pk.at[xm, n, cm])
    pk_g = gather_start(pk_region)

    def line(region, has):
        right, left, across = lk.take(3), lk.take(3), lk.take(4)
        passes = lk.take(3)

        def send(zs, ssem, rsem, to, when):
            copy = lk.make(region(zs, y), region(zs, y), ssem, rsem, to)
            pl.when(when)(copy.start)
            lk.pending.append((copy, when))

        def also(when, zs):
            return when if has is None else jnp.logical_and(when, has(zs))

        def step(k):
            for way, base in ((-1, right), (1, left)):
                if k == 0 and way == 1:
                    continue
                zs = z + way * k
                there = also(z >= k if way == -1 else z + k <= 3, zs)
                if k:
                    slot = base + k - 1
                    block = region(lax.rem(zs + 4, 4), y)
                    wait = lk.make(block, block, slot, slot, ynb)
                    pl.when(there)(wait.wait_recv)
                zs = lax.rem(zs + 4, 4)
                if k < 3 and (way == -1 or k == 0):
                    on = jnp.logical_and(there, z < 3)
                    send(zs, right + k, right + k, dev(x, zo(1), y, c), on)
                if k < 3 and (way == 1 or k == 0):
                    on = jnp.logical_and(there, z > 0)
                    send(zs, left + k, left + k, dev(x, zb(1), y, c), on)
                ssem = across + k if way == -1 else passes + k - 1
                send(zs, ssem, across + zs, ynb, there)

        def end():
            for zs in range(4):
                block = region(zs, 1 - y)
                wait = lk.make(block, block, across + zs, across + zs, ynb)
                if has is None:
                    wait.wait_recv()
                else:
                    pl.when(has(zs))(wait.wait_recv)

        return step, end

    def down_region(z_, y_):
        return g.w_down_all.at[lax.rem(z_, 2), y_]

    def down_has(z_):
        return (z_ + 4) // 2 == c + 2

    owner = z // 2
    dn_own = lk.take()
    dst = g.w_down_all.at[lax.rem(z, 2), y, c]
    dn_copy = lk.make(g.w_down, dst, dn_own, dn_own, sib)
    pl.when(owner != c)(dn_copy.start)
    lk.pending.append((dn_copy, owner != c))

    @pl.when(owner == c)
    def _():
        g.w_down_all[lax.rem(z, 2), y, c] = g.w_down[...]
        block = g.w_down_all.at[lax.rem(z, 2), y, 1 - c]
        lk.make(block, block, dn_own, dn_own, sib).wait_recv()

    down_step, down_end = line(down_region, down_has)
    up_step, up_end = line(up_region, None)
    back_step, back_end = line(back_region, None)
    down_step(0)

    lk.got(coef_s, g.coef.at[1 - x])
    cc = g.coef[0].astype(f32)
    sc = g.coef[1].astype(f32)

    def far(p, _):
        hr = g.far_re[pl.ds(p, 1), :]
        hi = g.far_im[pl.ds(p, 1), :]
        rows = pl.ds(aligned(16 * p, 16), 16)
        g.state[rows, 0:512] = cc * hr + sc * hi
        g.state[rows, 512:1024] = sc * hr - cc * hi
        return 0

    lax.fori_loop(0, 16, far, 0)
    for half in range(2):
        rows = slice(128 * half, 128 * half + 128)
        hi_, lo_ = split(g.state[rows, :])
        g.kern[rows, :] = (
            dot(hi_, g.near_hi[...]) + dot(lo_, g.near_hi[...]) + dot(hi_, g.near_lo[...])
        )
    for k in (1, 2, 3):
        gather_pass(pk_g, pk_region, k)
    ii = lax.broadcasted_iota(jnp.int32, (128, 128), 0)
    jj = lax.broadcasted_iota(jnp.int32, (128, 128), 1)
    flip = (ii + jj == 127).astype(bf16)

    def toeplitz(h, _):
        prev = jnp.zeros((128, 128), f32)
        for k in range(16):
            row = jnp.broadcast_to(g.kern[pl.ds(16 * k + h, 1), :], (128, 128))
            turned = pltpu.roll(row, 0, 1, stride=1, stride_axis=0)
            g.toep[h, k] = jnp.where(jj >= ii, turned, prev).astype(bf16)
            prev = turned
        return 0

    lax.fori_loop(0, 16, toeplitz, 0, unroll=2)
    down_step(1)

    gather_end(pk_g, pk_region)
    e_i = lax.broadcasted_iota(jnp.int32, (128, 1024), 0)
    e_j = lax.broadcasted_iota(jnp.int32, (128, 1024), 1)
    spread = jnp.logical_and(e_i < 32, lax.rem(e_j, 32) == e_i).astype(bf16)
    blk = lax.broadcasted_iota(jnp.int32, (16, 1024), 1) // 32
    acc = jnp.zeros((16, 1024), f32)
    for xm in range(2):
        for nm in range(8):
            for cm in range(2):
                rows = g.pk[xm, nm, cm, 32:48, :]
                acc = acc + jnp.where(
                    blk == 16 * xm + 2 * nm + cm, dot(rows, spread), 0.0
                )
    gain = acc[0:1, :]
    shift = acc[1:2, :]
    g.norm_rows[0:1, :] = gain
    g.norm_rows[1:2, :] = shift
    wv = g.pk[:, :, :, 0:32, :].reshape(1024, 128)
    g.w_val[...] = wv
    wvt = wv.T
    for t in range(8):
        at = 256 * (t % 4) + 128 * (t // 4)
        g.w_val_t[:, at : at + 128] = wvt[:, 128 * t : 128 * t + 128]

    def norm_block(read, q):
        def part(s_, _):
            rows = read(s_).astype(f32)
            mean = jnp.mean(rows, axis=-1, keepdims=True)
            cen = rows - mean
            var = jnp.mean(cen * cen, axis=-1, keepdims=True)
            out = (cen * lax.rsqrt(var + 1e-5) * g.norm_rows[0:1, :] + g.norm_rows[1:2, :]).astype(
                bf16
            )
            at = aligned(256 * q + 128 * s_, 128)
            g.normed[pl.ds(at, 128), :] = out
            for t in range(8):
                low = 256 * (t % 4) + 128 * (t // 4)
                g.normed_t[low : low + 128, pl.ds(at, 128)] = out[:, 128 * t : 128 * t + 128].T
            return 0

        lax.fori_loop(0, 2, part, 0)
        at = pl.ds(aligned(256 * q, 128), 256)
        pre = dot(g.w_val_t[...], g.normed_t[:, at])
        act, slope = gelu_parts(pre)
        g.val_slope[:, at] = slope
        g.val[:, at] = act.astype(bf16)

    norm_block(lambda s_: g.tokens[s_], r)
    lk.got(tok_sib, g.tok_all.at[r_sib])
    norm_block(lambda s_: g.tok_all[r_sib, s_], r_sib)
    lk.got(tok_x, g.tok_all.at[r_xn])
    tok_f = lk.put(g.tok_all.at[r_xn], g.tok_all.at[r_xn], sib)
    norm_block(lambda s_: g.tok_all[r_xn, s_], r_xn)
    lk.got(tok_f, g.tok_all.at[r_diag])
    norm_block(lambda s_: g.tok_all[r_diag, s_], r_diag)

    def channel_send(src, landing):
        slots = []
        for k in range(1, 8):
            to = lax.rem(n + k, 8)
            slots.append(
                lk.put(
                    src.at[pl.ds(aligned(16 * to, 16), 16), :],
                    landing.at[n],
                    (x, 2 * to + c),
                )
            )
        return slots

    def channel_got(slots, landing):
        for k in range(1, 8):
            lk.got(slots[k - 1], landing.at[lax.rem(n + 8 - k, 8)])

    def unpack(landing, put):
        def one(nm, _):
            for tb in range(8):
                s_, cm = 2 * (tb // 4) + tb % 2, (tb // 2) % 2
                put(s_, 2 * nm + cm, landing[nm, :, 128 * tb : 128 * tb + 128].astype(f32))
            return 0

        lax.fori_loop(0, 8, one, 0)

    def put_val(s_, i, tile):
        g.v32[pl.ds(32 * s_ + 16 + i, 16, stride=128), :] = tile
        g.vr32[pl.ds(16 * s_ + 15 - i, 16, stride=64), :] = tile

    def put_grad(s_, i, tile):
        g.v32[pl.ds(32 * s_ + 31 - i, 16, stride=128), :] = tile

    val_s = channel_send(g.val, g.val_in)
    g.val_in[n] = g.val[pl.ds(aligned(16 * n, 16), 16), :]
    down_step(2)
    for i, (to, xm, cm, rm) in enumerate(members):
        lk.got(up_s[i], g.w_up_all.at[xm, n, cm])
    up_step(0)
    down_step(3)

    zero = jnp.zeros((16, 128), f32)
    for i in range(64):
        g.v32[32 * i : 32 * i + 16, :] = zero
    diag_i = lax.broadcasted_iota(jnp.int32, (32, 32), 0) == lax.broadcasted_iota(
        jnp.int32, (32, 32), 1
    )
    skip_row = jnp.broadcast_to(g.skip[...].astype(f32), (32, 32))
    g.skip_b[...] = dot(jnp.where(diag_i, skip_row, 0.0).astype(bf16), jnp.ones((32, 128), bf16))

    channel_got(val_s, g.val_in)
    unpack(g.val_in, put_val)
    up_step(1)

    def conv_rows(h, k):
        rows = [g.v32[pl.ds(128 * h + 32 * s_ + 16 - k, 16), :] for s_ in range(4)]
        return jnp.concatenate(rows, axis=0)

    def conv(h, _):
        parts = [conv_rows(h, k) for k in range(16)]
        out = g.skip_b[pl.ds(16 * x + h, 1), :] * parts[0]
        for kk in range(8):
            lhs = jnp.concatenate([parts[2 * kk], parts[2 * kk + 1]], axis=1).astype(bf16)
            out = out + dot(lhs, g.toep[h, 2 * kk : 2 * kk + 2].reshape(256, 128))
        g.o32[pl.ds(aligned(64 * h, 64), 64), :] = out
        return 0

    def pack(out, back):
        def one(nm, _):
            for tb in range(8):
                s_, cm = 2 * (tb // 4) + tb % 2, (tb // 2) % 2
                i = 2 * nm + cm
                at = pl.ds(16 * s_ + (15 - i if back else i), 16, stride=64)
                out[nm, :, 128 * tb : 128 * tb + 128] = g.o32[at, :].astype(bf16)
            return 0

        lax.fori_loop(0, 8, one, 0)

    def channel_back(src, landing):
        slots = []
        for k in range(1, 8):
            to = lax.rem(n + k, 8)
            slots.append(
                lk.put(src.at[to], landing.at[pl.ds(aligned(16 * n, 16), 16), :], (x, 2 * to + c))
            )
        return slots

    def channel_back_got(slots, landing):
        for k in range(1, 8):
            at = aligned(16 * lax.rem(n + 8 - k, 8), 16)
            lk.got(slots[k - 1], landing.at[pl.ds(at, 16), :])

    lax.fori_loop(0, 16, conv, 0, unroll=2)
    pack(g.mix_out, False)
    mix_s = channel_back(g.mix_out, g.mix.at[r])
    g.mix[r, pl.ds(aligned(16 * n, 16), 16), :] = g.mix_out[n]

    up_step(2)
    for i, (to, xm, cm, rm) in enumerate(members):
        lk.got(back_s[i], g.w_back_all.at[cm, y, xm, z])
    back_step(0)
    lk.got(cot_x, g.cot_all.at[r_xn])
    cot_f = lk.put(g.cot_all.at[r_xn], g.cot_all.at[r_xn], sib)
    down_end()
    lk.got(cot_sib, g.cot_all.at[r_sib])
    lk.got(cot_f, g.cot_all.at[r_diag])
    down2d = g.w_down_all.reshape(768, 1024)
    cot2d = g.cot_all.reshape(1024, 1024)

    def hidden_tile(q, _):
        rows = pl.ds(aligned(256 * q, 256), 256)
        g.slope[rows, :] = dot_nt(cot2d[rows, :], down2d[...])
        return 0

    lax.fori_loop(0, 4, hidden_tile, 0)
    up_step(3)
    back_step(1)
    channel_back_got(mix_s, g.mix.at[r])
    mix_x = lk.put(g.mix.at[r], g.mix.at[r], xn)
    mix_sib = lk.put(g.mix.at[r], g.mix.at[r], sib)
    back_step(2)

    up_end()
    up2d = g.w_up_all.reshape(1024, 768)

    def up_tile(q, _):
        rows = pl.ds(aligned(256 * q, 256), 256)
        act, slope = gelu_parts(dot(g.normed[rows, :], up2d[...]))
        gh = g.slope[rows, :]
        g.act[rows, :] = act
        g.g_gate[rows, :] = (gh * act).astype(bf16)
        g.slope[rows, :] = gh * slope
        return 0

    back_step(3)
    lax.fori_loop(0, 4, up_tile, 0)
    lk.got(mix_x, g.mix.at[r_xn])
    mix_f = lk.put(g.mix.at[r_xn], g.mix.at[r_xn], sib)
    back_end()
    back2d = g.w_back_all.reshape(512, 768)

    def mixed_part(ranks, q):
        w = [back2d[pl.ds(aligned(128 * rr, 128), 128), :] for rr in ranks]
        w = w[0] if len(w) == 1 else jnp.concatenate(w, axis=0)
        return dot_nt(w, g.g_gate[pl.ds(aligned(512 * q, 512), 512), :])

    gm_s, gm_xs = [], []
    for q in range(2):
        at = slice(512 * q, 512 * q + 512)
        both = mixed_part((1 - c, 2 + 1 - c), q).astype(bf16)
        g.gm_send[:, :, at] = both.reshape(2, 128, 512)
        gm_s.append(lk.put(g.gm_send.at[:, :, at], g.gm_in.at[:, :, at], sib))
    lk.got(mix_sib, g.mix.at[r_sib])
    lk.got(mix_f, g.mix.at[r_diag])

    mix2d = g.mix.reshape(512, 1024)

    def back_tile(i, _):
        at = pl.ds(aligned(384 * i, 128), 384)
        part = dot(mix2d[...], g.g_gate[:, at]).astype(bf16)
        g.gb[:, :, :, at] = part.reshape(2, 2, 128, 384)
        return 0

    lax.fori_loop(0, 2, back_tile, 0)
    gb_y = lk.put(g.gb.at[:, 1 - y], g.gb_y, ynb)


    for q in range(2):
        at = slice(512 * q, 512 * q + 512)
        both = mixed_part((2 * (1 - x) + c, 2 * x + c), q)
        g.state[0:128, at] = both[128:256, :]
        lk.got(gm_s[q], g.gm_in.at[:, :, at])
        g.gm_x[:, at] = (both[0:128, :] + g.gm_in[1 - x, :, at].astype(f32)).astype(bf16)
        gm_xs.append(lk.put(g.gm_x.at[:, at], g.gm_xin.at[:, at], xn))


    def turn(i, _):
        rr, tb = i // 8, lax.rem(i, 8)
        rows = pl.ds(aligned(128 * tb, 128), 128)
        at = pl.ds(aligned(128 * rr, 128), 128)
        g.mix_tok[rows, at] = g.mix[rr, :, rows].T
        return 0

    lax.fori_loop(0, 32, turn, 0, unroll=4)

    def gate_tile(q, _):
        rows = pl.ds(aligned(256 * q, 256), 256)
        gate = dot(g.mix_tok[rows, :], back2d[...])
        hidden = (g.act[rows, :] * gate).astype(bf16)
        g.hidden[rows, :] = hidden
        g.hidden_t[:, rows] = hidden.T
        g.g_up[rows, :] = (g.slope[rows, :] * gate).astype(bf16)
        return 0

    lax.fori_loop(0, 4, gate_tile, 0)

    gd_y = []

    def down_grad(zl):
        def tile(i, _):
            at = pl.ds(aligned(512 * i, 512), 512)
            part = dot(g.hidden_t[384 * zl : 384 * zl + 384, :], cot2d[:, at]).astype(bf16)
            g.gd[zl, :, :, at] = part.reshape(2, 192, 512)
            return 0

        lax.fori_loop(0, 2, tile, 0)

    def down_send(zl):
        gd_y.append(lk.put(g.gd.at[zl, 1 - y], g.gd_y.at[zl], ynb))

    down_grad(0)
    down_grad(1)

    for tb in range(8):
        if tb % 4 == 0:
            half = slice(128 * tb, 128 * tb + 512)
            lk.got(gm_xs[tb // 4], g.gm_xin.at[:, half])
        at = slice(128 * tb, 128 * tb + 128)
        total = g.state[0:128, at] + g.gm_in[x, :, at].astype(f32) + g.gm_xin[:, at].astype(f32)
        g.w_val_t[:, at] = dot(total.astype(bf16), flip).astype(bf16)
    gm_cs = channel_send(g.w_val_t, g.gm_land)
    g.gm_land[n] = g.w_val_t[pl.ds(aligned(16 * n, 16), 16), :]

    down_send(0)
    down_send(1)

    z1 = z + 1 - 2 * lax.rem(z, 2)
    z2 = zo(2)
    z3 = 3 - z

    def put_add(mine, pair):
        return (mine[...].astype(f32) + pair[...].astype(f32)).astype(bf16)

    near_half = z // 2 == c
    gd_r = lk.take(3)
    d_pair = (lk.take(), lk.take())

    def down_owner(zl, when, zd, place):
        for cm in range(2):
            src = g.gd.at[zl, y, pl.ds(96 * cm, 96)]
            copy = lk.make(src, g.gd_in.at[place], lk.take(), gd_r + place, dev(x, zd, y, cm))
            pl.when(when)(copy.start)
            lk.pending.append((copy, when))

    def down_sum(zl):
        lk.got(gd_y[zl], g.gd_y.at[zl])
        total = g.gd[zl, y].astype(f32) + g.gd_y[zl].astype(f32)
        g.gd[zl, y] = total.astype(bf16)
        same = lax.rem(z, 2) == zl
        down_owner(zl, jnp.logical_and(near_half, jnp.logical_not(same)), z1, 1)
        copy = lk.make(g.gd.at[zl, y], g.gd_p, d_pair[zl], d_pair[zl], dev(x, z1, y, c))
        sends = jnp.logical_and(jnp.logical_not(near_half), jnp.logical_not(same))
        pl.when(sends)(copy.start)
        lk.pending.append((copy, sends))
        own = jnp.logical_and(near_half, same)

        @pl.when(own)
        def _():
            g.gd_in[0] = g.gd[zl, y, pl.ds(aligned(96 * c, 32), 96), :]

        other = g.gd.at[zl, y, pl.ds(aligned(96 * (1 - c), 32), 96)]
        copy = lk.make(other, g.gd_in.at[0], lk.take(), gd_r, sib)
        pl.when(own)(copy.start)
        lk.pending.append((copy, own))

    def down_far(zl):
        adds = jnp.logical_and(jnp.logical_not(near_half), lax.rem(z, 2) == zl)

        @pl.when(adds)
        def _():
            lk.make(g.gd_p, g.gd_p, d_pair[zl], d_pair[zl], ynb).wait_recv()
            g.gd[zl, y] = put_add(g.gd.at[zl, y], g.gd_p)

        down_owner(zl, adds, z2, 2)

    def back_pairs():
        near = lk.put(g.gb_z.at[:, z1], g.gb_in.at[0], dev(x, z1, y, c))
        pair = lk.put(g.gb_z.at[:, z3], g.gb_in.at[1], dev(x, z1, y, c))
        return near, pair

    def back_far(pair):
        lk.got(pair, g.gb_in.at[1])
        g.gb_z[:, z2] = put_add(g.gb_z.at[:, z2], g.gb_in.at[1])
        return lk.put(g.gb_z.at[:, z2], g.gb_in.at[2], dev(x, z2, y, c))

    def group_sum(part, send, land, xsend, xland):
        for xm in range(2):
            send[xm] = part(xm, 1 - c).astype(bf16)
        first = lk.put(send, land, sib)
        mine = part(1 - x, c)
        lk.got(first, land)
        xsend[...] = (mine + land[1 - x].astype(f32)).astype(bf16)
        second = lk.put(xsend, xland, xn)

        def own():
            return part(x, c) + land[x].astype(f32) + xland[...].astype(f32)

        return second, own

    def branch_part(xm, cm):
        rows = pl.ds(aligned(256 * (2 * xm + cm), 256), 256)
        return dot(g.hidden[rows, :], down2d[...])

    spare = g.normed.reshape(2, 2, 256, 1024)
    br_s, br_own = group_sum(
        branch_part, spare.at[0], g.br_in, g.tok_all.at[r].reshape(256, 1024), g.br_xin
    )

    other = pl.ds(aligned(64 * (1 - y), 64), 64)
    own64 = pl.ds(aligned(64 * y, 64), 64)
    up_y, gu_s = {}, {}
    up_to = {0: z, 1: z1, 2: z2, 3: z3}

    def up_part(k):
        z_d = up_to[k]
        rows = pl.ds(aligned(256 * z_d, 256), 256)
        part = dot(g.normed_t[rows, :], g.g_up[...]).astype(bf16)
        g.gu[z_d] = part.reshape(2, 128, 768)

    def up_grad(k):
        z_d = up_to[k]
        up_y[k] = lk.put(g.gu.at[z_d, :, other], g.gu_y.at[z_d], ynb)

    def up_sum(k):
        z_d = up_to[k]
        lk.got(up_y[k], g.gu_y.at[z_d])
        total = g.gu[z_d, :, own64, :].astype(f32) + g.gu_y[z_d].astype(f32)
        if k == 2:
            lk.got(gu_s[3], g.gu_in.at[0])
            total = total + g.gu_in[0].astype(f32)
        g.gu[z_d, :, own64, :] = total.astype(bf16)
        if k:
            to = dev(x, up_to[2 if k == 2 else 1], y, c)
            gu_s[k] = lk.put(g.gu.at[z_d, :, own64], g.gu_in.at[(1, 2, 0)[k - 1]], to)

    lk.got(gb_y, g.gb_y)
    total = g.gb[:, y].astype(f32) + g.gb_y[...].astype(f32)
    g.gb_z[...] = total.astype(bf16).reshape(4, 4, 16, 768)
    gb_near, gb_pair = back_pairs()
    for k in (3, 2, 1, 0):
        up_part(k)
    channel_got(gm_cs, g.gm_land)
    unpack(g.gm_land, put_grad)

    def conv_back(h, _):
        parts = [conv_rows(h, k) for k in range(16)]
        own = g.vr32[pl.ds(aligned(64 * h, 64), 64), :].T.astype(bf16)
        out = g.skip_b[pl.ds(16 * x + h, 1), :] * parts[0]
        lhs = []
        for kk in range(8):
            lhs.append(jnp.concatenate([parts[2 * kk], parts[2 * kk + 1]], axis=1).astype(bf16))
            out = out + dot(lhs[kk], g.toep[h, 2 * kk : 2 * kk + 2].reshape(256, 128))
        g.o32[pl.ds(aligned(64 * h, 64), 64), :] = out
        after = jnp.zeros((128, 128), f32)
        for kk in range(7, -1, -1):
            pair = dot(own, lhs[kk])
            for half in (1, 0):
                turned = pltpu.roll(
                    pair[:, 128 * half : 128 * half + 128], 0, 1, stride=1, stride_axis=0
                )
                lag = jnp.where(jj >= ii, turned, after)
                after = turned
                at = pl.ds(aligned((16 * (2 * kk + half) + h) * 8, 8), 8)
                g.gk8[at, :] = jnp.sum(lag.reshape(16, 8, 128), axis=0)
        return 0

    lax.fori_loop(0, 8, conv_back, 0, unroll=2)
    lax.fori_loop(8, 16, conv_back, 0, unroll=2)
    pack(g.gv_out, True)
    gv_s = channel_back(g.gv_out, g.g_val)
    g.g_val[pl.ds(aligned(16 * n, 16), 16), :] = g.gv_out[n]

    up_grad(3)
    down_sum(0)
    gb_far = back_far(gb_pair)
    down_sum(1)

    tall = g.gk8[pl.ds(0, 256, stride=8), :]
    for s_ in range(1, 8):
        tall = tall + g.gk8[pl.ds(s_, 256, stride=8), :]
    for half in range(2):
        hi_, lo_ = split(tall[128 * half : 128 * half + 128, :])
        g.state[128 * half : 128 * half + 128, :] = (
            dot(hi_, g.near_t_hi[...]) + dot(lo_, g.near_t_hi[...]) + dot(hi_, g.near_t_lo[...])
        )
    g.skip_sum[...] = tall[0:16, :]

    def far_back(p, carry):
        gc, gs = carry
        hr = g.far_re[pl.ds(p, 1), :]
        hi = g.far_im[pl.ds(p, 1), :]
        rows = pl.ds(aligned(16 * p, 16), 16)
        ur = g.state[rows, 0:512]
        ui = g.state[rows, 512:1024]
        return gc + hr * ur - hi * ui, gs + hr * ui + hi * ur

    blank = jnp.zeros((16, 512), f32)
    gc, gs = lax.fori_loop(0, 16, far_back, (blank, blank))
    g.gcoef[0] = gc
    g.gcoef[1] = gs
    gcoef_s = lk.put(g.gcoef.at[1 - x], g.gcoef_in, xn)
    skip_s = lk.put(g.skip_sum, g.skip_in, xn)

    channel_back_got(gv_s, g.g_val)
    for tb in range(8):
        at = slice(128 * tb, 128 * tb + 128)
        back = dot(g.g_val[:, at], flip)
        g.gvp_t[at, :] = (back * g.val_slope[:, at]).astype(bf16).T
    part = dot(g.normed_t[...], g.gvp_t[...]).astype(bf16)
    g.gv[...] = part.reshape(4, 2, 128, 128)
    gv_y = lk.put(g.gv.at[:, :, other], g.gv_y, ynb)

    def normed_part(xm, cm):
        rows = pl.ds(aligned(256 * (2 * xm + cm), 256), 256)
        return dot_nt(g.g_up[rows, :], up2d[...]) + dot_nt(g.gvp_t[rows, :], g.w_val[...])

    gn_s, gn_own = group_sum(
        normed_part, spare.at[1], g.gn_in, g.tok_all.at[r_sib].reshape(256, 1024), g.gn_xin
    )
    up_grad(2)
    up_grad(1)
    up_grad(0)
    up_sum(3)
    down_far(0)
    down_far(1)

    lk.got(gv_y, g.gv_y)
    g.gv_z[...] = (g.gv[:, :, own64, :].astype(f32) + g.gv_y[...].astype(f32)).astype(bf16)
    gv_zs = {}
    for k in (2, 1, 3):
        gv_zs[k] = lk.put(g.gv_z.at[zo(k)], g.gv_in.at[k - 1], dev(x, zo(k), y, c))

    up_sum(2)

    lk.got(br_s, g.br_xin)
    out = br_own().reshape(2, 128, 1024) + g.tokens[...].astype(f32)
    g.result[...] = out.astype(bf16)

    lk.got(gb_near, g.gb_in.at[0])
    lk.got(gb_far, g.gb_in.at[2])
    total = g.gb_z[:, z].astype(f32) + g.gb_in[0].astype(f32) + g.gb_in[2].astype(f32)
    g.gb_f[...] = total.astype(bf16)
    fin_b = [lk.put(g.gb_f.at[2 * cm + xm], g.fb_in.at[r], to) for to, xm, cm, rm in members]
    g.fb_in[r] = g.gb_f[2 * c + x]

    lk.got(gn_s, g.gn_xin)
    up_sum(1)
    g.state[...] = gn_own()

    def norm_back(i, carry):
        dg, ds = carry
        s_, part = i // 2, pl.ds(aligned(64 * lax.rem(i, 2), 64), 64)
        rows = g.tokens[s_, part, :].astype(f32)
        mean = jnp.mean(rows, axis=-1, keepdims=True)
        cen = rows - mean
        var = jnp.mean(cen * cen, axis=-1, keepdims=True)
        inv = lax.rsqrt(var + 1e-5)
        zn = cen * inv
        gn = g.state[pl.ds(aligned(64 * i, 64), 64), :]
        gg = gn * g.norm_rows[0:1, :]
        m1 = jnp.mean(gg, axis=-1, keepdims=True)
        m2 = jnp.mean(gg * zn, axis=-1, keepdims=True)
        g.g_tokens[s_, part, :] = g.cot[s_, part, :].astype(f32) + inv * (gg - m1 - zn * m2)
        dg = dg + jnp.sum(gn * zn, axis=0, keepdims=True)
        ds = ds + jnp.sum(gn, axis=0, keepdims=True)
        return dg, ds

    blank = jnp.zeros((1, 1024), f32)
    dg, ds = lax.fori_loop(0, 4, norm_back, (blank, blank))
    for zd in range(4):
        g.ng[zd, 0:1, :] = dg[:, 128 * zd : 128 * zd + 128]
        g.ng[zd, 1:2, :] = dg[:, 512 + 128 * zd : 640 + 128 * zd]
        g.ng[zd, 2:3, :] = ds[:, 128 * zd : 128 * zd + 128]
        g.ng[zd, 3:4, :] = ds[:, 512 + 128 * zd : 640 + 128 * zd]
        g.ng[zd, 4:8, :] = jnp.zeros((4, 128), f32)
    ng_s = []
    for k in range(1, 8):
        to = lax.rem(n + k, 8)
        ng_s.append(lk.put(g.ng.at[to // 2], g.ng_in.at[k - 1], (x, 2 * to + c)))

    up_sum(0)

    total = g.gu[z, :, own64, :].astype(f32)
    for k in (2, 1):
        lk.got(gu_s[k], g.gu_in.at[(1, 2, 0)[k - 1]])
        total = total + g.gu_in[(1, 2, 0)[k - 1]].astype(f32)
    g.gu_f[...] = total.reshape(2, 2, 32, 768).astype(bf16)
    fin_u = [lk.put(g.gu_f.at[xm, cm], g.fu_in.at[r], to) for to, xm, cm, rm in members]
    for k in (2, 1, 3):
        lk.got(gv_zs[k], g.gv_in.at[k - 1])
    total = g.gv_z[z].astype(f32)
    for k in range(3):
        total = total + g.gv_in[k].astype(f32)
    g.gv_f[...] = total.reshape(2, 2, 32, 128).astype(bf16)
    fin_v = [lk.put(g.gv_f.at[xm, cm], g.fv_in.at[r], to) for to, xm, cm, rm in members]
    g.fu_in[r] = g.gu_f[x, c]
    g.fv_in[r] = g.gv_f[x, c]

    from_sib = owner != c

    @pl.when(from_sib)
    def _():
        lk.make(g.gd_in.at[0], g.gd_in.at[0], gd_r, gd_r, sib).wait_recv()

    for place in (1, 2):
        region = g.gd_in.at[place]
        lk.make(region, region, gd_r + place, gd_r + place, sib).wait_recv()
    g.o_down[...] = (
        g.gd_in[0].astype(f32) + g.gd_in[1].astype(f32) + g.gd_in[2].astype(f32)
    )

    mine = pl.ds(aligned(16 * x, 16), 16)
    theirs = pl.ds(aligned(16 * (1 - x), 16), 16)
    lk.got(gcoef_s, g.gcoef_in)
    g.o_coef[mine, :] = g.gcoef[x]
    g.o_coef[theirs, :] = g.gcoef_in[...]
    lk.got(skip_s, g.skip_in)
    g.o_skip[mine, :] = g.skip_sum[...]
    g.o_skip[theirs, :] = g.skip_in[...]

    total = g.ng[z]
    for k in range(1, 8):
        lk.got(ng_s[k - 1], g.ng_in.at[k - 1])
        total = total + g.ng_in[k - 1]
    g.ng_f[...] = total
    ng_t = [lk.put(g.ng_f, g.ng_fin.at[i], to) for i, (to, xm, cm, rm) in enumerate(members)]

    for i, (to, xm, cm, rm) in enumerate(members):
        lk.got(fin_u[i], g.fu_in.at[rm])
        lk.got(fin_b[i], g.fb_in.at[rm])
        lk.got(fin_v[i], g.fv_in.at[rm])
    for i in range(3):
        lk.got(ng_t[i], g.ng_fin.at[i])
        total = total + g.ng_fin[i]
    total = jnp.where(x == 0, total, pltpu.roll(total, 7, 0))
    g.o_norm[...] = pltpu.roll(total, 128 - (64 * y + 32 * c), 1)
    lk.finish()
    assert lk.count <= N_SEMS


def start_of(copy):
    copy.start()
    return copy


def fast_body(
    tokens, norm_gain, norm_shift, w_up, w_value, w_back, w_down, mode_coef, skip_gain, cotangent
):
    states = 512
    length = tokens.shape[1] * lax.axis_size("tok")
    far_re, far_im, near_hi, near_lo, near_t_hi, near_t_lo = mode_tables(states, length)
    ins = dict(
        tokens=tokens,
        norm_gain=norm_gain.reshape(1, -1),
        norm_shift=norm_shift.reshape(1, -1),
        w_up=w_up,
        w_value=w_value,
        w_back=w_back,
        w_down=w_down,
        mode_coef=mode_coef,
        skip=skip_gain.reshape(1, -1),
        cot=cotangent,
        far_re=far_re,
        far_im=far_im,
        near_hi=near_hi,
        near_lo=near_lo,
        near_t_hi=near_t_hi,
        near_t_lo=near_t_lo,
    )
    outs = dict(
        result=((2, 128, 1024), bf16),
        g_tokens=((2, 128, 1024), f32),
        o_norm=((8, 128), f32),
        fu_in=((4, 32, 768), bf16),
        fv_in=((4, 32, 128), bf16),
        fb_in=((4, 16, 768), bf16),
        o_down=((96, 1024), f32),
        o_coef=((32, 512), f32),
        o_skip=((32, 128), f32),
    )
    scratch = dict(
        pk_send=((4, 48, 128), bf16),
        pk=((2, 8, 2, 48, 128), bf16),
        coef=((2, 16, 512), bf16),
        w_up_all=((2, 8, 2, 32, 768), bf16),
        w_back_all=((2, 2, 2, 4, 16, 768), bf16),
        w_down_all=((2, 2, 2, 96, 1024), bf16),
        tok_all=((4, 2, 128, 1024), bf16),
        cot_all=((4, 2, 128, 1024), bf16),
        state=((256, 1024), f32),
        kern=((256, 128), f32),
        toep=((16, 16, 128, 128), bf16),
        norm_rows=((8, 1024), f32),
        w_val=((1024, 128), bf16),
        w_val_t=((128, 1024), bf16),
        normed=((1024, 1024), bf16),
        normed_t=((1024, 1024), bf16),
        val_slope=((128, 1024), f32),
        val=((128, 1024), bf16),
        val_in=((8, 16, 1024), bf16),
        v32=((2048, 128), f32),
        vr32=((1024, 128), f32),
        o32=((1024, 128), f32),
        skip_b=((32, 128), f32),
        mix_out=((8, 16, 1024), bf16),
        mix=((4, 128, 1024), bf16),
        act=((1024, 768), f32),
        slope=((1024, 768), f32),
        g_gate=((1024, 768), bf16),
        gm_send=((2, 128, 1024), bf16),
        gm_in=((2, 128, 1024), bf16),
        gm_x=((128, 1024), bf16),
        gm_xin=((128, 1024), bf16),
        gm_land=((8, 16, 1024), bf16),
        mix_tok=((1024, 512), bf16),
        hidden=((1024, 768), bf16),
        hidden_t=((768, 1024), bf16),
        g_up=((1024, 768), bf16),
        gd=((2, 2, 192, 1024), bf16),
        gd_y=((2, 192, 1024), bf16),
        gd_in=((3, 96, 1024), bf16),
        gd_p=((192, 1024), bf16),
        gu=((4, 2, 128, 768), bf16),
        gu_y=((4, 2, 64, 768), bf16),
        gu_in=((3, 2, 64, 768), bf16),
        gu_f=((2, 2, 32, 768), bf16),
        gb=((2, 2, 128, 768), bf16),
        gb_y=((2, 128, 768), bf16),
        gb_z=((4, 4, 16, 768), bf16),
        gb_in=((3, 4, 16, 768), bf16),
        gb_f=((4, 16, 768), bf16),
        gv=((4, 2, 128, 128), bf16),
        gv_y=((4, 2, 64, 128), bf16),
        gv_z=((4, 2, 64, 128), bf16),
        gv_in=((3, 2, 64, 128), bf16),
        gv_f=((2, 2, 32, 128), bf16),
        gk8=((2048, 128), f32),
        skip_sum=((16, 128), f32),
        skip_in=((16, 128), f32),
        gcoef=((2, 16, 512), f32),
        gcoef_in=((16, 512), f32),
        gv_out=((8, 16, 1024), bf16),
        g_val=((128, 1024), bf16),
        gvp_t=((1024, 128), bf16),
        br_in=((2, 256, 1024), bf16),
        br_xin=((256, 1024), bf16),
        gn_in=((2, 256, 1024), bf16),
        gn_xin=((256, 1024), bf16),
        ng=((4, 8, 128), f32),
        ng_in=((7, 8, 128), f32),
        ng_f=((8, 128), f32),
        ng_fin=((3, 8, 128), f32),
    )
    names = list(ins) + list(outs) + list(scratch) + ["ssem", "rsem"]
    vmem = pl.BlockSpec(memory_space=pltpu.VMEM)
    got = pl.pallas_call(
        functools.partial(layer_kernel, names),
        out_shape=[jax.ShapeDtypeStruct(s, t) for s, t in outs.values()],
        in_specs=[vmem] * len(ins),
        out_specs=[vmem] * len(outs),
        scratch_shapes=[pltpu.VMEM(s, t) for s, t in scratch.values()]
        + [pltpu.SemaphoreType.DMA((N_SEMS,)), pltpu.SemaphoreType.DMA((N_SEMS,))],
        compiler_params=pltpu.CompilerParams(
            collective_id=0, has_side_effects=True, vmem_limit_bytes=64 << 20
        ),
    )(*ins.values())
    up_rows, back_rows = w_up.shape[0], w_back.shape[0]
    final = [
        jax.ShapeDtypeStruct((2, 128, 1024), bf16),
        jax.ShapeDtypeStruct((2, 128, 1024), f32),
        jax.ShapeDtypeStruct((1, 32), f32),
        jax.ShapeDtypeStruct((1, 32), f32),
        jax.ShapeDtypeStruct((up_rows, 3072), f32),
        jax.ShapeDtypeStruct((up_rows, 512), f32),
        jax.ShapeDtypeStruct((back_rows, 3072), f32),
        jax.ShapeDtypeStruct((96, 1024), f32),
        jax.ShapeDtypeStruct((32, 512), f32),
        jax.ShapeDtypeStruct((1, 32), f32),
    ]
    out = pl.pallas_call(
        last_kernel,
        out_shape=final,
        in_specs=[vmem] * len(outs),
        out_specs=[vmem] * len(final),
        compiler_params=pltpu.CompilerParams(vmem_limit_bytes=63 << 20),
    )(*got)
    return tuple(v.reshape(-1) if v.shape[0] == 1 else v for v in out)


def last_kernel(*refs):
    (result, g_tokens, norm, up, value, back, down, coef, skip), out = refs[:9], refs[9:]
    out[0][...] = result[...]
    out[1][...] = g_tokens[...]
    out[2][...] = norm[0:1, 0:32]
    out[3][...] = norm[2:3, 0:32]
    for rr in range(4):
        out[4][:, 768 * rr : 768 * rr + 768] = up[rr].astype(f32)
        out[6][:, 768 * rr : 768 * rr + 768] = back[rr].astype(f32)
    out[5][...] = sum(dot_nt(value[rr], channels_of(rr)) for rr in range(4))
    out[7][...] = down[...]
    out[8][...] = coef[...]
    same = lax.broadcasted_iota(jnp.int32, (32, 32), 0) == lax.broadcasted_iota(
        jnp.int32, (32, 32), 1
    )
    column = jnp.broadcast_to(skip[:, 127:128], (32, 32))
    out[9][...] = jnp.sum(jnp.where(same, column, 0.0), axis=0, keepdims=True)


def run(tokens, *rest):
    sizes = (lax.axis_size("item"), lax.axis_size("tok"), tokens.shape)
    if sizes == (2, 16, (2, 128, 1024)):
        return fast_body(tokens, *rest)
    return body(tokens, *rest)


def solution(mesh):
    in_specs = (
        P("item", "tok", None),
        P(("item", "tok")),
        P(("item", "tok")),
        P(("item", "tok"), None),
        P(("item", "tok"), None),
        P(("item", "tok"), None),
        P(("item", "tok"), None),
        P("tok", "item"),
        P("tok"),
        P("item", "tok", None),
    )
    out_specs = (
        P("item", "tok", None),
        P("item", "tok", None),
        P(("item", "tok")),
        P(("item", "tok")),
        P(("item", "tok"), None),
        P(("item", "tok"), None),
        P(("item", "tok"), None),
        P(("item", "tok"), None),
        P("tok", "item"),
        P("tok"),
    )
    return jax.shard_map(run, mesh=mesh, in_specs=in_specs, out_specs=out_specs, check_vma=False)
```
